32 devices in a mesh: alpha: 4 (over y, x), beta: 8 (over z, core).
Axes of the slice: x: 2, y: 2, z: 4, core: 2. Of those that a mesh axis runs over, the one named last changes fastest.
Arguments:
- coefficients: bfloat16 [1024, 2048], P('alpha', 'beta'), may hold values from -6 to 6
- diagonal: float32 [1024, 2048], P('alpha', 'beta'), may hold values from 0.3 to 3
- integrals: bfloat16 [324, 324], replicated, may hold values from -0.02734375 to 0.02734375
- alpha_row: int32 [324, 1024], replicated, may hold values from 0 to 1023
- alpha_sign: int32 [324, 1024], replicated, may hold values from -1 to 1
- beta_block: int32 [32, 324], P('beta'), may hold values from 0 to 31
- beta_sign: int32 [32, 20736], P('beta'), may hold values from -1 to 1
- block_irrep: int32 [16], replicated, may hold values from 0 to 7, as said below
Outputs:
- sigma: float32 [1024, 2048], P('alpha', 'beta')
The draws below stay inside these ranges and needn't reach their ends.
Inputs may be any that keep to these rules, and one draw needn't show every extreme that they name: `block_irrep`: irrep 0 is the window's. The 4 blocks held by one index of alpha include 1 to 4 blocks of irrep 0, and some index holds 4 of them.
All inputs are finite; a program needn't handle non-finite values.
Results may differ from the reference program's by a relative error of at most 0.0003.
Values may be sent and summed in bfloat16 or wider, within the bound.
No kernel may reach another device: no remote copies, remote signals or barrier semaphores. Data moves between devices by JAX's collectives and lax.ppermute only.
A program may use at most 128 MiB of HBM per device.

```python
import math
import jax
import jax.numpy as jnp
from jax import lax

P_SIZE = 324
BLOCK = 64
AB_DEV = 4
NA = 1024
NB = 2048
NBB = 32
N_ALPHA = 4


def draw_block_irrep(key, part):
    key_count, key_heavy, key_order, key_other = jax.random.split(key, 4)
    upper = max(1, AB_DEV // 2)
    counts = jax.random.randint(key_count, (N_ALPHA,), 1, upper + 1)
    heavy = jax.random.randint(key_heavy, (), 0, N_ALPHA)
    device_iota = jnp.arange(N_ALPHA, dtype=jnp.int32)
    counts = jnp.where(device_iota == heavy, AB_DEV, counts)
    order_keys = jax.random.split(key_order, N_ALPHA)
    orders = jax.vmap(lambda single: jax.random.permutation(single, AB_DEV))(order_keys)
    live_mask = orders < counts[:, None]
    others = jax.random.randint(key_other, (N_ALPHA, AB_DEV), 1, 8)
    return jnp.where(live_mask, 0, others).reshape(-1).astype(jnp.int32)


def plant(entries, own_key, low, top_value):
    longest = entries.shape.index(max(entries.shape))
    spots = []
    for shift in (0, 1):
        where = [jax.random.randint(jax.random.fold_in(own_key, axis), (), 0, length) for axis, length in enumerate(entries.shape)]
        where[longest] = (where[longest] + shift) % entries.shape[longest]
        spots.append(tuple(where))
    return entries.at[spots[0]].set(low).at[spots[1]].set(top_value)


def steps_of(stream_key, dims, cuts, least, largest):
    level = 1.0
    for dim, parts in cuts:
        heights = jax.random.uniform(jax.random.fold_in(jax.random.fold_in(stream_key, 6), dim), (parts,), jnp.float32, least / len(cuts), largest / len(cuts))
        level = level * jnp.repeat(jnp.exp(heights), dims[dim] // parts).reshape((-1,) + (1,) * (len(dims) - 1 - dim))
    return level


def centred(own_key, shape, spread, limit, shards=(), kind=jnp.bfloat16):
    values = spread * jax.random.normal(own_key, shape, jnp.float32)
    if shards:
        values = values * steps_of(own_key, shape, shards, -0.22, 0.18)
    return jnp.clip(values, -limit, limit).astype(kind)


def setup_inputs(seed: int = 0) -> dict:
    streams_of = jax.random.split(jax.random.key(seed), 9)
    return {
        "coefficients": centred(streams_of[0], (NA, NB), 1.0, 6.0, ((0, 4), (1, 8))),
        "diagonal": jnp.clip(jnp.exp(math.log(3.0) - 2.3025851 * jax.random.uniform(streams_of[1], (NA, NB), jnp.float32) ** steps_of(streams_of[1], (NA, NB), ((0, 4), (1, 8)), -0.2, 0.2)), 0.3, 3.0),
        "integrals": centred(streams_of[2], (P_SIZE, P_SIZE), (P_SIZE * P_SIZE // 2) ** -0.5, 0.02734375),
        "alpha_row": plant(jax.random.randint(streams_of[3], (P_SIZE, NA), 0, NA), jax.random.fold_in(streams_of[3], 1), 0, NA - 1).astype(jnp.int32),
        "alpha_sign": plant(jax.random.randint(streams_of[4], (P_SIZE, NA), -1, 2), jax.random.fold_in(streams_of[4], 1), -1, 1).astype(jnp.int32),
        "beta_block": plant(jax.random.randint(streams_of[5], (NBB, P_SIZE), 0, NBB), jax.random.fold_in(streams_of[5], 1), 0, NBB - 1).astype(jnp.int32),
        "beta_sign": plant(jax.random.randint(streams_of[6], (NBB, P_SIZE * BLOCK), -1, 2), jax.random.fold_in(streams_of[6], 1), -1, 1).astype(jnp.int32),
        "block_irrep": draw_block_irrep(jax.random.fold_in(streams_of[8], 71), 0),
    }


def reference(coefficients, diagonal, integrals, alpha_row, alpha_sign, beta_block, beta_sign, block_irrep):
    live_rows = jnp.repeat((block_irrep == 0).astype(jnp.int32), BLOCK)
    coeff_live = jnp.where(live_rows[:, None] == 1, coefficients, jnp.zeros_like(coefficients))
    coeff_float = coeff_live.astype(jnp.float32)
    integ_float = integrals.astype(jnp.float32)
    beta_ids = beta_block.reshape(-1)
    beta_signs = beta_sign.reshape(NBB, P_SIZE, BLOCK).astype(jnp.float32)
    step_rows = min(16, BLOCK)
    first_rows = jnp.arange(NA // step_rows, dtype=jnp.int32) * step_rows

    def one_block(first_row):
        row_ids = lax.dynamic_slice_in_dim(alpha_row, first_row, step_rows, 1)
        sign_vals = lax.dynamic_slice_in_dim(alpha_sign, first_row, step_rows, 1).astype(jnp.float32)
        replaced = coeff_float[row_ids] * sign_vals[:, :, None]
        mixed = jnp.einsum("qp,prj->qrj", integ_float, replaced, precision=lax.Precision.HIGHEST)
        mixed = mixed.reshape(P_SIZE, step_rows, NBB, BLOCK).transpose(2, 0, 1, 3)
        weighted = mixed * beta_signs[:, :, None, :]
        summed = jax.ops.segment_sum(weighted.reshape(NBB * P_SIZE, step_rows * BLOCK), beta_ids, num_segments=NBB)
        return summed.reshape(NBB, step_rows, BLOCK).transpose(1, 0, 2).reshape(step_rows, NB)

    ab_term = lax.map(one_block, first_rows).reshape(NA, NB)
    total = diagonal * coefficients.astype(jnp.float32) + ab_term
    return jnp.where(live_rows[:, None] == 1, total, jnp.zeros_like(total))
```

```python
import functools

import jax
import jax.numpy as jnp
from jax import lax
from jax.experimental import pallas as pl
from jax.experimental.pallas import tpu as pltpu
from jax.sharding import PartitionSpec as P

LANES = 128
VMEM = pl.BlockSpec(memory_space=pltpu.VMEM)
SMEM = pl.BlockSpec(memory_space=pltpu.SMEM)


def round_up(size, step):
    return -(-size // step) * step


class Sizes:
    def __init__(self, coefficients, integrals, alpha_row, beta_sign, block_irrep):
        self.n_alpha = lax.axis_size("alpha")
        self.n_beta = lax.axis_size("beta")
        self.devices = self.n_alpha * self.n_beta
        self.rows, self.cols = coefficients.shape
        self.pairs = integrals.shape[0]
        self.block = beta_sign.shape[1] // self.pairs
        self.src = self.cols // self.block
        self.targets = self.n_beta * self.src
        self.all_rows = alpha_row.shape[1]
        self.blocks = block_irrep.shape[0]
        self.own = self.rows // self.block
        self.share = max(1, self.devices // self.block)
        self.sets = self.devices // self.share
        self.strings = self.block // self.sets
        self.halves = self.rows // LANES
        self.tiles = self.all_rows // LANES
        self.per = max(1, self.src // self.n_alpha)
        self.senders = self.src // self.per
        self.group = self.src * self.strings
        self.lists = self.n_beta * self.group
        self.pair_rows = round_up(self.pairs, 8)
        self.pair_lanes = round_up(self.pairs, LANES)
        self.pair_tiles = self.pair_lanes // LANES
        self.coef_rows = self.halves * self.group
        self.sign_rows = self.per * self.strings * self.pair_tiles
        self.pack = round_up(self.coef_rows + self.sign_rows, 8)


def pack_kernel(z, coef_ref, sign_ref, out_ref, scratch):
    scratch[...] = jnp.zeros_like(scratch)
    turned = coef_ref[...].astype(jnp.float32).T
    for half in range(z.halves):
        for g in range(z.group):
            row = half * z.group + g
            for part in range(z.share):
                scratch[pl.ds(row + part * z.pack, z.sets, stride=z.share * z.pack), :] = turned[
                    g * z.sets : (g + 1) * z.sets, half * LANES : (half + 1) * LANES
                ]
    for s in range(z.per):
        code = sign_ref[s].T
        code = jnp.concatenate(
            [code, jnp.zeros((z.block, z.pair_lanes - z.pairs), jnp.float32)], axis=1
        )
        for cc in range(z.strings):
            for k in range(z.pair_tiles):
                row = z.coef_rows + (s * z.strings + cc) * z.pair_tiles + k
                for part in range(z.share):
                    scratch[pl.ds(row + part * z.pack, z.sets, stride=z.share * z.pack), :] = code[
                        cc * z.sets : (cc + 1) * z.sets, k * LANES : (k + 1) * LANES
                    ]
    out_ref[...] = scratch[...].astype(jnp.bfloat16)


def main_kernel(
    z,
    irrep_ref,
    part_ref,
    rx_ref,
    integ_ref,
    row_ref,
    sign_ref,
    out_ref,
    rxf,
    full,
    table,
    codes,
    weights,
    lane_of,
    chunk_of,
    sign_of,
    acc,
    result,
    rank_ref,
    list_ref,
):
    f32 = jnp.float32
    half_block = z.block
    count = jnp.int32(0)
    lane_row = lax.broadcasted_iota(jnp.int32, (1, LANES), 1)
    ranks = jnp.full((1, LANES), -1, jnp.int32)
    for g in range(z.blocks):
        live = irrep_ref[g] == 0
        rank = jnp.where(live, count, -1)
        rank_ref[g] = rank
        list_ref[count] = g
        ranks = jnp.where(lane_row == g, rank, ranks)
        count = count + live.astype(jnp.int32)
    list_ref[count] = 0
    n_tiles = (count + 1) // 2

    rxf[...] = rx_ref[...].astype(f32)
    for i in range(z.n_alpha):
        base = i * z.n_beta * z.pack
        for half in range(z.halves):
            for g in range(z.group):
                full[i * z.halves + half, pl.ds(g, z.n_beta, stride=z.group), :] = rxf[
                    pl.ds(base + half * z.group + g, z.n_beta, stride=z.pack), :
                ]
        for s in range(z.per if i < z.senders else 0):
            for cc in range(z.strings):
                for k in range(z.pair_tiles):
                    source = base + z.coef_rows + (s * z.strings + cc) * z.pair_tiles + k
                    dest = (i * z.per + s) * z.strings + cc
                    codes[k, pl.ds(dest, z.n_beta, stride=z.group), :] = rxf[
                        pl.ds(source, z.n_beta, stride=z.pack), :
                    ]

    step = min(8, z.lists)
    target = (lax.broadcasted_iota(jnp.int32, (z.targets, z.pair_lanes), 0) + 1).astype(f32)

    def weight_step(n, carry):
        parts = []
        for m in range(step):
            code = jnp.concatenate(
                [codes[k, pl.ds(n * step + m, 1), :] for k in range(z.pair_tiles)], axis=1
            )
            hit = jnp.where(code == target, 1.0, 0.0) - jnp.where(code == -target, 1.0, 0.0)
            parts.append(hit)
        hits = jnp.concatenate(parts, axis=0).astype(jnp.bfloat16)
        found = jnp.dot(hits, integ_ref[...], preferred_element_type=f32)
        high = found.astype(jnp.bfloat16)
        low = (found - high.astype(f32)).astype(jnp.bfloat16)
        for m in range(step):
            rows = slice(m * z.targets, (m + 1) * z.targets)
            weights[n * step + m, 0 : z.targets, :] = high[rows]
            weights[n * step + m, z.targets : 2 * z.targets, :] = low[rows]
        return carry

    lax.fori_loop(0, z.lists // step, weight_step, 0)

    lane_list = lax.broadcasted_iota(jnp.int32, (z.lists, LANES), 1)
    lane_pair = lax.broadcasted_iota(jnp.int32, (z.pairs, LANES), 1)
    tail = z.pair_rows - 8

    def compact_step(u, carry):
        first, second = list_ref[2 * u], list_ref[2 * u + 1]
        left_shift = (first % 2) * half_block
        right_shift = (1 - second % 2) * half_block
        left = pltpu.roll(full[first // 2], left_shift, 1)
        right = pltpu.roll(full[second // 2], right_shift, 1)
        table[u] = jnp.where(lane_list < half_block, left, right)

        def merged(ref):
            at_first = pl.ds(pl.multiple_of(first // 2 * LANES, LANES), LANES)
            at_second = pl.ds(pl.multiple_of(second // 2 * LANES, LANES), LANES)
            return jnp.where(
                lane_pair < half_block,
                pltpu.roll(ref[:, at_first], left_shift, 1),
                pltpu.roll(ref[:, at_second], right_shift, 1),
            )

        source = merged(row_ref)
        signs = merged(sign_ref)
        block = lax.shift_right_logical(source, 6)
        rank = jnp.take_along_axis(
            jnp.broadcast_to(ranks, (z.pairs, LANES)), block, axis=1, mode="promise_in_bounds"
        )
        spot = rank * half_block + (source & (half_block - 1))
        inside = (lane_pair < half_block) | (2 * u + 1 < count)
        used = (rank >= 0) & (signs != 0) & inside
        lane_of[u, tail : z.pair_rows, :] = jnp.zeros((8, LANES), jnp.int32)
        chunk_of[u, tail : z.pair_rows, :] = jnp.full((8, LANES), -1, jnp.int32)
        sign_of[u, tail : z.pair_rows, :] = jnp.zeros((8, LANES), f32)
        lane_of[u, 0 : z.pairs, :] = spot & (LANES - 1)
        chunk_of[u, 0 : z.pairs, :] = jnp.where(used, lax.shift_right_logical(spot, 7), -1)
        sign_of[u, 0 : z.pairs, :] = signs.astype(f32)
        return carry

    lax.fori_loop(0, n_tiles, compact_step, 0)

    groups = z.pair_rows // 8
    padding = jnp.zeros((z.pair_lanes - z.pair_rows, LANES), f32)

    def run(depth):
        def one_tile(u, carry):
            acc[...] = jnp.zeros_like(acc)

            def one_source(s, inner):
                base = s * z.strings
                pieces = [[] for _ in range(z.strings)]
                tables = [
                    [
                        jnp.broadcast_to(table[k, pl.ds(base + cc, 1), :], (8, LANES))
                        for k in range(depth)
                    ]
                    for cc in range(z.strings)
                ]
                for m in range(groups):
                    at = slice(m * 8, m * 8 + 8)
                    lanes = lane_of[u, at, :]
                    chunk = chunk_of[u, at, :]
                    sign = sign_of[u, at, :]
                    hits = [chunk == k for k in range(depth)]
                    for cc in range(z.strings):
                        value = jnp.zeros((8, LANES), f32)
                        for k in range(depth):
                            taken = jnp.take_along_axis(
                                tables[cc][k], lanes, axis=1, mode="promise_in_bounds"
                            )
                            value = jnp.where(hits[k], taken, value)
                        pieces[cc].append(value * sign)
                for cc in range(z.strings):
                    picked = jnp.concatenate(pieces[cc] + [padding], axis=0)
                    acc[cc] += jnp.dot(
                        weights[base + cc], picked.astype(jnp.bfloat16), preferred_element_type=f32
                    )
                return inner

            lax.fori_loop(0, z.targets, one_source, 0)
            for cc in range(z.strings):
                total = acc[cc, 0 : z.targets, :] + acc[cc, z.targets : 2 * z.targets, :]
                result[u, pl.ds(cc, z.targets, stride=z.strings), :] = total
            return carry

        if z.share == 1:
            lax.fori_loop(0, n_tiles, one_tile, 0)
        else:
            part = part_ref[0]
            mine = (n_tiles - part + z.share - 1) // z.share
            lax.fori_loop(0, mine, lambda n, carry: one_tile(n * z.share + part, carry), 0)

    depths = sorted({min(d, z.tiles) for d in (4, 5, 6, 8, z.tiles)})
    lower = 0
    for depth in depths:
        pl.when((n_tiles > lower) & (n_tiles <= depth))(functools.partial(run, depth))
        lower = depth

    wide = z.src * z.strings
    lane_out = lax.broadcasted_iota(jnp.int32, (z.targets * z.strings, LANES), 1)
    for w in range(z.tiles):
        sides = []
        for side in range(2):
            rank = rank_ref[2 * w + side]
            spot = jnp.maximum(rank, 0)
            shift = ((spot + side) % 2) * half_block
            moved = pltpu.roll(result[spot // 2], shift, 1)
            here = rank >= 0
            if z.share > 1:
                here = here & ((spot // 2) % z.share == part_ref[0])
            sides.append(jnp.where(here, moved, 0.0))
        both = jnp.where(lane_out < half_block, sides[0], sides[1])
        for j in range(z.n_beta):
            device = w // z.halves * z.n_beta + j
            out_ref[device, w % z.halves] = both[j * wide : (j + 1) * wide]


def finish_kernel(z, irrep_ref, rx_ref, diag_ref, coef_ref, out_ref):
    wide = z.src * z.strings
    stride = z.share * z.halves * wide

    def column(first):
        rows = [
            rx_ref[pl.ds(part * z.halves * wide + first, z.sets, stride=stride), :]
            for part in range(z.share)
        ]
        return functools.reduce(jnp.add, rows)

    columns = []
    for t in range(z.src):
        for cc in range(z.strings):
            firsts = [h * wide + t * z.strings + cc for h in range(z.halves)]
            columns.append(jnp.concatenate([column(first) for first in firsts], axis=1))
    added = jnp.concatenate(columns, axis=0).T
    total = diag_ref[...] * coef_ref[...].astype(jnp.float32) + added
    for b in range(z.own):
        at = slice(b * z.block, (b + 1) * z.block)
        out_ref[at, :] = jnp.where(irrep_ref[b] == 0, total[at], 0.0)


def on_device(
    coefficients, diagonal, integrals, alpha_row, alpha_sign, beta_block, beta_sign, block_irrep
):
    z = Sizes(coefficients, integrals, alpha_row, beta_sign, block_irrep)
    f32, i32, bf16 = jnp.float32, jnp.int32, jnp.bfloat16
    alpha_rank = lax.axis_index("alpha")
    params = pltpu.CompilerParams(vmem_limit_bytes=56 * 1024 * 1024)

    first = jnp.minimum(alpha_rank, z.senders - 1) * z.per
    own_signs = lax.dynamic_slice_in_dim(beta_sign, first, z.per, 0)
    own_blocks = lax.dynamic_slice_in_dim(beta_block, first, z.per, 0)
    code = own_signs.reshape(z.per, z.pairs, z.block) * (own_blocks + 1)[:, :, None]
    packed = pl.pallas_call(
        functools.partial(pack_kernel, z),
        out_shape=jax.ShapeDtypeStruct((z.devices * z.pack, LANES), bf16),
        in_specs=[VMEM, VMEM],
        out_specs=VMEM,
        scratch_shapes=[pltpu.VMEM((z.devices * z.pack, LANES), f32)],
        compiler_params=params,
    )(coefficients, code.astype(f32))
    arrived = lax.all_to_all(
        packed.reshape(z.devices, z.pack, LANES), ("alpha", "beta"), 0, 0, tiled=True
    ).reshape(z.devices * z.pack, LANES)

    pad = z.pair_lanes - z.pairs
    wide = z.src * z.strings
    part = (alpha_rank * z.n_beta + lax.axis_index("beta")) % z.share
    integ = jnp.pad(integrals, ((0, pad), (0, pad)))
    terms = pl.pallas_call(
        functools.partial(main_kernel, z),
        out_shape=jax.ShapeDtypeStruct((z.devices, z.halves, wide, LANES), f32),
        in_specs=[SMEM, SMEM, VMEM, VMEM, VMEM, VMEM],
        out_specs=VMEM,
        scratch_shapes=[
            pltpu.VMEM((z.devices * z.pack, LANES), f32),
            pltpu.VMEM((z.tiles, z.lists, LANES), f32),
            pltpu.VMEM((z.tiles, z.lists, LANES), f32),
            pltpu.VMEM((z.pair_tiles, z.lists, LANES), f32),
            pltpu.VMEM((z.lists, 2 * z.targets, z.pair_lanes), bf16),
            pltpu.VMEM((z.tiles, z.pair_rows, LANES), i32),
            pltpu.VMEM((z.tiles, z.pair_rows, LANES), i32),
            pltpu.VMEM((z.tiles, z.pair_rows, LANES), f32),
            pltpu.VMEM((z.strings, 2 * z.targets, LANES), f32),
            pltpu.VMEM((z.tiles, z.targets * z.strings, LANES), f32),
            pltpu.SMEM((z.blocks,), i32),
            pltpu.SMEM((z.blocks + 2,), i32),
        ],
        compiler_params=params,
    )(block_irrep, part.astype(i32)[None], arrived, integ, alpha_row, alpha_sign)

    back = lax.all_to_all(terms, ("alpha", "beta"), 0, 0, tiled=True).reshape(-1, LANES)
    own_irrep = lax.dynamic_slice_in_dim(block_irrep, alpha_rank * z.own, z.own, 0)
    return pl.pallas_call(
        functools.partial(finish_kernel, z),
        out_shape=jax.ShapeDtypeStruct((z.rows, z.cols), f32),
        in_specs=[SMEM, VMEM, VMEM, VMEM],
        out_specs=VMEM,
        compiler_params=params,
    )(own_irrep, back, diagonal, coefficients)


def solution(mesh):
    return jax.shard_map(
        on_device,
        mesh=mesh,
        in_specs=(
            P("alpha", "beta"),
            P("alpha", "beta"),
            P(),
            P(),
            P(),
            P("beta", None),
            P("beta", None),
            P(),
        ),
        out_specs=P("alpha", "beta"),
        check_vma=False,
    )
```

```python
import functools

import jax
import jax.numpy as jnp
from jax import lax
from jax.experimental import pallas as pl
from jax.experimental.pallas import tpu as pltpu
from jax.sharding import PartitionSpec as P

LANES = 128
DEPTH = 256
VMEM = pl.BlockSpec(memory_space=pltpu.VMEM)
SMEM = pl.BlockSpec(memory_space=pltpu.SMEM)


def round_up(size, step):
    return -(-size // step) * step


class Sizes:
    def __init__(self, coefficients, integrals, alpha_row, beta_sign, block_irrep):
        self.n_alpha = lax.axis_size("alpha")
        self.n_beta = lax.axis_size("beta")
        self.devices = self.n_alpha * self.n_beta
        self.rows, self.cols = coefficients.shape
        self.pairs = integrals.shape[0]
        self.block = beta_sign.shape[1] // self.pairs
        self.src = self.cols // self.block
        self.targets = self.n_beta * self.src
        self.all_rows = alpha_row.shape[1]
        self.blocks = block_irrep.shape[0]
        self.own = self.rows // self.block
        self.share = max(1, self.devices // self.block)
        self.sets = self.devices // self.share
        self.strings = self.block // self.sets
        self.halves = self.rows // LANES
        self.tiles = self.all_rows // LANES
        self.per = max(1, self.src // self.n_alpha)
        self.senders = self.src // self.per
        self.group = self.src * self.strings
        self.lists = self.n_beta * self.group
        self.pair_rows = round_up(self.pairs, 8)
        self.chunk_pairs = DEPTH // self.targets
        self.chunks = self.pair_rows // self.chunk_pairs
        self.pair_lanes = round_up(self.pairs, LANES)
        self.pair_tiles = self.pair_lanes // LANES
        self.coef_rows = self.halves * self.group
        self.sign_rows = self.per * self.strings * self.pair_tiles
        self.pack = round_up(self.coef_rows + self.sign_rows, 8)


def pack_kernel(z, coef_ref, sign_ref, out_ref, scratch):
    scratch[...] = jnp.zeros_like(scratch)
    turned = coef_ref[...].astype(jnp.float32).T
    for half in range(z.halves):
        for g in range(z.group):
            row = half * z.group + g
            for part in range(z.share):
                scratch[pl.ds(row + part * z.pack, z.sets, stride=z.share * z.pack), :] = turned[
                    g * z.sets : (g + 1) * z.sets, half * LANES : (half + 1) * LANES
                ]
    for s in range(z.per):
        code = sign_ref[s].T
        code = jnp.concatenate(
            [code, jnp.zeros((z.block, z.pair_lanes - z.pairs), jnp.float32)], axis=1
        )
        for cc in range(z.strings):
            for k in range(z.pair_tiles):
                row = z.coef_rows + (s * z.strings + cc) * z.pair_tiles + k
                for part in range(z.share):
                    scratch[pl.ds(row + part * z.pack, z.sets, stride=z.share * z.pack), :] = code[
                        cc * z.sets : (cc + 1) * z.sets, k * LANES : (k + 1) * LANES
                    ]
    out_ref[...] = scratch[...].astype(jnp.bfloat16)


def main_kernel(
    z,
    irrep_ref,
    part_ref,
    rx_ref,
    integ_ref,
    row_ref,
    sign_ref,
    out_ref,
    rxf,
    full,
    table,
    codes,
    tall,
    weights,
    spot_of,
    chunk_of,
    sign_of,
    acc,
    result,
    rank_ref,
    list_ref,
):
    f32, bf16 = jnp.float32, jnp.bfloat16
    half_block = z.block
    count = jnp.int32(0)
    lane_row = lax.broadcasted_iota(jnp.int32, (1, LANES), 1)
    ranks = jnp.full((1, LANES), -1, jnp.int32)
    for g in range(z.blocks):
        live = irrep_ref[g] == 0
        rank = jnp.where(live, count, -1)
        rank_ref[g] = rank
        list_ref[count] = g
        ranks = jnp.where(lane_row == g, rank, ranks)
        count = count + live.astype(jnp.int32)
    for extra in range(4):
        list_ref[count + extra] = 0
    n_tiles = (count + 1) // 2

    rxf[...] = rx_ref[...].astype(f32)
    for i in range(z.n_alpha):
        base = i * z.n_beta * z.pack
        for half in range(z.halves):
            for s in range(z.src):
                for cc in range(z.strings):
                    source = base + half * z.group + s * z.strings + cc
                    dest = cc * z.targets + s
                    full[i * z.halves + half, pl.ds(dest, z.n_beta, stride=z.src), :] = rxf[
                        pl.ds(source, z.n_beta, stride=z.pack), :
                    ]
        for s in range(z.per if i < z.senders else 0):
            for cc in range(z.strings):
                for k in range(z.pair_tiles):
                    source = base + z.coef_rows + (s * z.strings + cc) * z.pair_tiles + k
                    dest = (i * z.per + s) * z.strings + cc
                    codes[k, pl.ds(dest, z.n_beta, stride=z.group), :] = rxf[
                        pl.ds(source, z.n_beta, stride=z.pack), :
                    ]

    step = 4
    target = (lax.broadcasted_iota(jnp.int32, (z.targets, z.pair_lanes), 0) + 1).astype(f32)

    def weight_step(n, carry):
        parts = []
        for m in range(step * z.strings):
            code = jnp.concatenate(
                [codes[k, pl.ds(n * step * z.strings + m, 1), :] for k in range(z.pair_tiles)],
                axis=1,
            )
            hit = jnp.where(code == target, 1.0, 0.0) - jnp.where(code == -target, 1.0, 0.0)
            parts.append(hit)
        hits = jnp.concatenate(parts, axis=0).astype(bf16)
        found = jnp.dot(hits, integ_ref[...], preferred_element_type=f32)
        high = found.astype(bf16).astype(f32)
        low = found - high
        for m in range(step):
            rows = []
            for cc in range(z.strings):
                at = (m * z.strings + cc) * z.targets
                rows += [high[at : at + z.targets], low[at : at + z.targets]]
            turned = jnp.concatenate(rows, axis=0).T
            tall[pl.ds(n * step + m, z.pair_rows, stride=z.targets), :] = turned[0 : z.pair_rows]
        return carry

    lax.fori_loop(0, z.targets // step, weight_step, 0)

    def turn_step(n, carry):
        at = pl.multiple_of(n * DEPTH, DEPTH)
        weights[n] = tall[pl.ds(at, DEPTH), :].T.astype(bf16)
        return carry

    lax.fori_loop(0, z.chunks, turn_step, 0)

    lane_list = lax.broadcasted_iota(jnp.int32, (z.lists, LANES), 1)
    lane_pair = lax.broadcasted_iota(jnp.int32, (z.pairs, LANES), 1)
    tail = z.pair_rows - 8
    chunk_tiles = DEPTH // LANES

    def compact_step(u, carry):
        first, second = list_ref[2 * u], list_ref[2 * u + 1]
        left_shift = (first % 2) * half_block
        right_shift = (1 - second % 2) * half_block
        left = pltpu.roll(full[first // 2], left_shift, 1)
        right = pltpu.roll(full[second // 2], right_shift, 1)
        left = jnp.where(2 * u < count, left, 0.0)
        right = jnp.where(2 * u + 1 < count, right, 0.0)
        table[u // chunk_tiles, u % chunk_tiles] = jnp.where(
            lane_list < half_block, left, right
        ).astype(bf16)

        def merged(ref):
            at_first = pl.ds(pl.multiple_of(first // 2 * LANES, LANES), LANES)
            at_second = pl.ds(pl.multiple_of(second // 2 * LANES, LANES), LANES)
            return jnp.where(
                lane_pair < half_block,
                pltpu.roll(ref[:, at_first], left_shift, 1),
                pltpu.roll(ref[:, at_second], right_shift, 1),
            )

        source = merged(row_ref)
        signs = merged(sign_ref)
        block = source // half_block
        rank = jnp.take_along_axis(
            jnp.broadcast_to(ranks, (z.pairs, LANES)), block, axis=1, mode="promise_in_bounds"
        )
        spot = rank * half_block + (source & (half_block - 1))
        inside = (lane_pair < half_block) | (2 * u + 1 < count)
        used = (rank >= 0) & inside
        spot_of[u, tail : z.pair_rows, :] = jnp.zeros((8, LANES), f32)
        chunk_of[u, tail : z.pair_rows, :] = jnp.zeros((8, LANES), f32)
        sign_of[u, tail : z.pair_rows, :] = jnp.zeros((8, LANES), f32)
        spot_of[u, 0 : z.pairs, :] = (spot & (DEPTH - 1)).astype(f32)
        chunk_of[u, 0 : z.pairs, :] = (spot // DEPTH).astype(f32)
        sign_of[u, 0 : z.pairs, :] = jnp.where(used, signs, 0).astype(f32)
        return carry

    lax.fori_loop(0, (n_tiles + chunk_tiles - 1) // chunk_tiles * chunk_tiles, compact_step, 0)

    local = lax.broadcasted_iota(jnp.int32, (DEPTH, 2 * LANES), 0).astype(f32)
    side = 2 * z.targets

    def run(depth):
        def one_tile(u, carry):
            acc[...] = jnp.zeros_like(acc)
            lists = jnp.concatenate(
                [
                    jnp.concatenate([table[m, k] for k in range(chunk_tiles)], axis=1)
                    for m in range(depth)
                ],
                axis=0,
            )

            def one_chunk(n, inner):
                pieces = []
                for pair in range(z.chunk_pairs // 2):
                    p = n * z.chunk_pairs + 2 * pair

                    def both(ref):
                        return jnp.concatenate(
                            [ref[u, pl.ds(p, 1), :], ref[u, pl.ds(p + 1, 1), :]], axis=1
                        )

                    pick = jnp.where(local == both(spot_of), both(sign_of), 0.0).astype(bf16)
                    found = jnp.dot(lists, pick, preferred_element_type=f32)
                    value = found[0 : z.lists]
                    chunk = both(chunk_of)
                    for m in range(1, depth):
                        value = jnp.where(chunk == m, found[m * z.lists : (m + 1) * z.lists], value)
                    value = value.astype(bf16)
                    for q in range(2):
                        lanes = slice(q * LANES, (q + 1) * LANES)
                        pieces.append(
                            jnp.concatenate(
                                [
                                    value[cc * z.targets : (cc + 1) * z.targets, lanes]
                                    for cc in range(z.strings)
                                ],
                                axis=1,
                            )
                        )
                picked = jnp.concatenate(pieces, axis=0)
                total = jnp.dot(weights[n], picked, preferred_element_type=f32)
                for cc in range(z.strings):
                    acc[cc] += total[
                        cc * side : (cc + 1) * side, cc * LANES : (cc + 1) * LANES
                    ]
                return inner

            lax.fori_loop(0, z.chunks, one_chunk, 0)
            for cc in range(z.strings):
                total = acc[cc, 0 : z.targets, :] + acc[cc, z.targets : 2 * z.targets, :]
                result[u, pl.ds(cc, z.targets, stride=z.strings), :] = total
            return carry

        if z.share == 1:
            lax.fori_loop(0, n_tiles, one_tile, 0)
        else:
            part = part_ref[0]
            mine = (n_tiles - part + z.share - 1) // z.share
            lax.fori_loop(0, mine, lambda n, carry: one_tile(n * z.share + part, carry), 0)

    most = z.tiles // chunk_tiles
    lower = 0
    for depth in sorted({min(d, most) for d in (2, 3, 4, most)}):
        pl.when((count > lower) & (count <= depth * DEPTH // z.block))(
            functools.partial(run, depth)
        )
        lower = depth * DEPTH // z.block

    wide = z.src * z.strings
    lane_out = lax.broadcasted_iota(jnp.int32, (z.targets * z.strings, LANES), 1)
    for w in range(z.tiles):
        sides = []
        for at_side in range(2):
            rank = rank_ref[2 * w + at_side]
            spot = jnp.maximum(rank, 0)
            shift = ((spot + at_side) % 2) * half_block
            moved = pltpu.roll(result[spot // 2], shift, 1)
            here = rank >= 0
            if z.share > 1:
                here = here & ((spot // 2) % z.share == part_ref[0])
            sides.append(jnp.where(here, moved, 0.0))
        both = jnp.where(lane_out < half_block, sides[0], sides[1])
        for j in range(z.n_beta):
            device = w // z.halves * z.n_beta + j
            out_ref[device, w % z.halves] = both[j * wide : (j + 1) * wide]


def finish_kernel(z, irrep_ref, rx_ref, diag_ref, coef_ref, out_ref):
    wide = z.src * z.strings
    stride = z.share * z.halves * wide

    def column(first):
        rows = [
            rx_ref[pl.ds(part * z.halves * wide + first, z.sets, stride=stride), :]
            for part in range(z.share)
        ]
        return functools.reduce(jnp.add, rows)

    columns = []
    for t in range(z.src):
        for cc in range(z.strings):
            firsts = [h * wide + t * z.strings + cc for h in range(z.halves)]
            columns.append(jnp.concatenate([column(first) for first in firsts], axis=1))
    added = jnp.concatenate(columns, axis=0).T
    total = diag_ref[...] * coef_ref[...].astype(jnp.float32) + added
    for b in range(z.own):
        at = slice(b * z.block, (b + 1) * z.block)
        out_ref[at, :] = jnp.where(irrep_ref[b] == 0, total[at], 0.0)


def on_device(
    coefficients, diagonal, integrals, alpha_row, alpha_sign, beta_block, beta_sign, block_irrep
):
    z = Sizes(coefficients, integrals, alpha_row, beta_sign, block_irrep)
    f32, i32, bf16 = jnp.float32, jnp.int32, jnp.bfloat16
    alpha_rank = lax.axis_index("alpha")
    params = pltpu.CompilerParams(vmem_limit_bytes=56 * 1024 * 1024)

    first = jnp.minimum(alpha_rank, z.senders - 1) * z.per
    own_signs = lax.dynamic_slice_in_dim(beta_sign, first, z.per, 0)
    own_blocks = lax.dynamic_slice_in_dim(beta_block, first, z.per, 0)
    code = own_signs.reshape(z.per, z.pairs, z.block) * (own_blocks + 1)[:, :, None]
    packed = pl.pallas_call(
        functools.partial(pack_kernel, z),
        out_shape=jax.ShapeDtypeStruct((z.devices * z.pack, LANES), bf16),
        in_specs=[VMEM, VMEM],
        out_specs=VMEM,
        scratch_shapes=[pltpu.VMEM((z.devices * z.pack, LANES), f32)],
        compiler_params=params,
    )(coefficients, code.astype(f32))
    arrived = lax.all_to_all(
        packed.reshape(z.devices, z.pack, LANES), ("alpha", "beta"), 0, 0, tiled=True
    ).reshape(z.devices * z.pack, LANES)

    pad = z.pair_lanes - z.pairs
    wide = z.src * z.strings
    part = (alpha_rank * z.n_beta + lax.axis_index("beta")) % z.share
    integ = jnp.pad(integrals, ((0, pad), (0, pad)))
    terms = pl.pallas_call(
        functools.partial(main_kernel, z),
        out_shape=jax.ShapeDtypeStruct((z.devices, z.halves, wide, LANES), f32),
        in_specs=[SMEM, SMEM, VMEM, VMEM, VMEM, VMEM],
        out_specs=VMEM,
        scratch_shapes=[
            pltpu.VMEM((z.devices * z.pack, LANES), f32),
            pltpu.VMEM((z.tiles, z.lists, LANES), f32),
            pltpu.VMEM((z.tiles * LANES // DEPTH, DEPTH // LANES, z.lists, LANES), bf16),
            pltpu.VMEM((z.pair_tiles, z.lists, LANES), f32),
            pltpu.VMEM((z.pair_rows * z.targets, LANES), f32),
            pltpu.VMEM((z.chunks, LANES, DEPTH), bf16),
            pltpu.VMEM((z.tiles, z.pair_rows, LANES), f32),
            pltpu.VMEM((z.tiles, z.pair_rows, LANES), f32),
            pltpu.VMEM((z.tiles, z.pair_rows, LANES), f32),
            pltpu.VMEM((z.strings, 2 * z.targets, LANES), f32),
            pltpu.VMEM((z.tiles, z.targets * z.strings, LANES), f32),
            pltpu.SMEM((z.blocks,), i32),
            pltpu.SMEM((z.blocks + 8,), i32),
        ],
        compiler_params=params,
    )(block_irrep, part.astype(i32)[None], arrived, integ, alpha_row, alpha_sign)

    back = lax.all_to_all(terms, ("alpha", "beta"), 0, 0, tiled=True).reshape(-1, LANES)
    own_irrep = lax.dynamic_slice_in_dim(block_irrep, alpha_rank * z.own, z.own, 0)
    return pl.pallas_call(
        functools.partial(finish_kernel, z),
        out_shape=jax.ShapeDtypeStruct((z.rows, z.cols), f32),
        in_specs=[SMEM, VMEM, VMEM, VMEM],
        out_specs=VMEM,
        compiler_params=params,
    )(own_irrep, back, diagonal, coefficients)


def solution(mesh):
    return jax.shard_map(
        on_device,
        mesh=mesh,
        in_specs=(
            P("alpha", "beta"),
            P("alpha", "beta"),
            P(),
            P(),
            P(),
            P("beta", None),
            P("beta", None),
            P(),
        ),
        out_specs=P("alpha", "beta"),
        check_vma=False,
    )
```

```python
import functools

import jax
import jax.numpy as jnp
from jax import lax
from jax.experimental import pallas as pl
from jax.experimental.pallas import tpu as pltpu
from jax.sharding import PartitionSpec as P

LANES = 128
DEPTH = 256
VMEM = pl.BlockSpec(memory_space=pltpu.VMEM)
SMEM = pl.BlockSpec(memory_space=pltpu.SMEM)


def round_up(size, step):
    return -(-size // step) * step


class Sizes:
    def __init__(self, coefficients, integrals, alpha_row, beta_sign, block_irrep):
        self.n_alpha = lax.axis_size("alpha")
        self.n_beta = lax.axis_size("beta")
        self.devices = self.n_alpha * self.n_beta
        self.rows, self.cols = coefficients.shape
        self.pairs = integrals.shape[0]
        self.block = beta_sign.shape[1] // self.pairs
        self.src = self.cols // self.block
        self.targets = self.n_beta * self.src
        self.all_rows = alpha_row.shape[1]
        self.blocks = block_irrep.shape[0]
        self.own = self.rows // self.block
        self.share = max(1, self.devices // self.block)
        self.sets = self.devices // self.share
        self.strings = self.block // self.sets
        self.halves = self.rows // LANES
        self.tiles = self.all_rows // LANES
        self.per = max(1, self.src // self.n_alpha)
        self.senders = self.src // self.per
        self.group = self.src * self.strings
        self.lists = self.n_beta * self.group
        self.pair_rows = round_up(self.pairs, 8)
        self.chunk_pairs = DEPTH // self.targets
        self.chunks = self.pair_rows // self.chunk_pairs
        self.pair_lanes = round_up(self.pairs, LANES)
        self.pair_tiles = self.pair_lanes // LANES
        self.coef_rows = self.halves * self.group
        self.sign_rows = self.per * self.strings * self.pair_tiles
        self.pack = round_up(self.coef_rows + self.sign_rows, 8)


def pack_kernel(z, coef_ref, sign_ref, out_ref, scratch):
    scratch[...] = jnp.zeros_like(scratch)
    turned = coef_ref[...].astype(jnp.float32).T
    for half in range(z.halves):
        for g in range(z.group):
            row = half * z.group + g
            for part in range(z.share):
                scratch[pl.ds(row + part * z.pack, z.sets, stride=z.share * z.pack), :] = turned[
                    g * z.sets : (g + 1) * z.sets, half * LANES : (half + 1) * LANES
                ]
    for s in range(z.per):
        code = sign_ref[s].T
        code = jnp.concatenate(
            [code, jnp.zeros((z.block, z.pair_lanes - z.pairs), jnp.float32)], axis=1
        )
        for cc in range(z.strings):
            for k in range(z.pair_tiles):
                row = z.coef_rows + (s * z.strings + cc) * z.pair_tiles + k
                for part in range(z.share):
                    scratch[pl.ds(row + part * z.pack, z.sets, stride=z.share * z.pack), :] = code[
                        cc * z.sets : (cc + 1) * z.sets, k * LANES : (k + 1) * LANES
                    ]
    out_ref[...] = scratch[...].astype(jnp.bfloat16)


def main_kernel(
    z,
    irrep_ref,
    part_ref,
    rx_ref,
    integ_ref,
    row_ref,
    sign_ref,
    out_ref,
    rxf,
    full,
    table,
    codes,
    tall,
    weights,
    spot_of,
    chunk_of,
    sign_of,
    acc,
    held,
    result,
    rank_ref,
    list_ref,
):
    f32, bf16 = jnp.float32, jnp.bfloat16
    half_block = z.block
    count = jnp.int32(0)
    lane_row = lax.broadcasted_iota(jnp.int32, (1, LANES), 1)
    ranks = jnp.full((1, LANES), -1, jnp.int32)
    for g in range(z.blocks):
        live = irrep_ref[g] == 0
        rank = jnp.where(live, count, -1)
        rank_ref[g] = rank
        list_ref[count] = g
        ranks = jnp.where(lane_row == g, rank, ranks)
        count = count + live.astype(jnp.int32)
    for extra in range(4):
        list_ref[count + extra] = 0
    n_tiles = (count + 1) // 2

    rxf[...] = rx_ref[...].astype(f32)
    for i in range(z.n_alpha):
        base = i * z.n_beta * z.pack
        for half in range(z.halves):
            for s in range(z.src):
                for cc in range(z.strings):
                    source = base + half * z.group + s * z.strings + cc
                    dest = cc * z.targets + s
                    full[i * z.halves + half, pl.ds(dest, z.n_beta, stride=z.src), :] = rxf[
                        pl.ds(source, z.n_beta, stride=z.pack), :
                    ]
        for s in range(z.per if i < z.senders else 0):
            for cc in range(z.strings):
                for k in range(z.pair_tiles):
                    source = base + z.coef_rows + (s * z.strings + cc) * z.pair_tiles + k
                    dest = (i * z.per + s) * z.strings + cc
                    codes[k, pl.ds(dest, z.n_beta, stride=z.group), :] = rxf[
                        pl.ds(source, z.n_beta, stride=z.pack), :
                    ]

    step = 4
    target = (lax.broadcasted_iota(jnp.int32, (z.targets, z.pair_lanes), 0) + 1).astype(f32)

    def weight_step(n, carry):
        parts = []
        for m in range(step * z.strings):
            code = jnp.concatenate(
                [codes[k, pl.ds(n * step * z.strings + m, 1), :] for k in range(z.pair_tiles)],
                axis=1,
            )
            hit = jnp.where(code == target, 1.0, 0.0) - jnp.where(code == -target, 1.0, 0.0)
            parts.append(hit)
        hits = jnp.concatenate(parts, axis=0).astype(bf16)
        found = jnp.dot(hits, integ_ref[...], preferred_element_type=f32)
        high = found.astype(bf16).astype(f32)
        low = found - high
        for m in range(step):
            rows = []
            for cc in range(z.strings):
                at = (m * z.strings + cc) * z.targets
                rows += [high[at : at + z.targets], low[at : at + z.targets]]
            turned = jnp.concatenate(rows, axis=0).T
            tall[pl.ds(n * step + m, z.pair_rows, stride=z.targets), :] = turned[0 : z.pair_rows]
        return carry

    lax.fori_loop(0, z.targets // step, weight_step, 0)

    def turn_step(n, carry):
        at = pl.multiple_of(n * DEPTH, DEPTH)
        weights[n] = tall[pl.ds(at, DEPTH), :].T.astype(bf16)
        return carry

    lax.fori_loop(0, z.chunks, turn_step, 0)

    lane_list = lax.broadcasted_iota(jnp.int32, (z.lists, LANES), 1)
    lane_pair = lax.broadcasted_iota(jnp.int32, (z.pairs, LANES), 1)
    tail = z.pair_rows - 8
    chunk_tiles = DEPTH // LANES

    def compact_step(u, carry):
        first, second = list_ref[2 * u], list_ref[2 * u + 1]
        left_shift = (first % 2) * half_block
        right_shift = (1 - second % 2) * half_block
        left = pltpu.roll(full[first // 2], left_shift, 1)
        right = pltpu.roll(full[second // 2], right_shift, 1)
        left = jnp.where(2 * u < count, left, 0.0)
        right = jnp.where(2 * u + 1 < count, right, 0.0)
        at_list = pl.ds(pl.multiple_of(u // chunk_tiles * z.lists, z.lists), z.lists)
        at_lane = pl.ds(pl.multiple_of(u % chunk_tiles * LANES, LANES), LANES)
        table[at_list, at_lane] = jnp.where(lane_list < half_block, left, right).astype(bf16)

        def merged(ref):
            at_first = pl.ds(pl.multiple_of(first // 2 * LANES, LANES), LANES)
            at_second = pl.ds(pl.multiple_of(second // 2 * LANES, LANES), LANES)
            return jnp.where(
                lane_pair < half_block,
                pltpu.roll(ref[:, at_first], left_shift, 1),
                pltpu.roll(ref[:, at_second], right_shift, 1),
            )

        source = merged(row_ref)
        signs = merged(sign_ref)
        block = source // half_block
        rank = jnp.take_along_axis(
            jnp.broadcast_to(ranks, (z.pairs, LANES)), block, axis=1, mode="promise_in_bounds"
        )
        spot = rank * half_block + (source & (half_block - 1))
        inside = (lane_pair < half_block) | (2 * u + 1 < count)
        used = (rank >= 0) & inside
        spot_of[u, tail : z.pair_rows, :] = jnp.zeros((8, LANES), f32)
        chunk_of[u, tail : z.pair_rows, :] = jnp.zeros((8, LANES), f32)
        sign_of[u, tail : z.pair_rows, :] = jnp.zeros((8, LANES), f32)
        spot_of[u, 0 : z.pairs, :] = (spot & (DEPTH - 1)).astype(f32)
        chunk_of[u, 0 : z.pairs, :] = (spot // DEPTH).astype(f32)
        sign_of[u, 0 : z.pairs, :] = jnp.where(used, signs, 0).astype(f32)
        return carry

    lax.fori_loop(0, (n_tiles + chunk_tiles - 1) // chunk_tiles * chunk_tiles, compact_step, 0)

    local = lax.broadcasted_iota(jnp.int32, (DEPTH, LANES), 0).astype(f32)
    side = 2 * z.targets

    def run(depth):
        def one_tile(u, carry):
            acc[...] = jnp.zeros_like(acc)
            held[...] = jnp.zeros_like(held)

            def spread(n):
                total = jnp.dot(weights[n], held[...], preferred_element_type=f32)
                for cc in range(z.strings):
                    acc[cc] += total[
                        cc * side : (cc + 1) * side, cc * LANES : (cc + 1) * LANES
                    ]

            def one_chunk(n, inner):
                spread(jnp.maximum(n - 1, 0))
                picks, chunk = [], []
                for q in range(z.chunk_pairs):
                    at = pl.ds(n * z.chunk_pairs + q, 1)
                    picks.append(jnp.where(local == spot_of[u, at, :], sign_of[u, at, :], 0.0))
                    chunk.append(chunk_of[u, at, :])
                pick = jnp.concatenate([one.astype(bf16) for one in picks], axis=1)
                found = jnp.dot(
                    table[0 : depth * z.lists, :], pick, preferred_element_type=f32
                )
                for q in range(z.chunk_pairs):
                    lanes = slice(q * LANES, (q + 1) * LANES)
                    value = found[0 : z.lists, lanes]
                    for m in range(1, depth):
                        other = found[m * z.lists : (m + 1) * z.lists, lanes]
                        value = jnp.where(chunk[q] == m, other, value)
                    value = value.astype(bf16)
                    for cc in range(z.strings):
                        held[
                            q * z.targets : (q + 1) * z.targets, cc * LANES : (cc + 1) * LANES
                        ] = value[cc * z.targets : (cc + 1) * z.targets]
                return inner

            lax.fori_loop(0, z.chunks, one_chunk, 0)
            spread(z.chunks - 1)
            for cc in range(z.strings):
                total = acc[cc, 0 : z.targets, :] + acc[cc, z.targets : 2 * z.targets, :]
                result[u, pl.ds(cc, z.targets, stride=z.strings), :] = total
            return carry

        if z.share == 1:
            lax.fori_loop(0, n_tiles, one_tile, 0)
        else:
            part = part_ref[0]
            mine = (n_tiles - part + z.share - 1) // z.share
            lax.fori_loop(0, mine, lambda n, carry: one_tile(n * z.share + part, carry), 0)

    most = z.tiles // chunk_tiles
    lower = 0
    for depth in sorted({min(d, most) for d in (2, 3, 4, most)}):
        pl.when((count > lower) & (count <= depth * DEPTH // z.block))(
            functools.partial(run, depth)
        )
        lower = depth * DEPTH // z.block

    wide = z.src * z.strings
    lane_out = lax.broadcasted_iota(jnp.int32, (z.targets * z.strings, LANES), 1)
    for w in range(z.tiles):
        sides = []
        for at_side in range(2):
            rank = rank_ref[2 * w + at_side]
            spot = jnp.maximum(rank, 0)
            shift = ((spot + at_side) % 2) * half_block
            moved = pltpu.roll(result[spot // 2], shift, 1)
            here = rank >= 0
            if z.share > 1:
                here = here & ((spot // 2) % z.share == part_ref[0])
            sides.append(jnp.where(here, moved, 0.0))
        both = jnp.where(lane_out < half_block, sides[0], sides[1])
        for j in range(z.n_beta):
            device = w // z.halves * z.n_beta + j
            out_ref[device, w % z.halves] = both[j * wide : (j + 1) * wide]


def finish_kernel(z, irrep_ref, rx_ref, diag_ref, coef_ref, out_ref):
    wide = z.src * z.strings
    stride = z.share * z.halves * wide

    def column(first):
        rows = [
            rx_ref[pl.ds(part * z.halves * wide + first, z.sets, stride=stride), :]
            for part in range(z.share)
        ]
        return functools.reduce(jnp.add, rows)

    columns = []
    for t in range(z.src):
        for cc in range(z.strings):
            firsts = [h * wide + t * z.strings + cc for h in range(z.halves)]
            columns.append(jnp.concatenate([column(first) for first in firsts], axis=1))
    added = jnp.concatenate(columns, axis=0).T
    total = diag_ref[...] * coef_ref[...].astype(jnp.float32) + added
    for b in range(z.own):
        at = slice(b * z.block, (b + 1) * z.block)
        out_ref[at, :] = jnp.where(irrep_ref[b] == 0, total[at], 0.0)


def on_device(
    coefficients, diagonal, integrals, alpha_row, alpha_sign, beta_block, beta_sign, block_irrep
):
    z = Sizes(coefficients, integrals, alpha_row, beta_sign, block_irrep)
    f32, i32, bf16 = jnp.float32, jnp.int32, jnp.bfloat16
    alpha_rank = lax.axis_index("alpha")
    params = pltpu.CompilerParams(vmem_limit_bytes=56 * 1024 * 1024)

    first = jnp.minimum(alpha_rank, z.senders - 1) * z.per
    own_signs = lax.dynamic_slice_in_dim(beta_sign, first, z.per, 0)
    own_blocks = lax.dynamic_slice_in_dim(beta_block, first, z.per, 0)
    code = own_signs.reshape(z.per, z.pairs, z.block) * (own_blocks + 1)[:, :, None]
    packed = pl.pallas_call(
        functools.partial(pack_kernel, z),
        out_shape=jax.ShapeDtypeStruct((z.devices * z.pack, LANES), bf16),
        in_specs=[VMEM, VMEM],
        out_specs=VMEM,
        scratch_shapes=[pltpu.VMEM((z.devices * z.pack, LANES), f32)],
        compiler_params=params,
    )(coefficients, code.astype(f32))
    arrived = lax.all_to_all(
        packed.reshape(z.devices, z.pack, LANES), ("alpha", "beta"), 0, 0, tiled=True
    ).reshape(z.devices * z.pack, LANES)

    pad = z.pair_lanes - z.pairs
    wide = z.src * z.strings
    part = (alpha_rank * z.n_beta + lax.axis_index("beta")) % z.share
    integ = jnp.pad(integrals, ((0, pad), (0, pad)))
    terms = pl.pallas_call(
        functools.partial(main_kernel, z),
        out_shape=jax.ShapeDtypeStruct((z.devices, z.halves, wide, LANES), f32),
        in_specs=[SMEM, SMEM, VMEM, VMEM, VMEM, VMEM],
        out_specs=VMEM,
        scratch_shapes=[
            pltpu.VMEM((z.devices * z.pack, LANES), f32),
            pltpu.VMEM((z.tiles, z.lists, LANES), f32),
            pltpu.VMEM((z.tiles * LANES // DEPTH * z.lists, DEPTH), bf16),
            pltpu.VMEM((z.pair_tiles, z.lists, LANES), f32),
            pltpu.VMEM((z.pair_rows * z.targets, LANES), f32),
            pltpu.VMEM((z.chunks, LANES, DEPTH), bf16),
            pltpu.VMEM((z.tiles, z.pair_rows, LANES), f32),
            pltpu.VMEM((z.tiles, z.pair_rows, LANES), f32),
            pltpu.VMEM((z.tiles, z.pair_rows, LANES), f32),
            pltpu.VMEM((z.strings, 2 * z.targets, LANES), f32),
            pltpu.VMEM((DEPTH, z.strings * LANES), bf16),
            pltpu.VMEM((z.tiles, z.targets * z.strings, LANES), f32),
            pltpu.SMEM((z.blocks,), i32),
            pltpu.SMEM((z.blocks + 8,), i32),
        ],
        compiler_params=params,
    )(block_irrep, part.astype(i32)[None], arrived, integ, alpha_row, alpha_sign)

    back = lax.all_to_all(terms, ("alpha", "beta"), 0, 0, tiled=True).reshape(-1, LANES)
    own_irrep = lax.dynamic_slice_in_dim(block_irrep, alpha_rank * z.own, z.own, 0)
    return pl.pallas_call(
        functools.partial(finish_kernel, z),
        out_shape=jax.ShapeDtypeStruct((z.rows, z.cols), f32),
        in_specs=[SMEM, VMEM, VMEM, VMEM],
        out_specs=VMEM,
        compiler_params=params,
    )(own_irrep, back, diagonal, coefficients)


def solution(mesh):
    return jax.shard_map(
        on_device,
        mesh=mesh,
        in_specs=(
            P("alpha", "beta"),
            P("alpha", "beta"),
            P(),
            P(),
            P(),
            P("beta", None),
            P("beta", None),
            P(),
        ),
        out_specs=P("alpha", "beta"),
        check_vma=False,
    )
```

```python
import functools

import jax
import jax.numpy as jnp
from jax import lax
from jax.experimental import pallas as pl
from jax.experimental.pallas import tpu as pltpu
from jax.sharding import PartitionSpec as P

LANES = 128
DEPTH = 512
SPAN = 256
VMEM = pl.BlockSpec(memory_space=pltpu.VMEM)
SMEM = pl.BlockSpec(memory_space=pltpu.SMEM)


def round_up(size, step):
    return -(-size // step) * step


class Sizes:
    def __init__(self, coefficients, integrals, alpha_row, beta_sign, block_irrep):
        self.n_alpha = lax.axis_size("alpha")
        self.n_beta = lax.axis_size("beta")
        self.devices = self.n_alpha * self.n_beta
        self.rows, self.cols = coefficients.shape
        self.pairs = integrals.shape[0]
        self.block = beta_sign.shape[1] // self.pairs
        self.src = self.cols // self.block
        self.targets = self.n_beta * self.src
        self.all_rows = alpha_row.shape[1]
        self.blocks = block_irrep.shape[0]
        self.own = self.rows // self.block
        self.share = max(1, self.devices // self.block)
        self.sets = self.devices // self.share
        self.strings = self.block // self.sets
        self.halves = self.rows // LANES
        self.tiles = self.all_rows // LANES
        self.per = max(1, self.src // self.n_alpha)
        self.senders = self.src // self.per
        self.group = self.src * self.strings
        self.lists = self.n_beta * self.group
        self.chunk_pairs = DEPTH // self.targets
        self.pair_rows = round_up(self.pairs, self.chunk_pairs)
        self.chunks = self.pair_rows // self.chunk_pairs
        self.pair_lanes = round_up(self.pairs, LANES)
        self.pair_tiles = self.pair_lanes // LANES
        self.coef_rows = self.halves * self.group
        self.sign_rows = self.per * self.strings * self.pair_tiles
        self.pack = round_up(self.coef_rows + self.sign_rows, 8)


def pack_kernel(z, coef_ref, sign_ref, out_ref, scratch):
    scratch[...] = jnp.zeros_like(scratch)
    turned = coef_ref[...].astype(jnp.float32).T
    for half in range(z.halves):
        for g in range(z.group):
            row = half * z.group + g
            for part in range(z.share):
                scratch[pl.ds(row + part * z.pack, z.sets, stride=z.share * z.pack), :] = turned[
                    g * z.sets : (g + 1) * z.sets, half * LANES : (half + 1) * LANES
                ]
    for s in range(z.per):
        code = sign_ref[s].T
        code = jnp.concatenate(
            [code, jnp.zeros((z.block, z.pair_lanes - z.pairs), jnp.float32)], axis=1
        )
        for cc in range(z.strings):
            for k in range(z.pair_tiles):
                row = z.coef_rows + (s * z.strings + cc) * z.pair_tiles + k
                for part in range(z.share):
                    scratch[pl.ds(row + part * z.pack, z.sets, stride=z.share * z.pack), :] = code[
                        cc * z.sets : (cc + 1) * z.sets, k * LANES : (k + 1) * LANES
                    ]
    out_ref[...] = scratch[...].astype(jnp.bfloat16)


def main_kernel(
    z,
    irrep_ref,
    part_ref,
    rx_ref,
    integ_ref,
    row_ref,
    sign_ref,
    out_ref,
    rxf,
    full,
    table,
    codes,
    tall,
    weights,
    spot_of,
    chunk_of,
    sign_of,
    acc,
    held,
    result,
    rank_ref,
    list_ref,
):
    f32, bf16 = jnp.float32, jnp.bfloat16
    half_block = z.block
    count = jnp.int32(0)
    lane_row = lax.broadcasted_iota(jnp.int32, (1, LANES), 1)
    ranks = jnp.full((1, LANES), -1, jnp.int32)
    for g in range(z.blocks):
        live = irrep_ref[g] == 0
        rank = jnp.where(live, count, -1)
        rank_ref[g] = rank
        list_ref[count] = g
        ranks = jnp.where(lane_row == g, rank, ranks)
        count = count + live.astype(jnp.int32)
    for extra in range(4):
        list_ref[count + extra] = 0
    n_tiles = (count + 1) // 2

    rxf[...] = rx_ref[...].astype(f32)
    for i in range(z.n_alpha):
        base = i * z.n_beta * z.pack
        for half in range(z.halves):
            for s in range(z.src):
                for cc in range(z.strings):
                    source = base + half * z.group + s * z.strings + cc
                    dest = cc * z.targets + s
                    full[i * z.halves + half, pl.ds(dest, z.n_beta, stride=z.src), :] = rxf[
                        pl.ds(source, z.n_beta, stride=z.pack), :
                    ]
        for s in range(z.per if i < z.senders else 0):
            for cc in range(z.strings):
                for k in range(z.pair_tiles):
                    source = base + z.coef_rows + (s * z.strings + cc) * z.pair_tiles + k
                    dest = (i * z.per + s) * z.strings + cc
                    codes[k, pl.ds(dest, z.n_beta, stride=z.group), :] = rxf[
                        pl.ds(source, z.n_beta, stride=z.pack), :
                    ]

    step = 4
    target = (lax.broadcasted_iota(jnp.int32, (z.targets, z.pair_lanes), 0) + 1).astype(f32)

    def weight_step(n, carry):
        parts = []
        for m in range(step * z.strings):
            code = jnp.concatenate(
                [codes[k, pl.ds(n * step * z.strings + m, 1), :] for k in range(z.pair_tiles)],
                axis=1,
            )
            hit = jnp.where(code == target, 1.0, 0.0) - jnp.where(code == -target, 1.0, 0.0)
            parts.append(hit)
        hits = jnp.concatenate(parts, axis=0).astype(bf16)
        found = jnp.dot(hits, integ_ref[...], preferred_element_type=f32)
        high = found.astype(bf16).astype(f32)
        low = found - high
        for m in range(step):
            rows = []
            for cc in range(z.strings):
                at = (m * z.strings + cc) * z.targets
                rows += [high[at : at + z.targets], low[at : at + z.targets]]
            turned = jnp.concatenate(rows, axis=0).T
            tall[pl.ds(n * step + m, z.pair_rows, stride=z.targets), :] = turned[0 : z.pair_rows]
        return carry

    lax.fori_loop(0, z.targets // step, weight_step, 0)

    def turn_step(n, carry):
        at = pl.multiple_of(n * DEPTH, DEPTH)
        weights[n] = tall[pl.ds(at, DEPTH), :].T.astype(bf16)
        return carry

    lax.fori_loop(0, z.chunks, turn_step, 0)

    lane_list = lax.broadcasted_iota(jnp.int32, (z.lists, LANES), 1)
    lane_pair = lax.broadcasted_iota(jnp.int32, (z.pairs, LANES), 1)
    tail = z.pairs // 8 * 8
    chunk_tiles = SPAN // LANES

    def compact_step(u, carry):
        first, second = list_ref[2 * u], list_ref[2 * u + 1]
        left_shift = (first % 2) * half_block
        right_shift = (1 - second % 2) * half_block
        left = pltpu.roll(full[first // 2], left_shift, 1)
        right = pltpu.roll(full[second // 2], right_shift, 1)
        left = jnp.where(2 * u < count, left, 0.0)
        right = jnp.where(2 * u + 1 < count, right, 0.0)
        at_list = pl.ds(pl.multiple_of(u // chunk_tiles * z.lists, z.lists), z.lists)
        at_lane = pl.ds(pl.multiple_of(u % chunk_tiles * LANES, LANES), LANES)
        table[at_list, at_lane] = jnp.where(lane_list < half_block, left, right).astype(bf16)

        def merged(ref):
            at_first = pl.ds(pl.multiple_of(first // 2 * LANES, LANES), LANES)
            at_second = pl.ds(pl.multiple_of(second // 2 * LANES, LANES), LANES)
            return jnp.where(
                lane_pair < half_block,
                pltpu.roll(ref[:, at_first], left_shift, 1),
                pltpu.roll(ref[:, at_second], right_shift, 1),
            )

        source = merged(row_ref)
        signs = merged(sign_ref)
        block = source // half_block
        rank = jnp.take_along_axis(
            jnp.broadcast_to(ranks, (z.pairs, LANES)), block, axis=1, mode="promise_in_bounds"
        )
        spot = rank * half_block + (source & (half_block - 1))
        inside = (lane_pair < half_block) | (2 * u + 1 < count)
        used = (rank >= 0) & inside
        spot_of[u, tail : z.pair_rows, :] = jnp.zeros((z.pair_rows - tail, LANES), f32)
        chunk_of[u, tail : z.pair_rows, :] = jnp.zeros((z.pair_rows - tail, LANES), f32)
        sign_of[u, tail : z.pair_rows, :] = jnp.zeros((z.pair_rows - tail, LANES), f32)
        spot_of[u, 0 : z.pairs, :] = (spot & (SPAN - 1)).astype(f32)
        chunk_of[u, 0 : z.pairs, :] = (spot // SPAN).astype(f32)
        sign_of[u, 0 : z.pairs, :] = jnp.where(used, signs, 0).astype(f32)
        return carry

    lax.fori_loop(0, (n_tiles + chunk_tiles - 1) // chunk_tiles * chunk_tiles, compact_step, 0)

    local = lax.broadcasted_iota(jnp.int32, (SPAN, LANES), 0).astype(f32).astype(bf16)
    nothing = jnp.zeros((SPAN, LANES), bf16)
    side = 2 * z.targets

    def tall_row(row):
        few = jnp.broadcast_to(row, (16, LANES)).astype(bf16)
        return jnp.concatenate([few] * (SPAN // 16), axis=0)

    def run(depth):
        def one_tile(u, carry):
            acc[...] = jnp.zeros_like(acc)
            held[...] = jnp.zeros_like(held)

            def spread(n):
                total = jnp.dot(weights[n], held[...], preferred_element_type=f32)
                for cc in range(z.strings):
                    acc[cc] += total[
                        cc * side : (cc + 1) * side, cc * LANES : (cc + 1) * LANES
                    ]

            def one_chunk(n, inner):
                spread(jnp.maximum(n - 1, 0))
                picks, chunk = [], []
                for q in range(z.chunk_pairs):
                    at = pl.ds(n * z.chunk_pairs + q, 1)
                    hit = local == tall_row(spot_of[u, at, :])
                    picks.append(jnp.where(hit, tall_row(sign_of[u, at, :]), nothing))
                    chunk.append(chunk_of[u, at, :])
                pick = jnp.concatenate(picks, axis=1)
                found = jnp.dot(
                    table[0 : depth * z.lists, :], pick, preferred_element_type=f32
                )
                for q in range(z.chunk_pairs):
                    lanes = slice(q * LANES, (q + 1) * LANES)
                    value = found[0 : z.lists, lanes]
                    for m in range(1, depth):
                        other = found[m * z.lists : (m + 1) * z.lists, lanes]
                        value = jnp.where(chunk[q] == m, other, value)
                    value = value.astype(bf16)
                    for cc in range(z.strings):
                        held[
                            q * z.targets : (q + 1) * z.targets, cc * LANES : (cc + 1) * LANES
                        ] = value[cc * z.targets : (cc + 1) * z.targets]
                return inner

            lax.fori_loop(0, z.chunks, one_chunk, 0)
            spread(z.chunks - 1)
            for cc in range(z.strings):
                total = acc[cc, 0 : z.targets, :] + acc[cc, z.targets : 2 * z.targets, :]
                result[u, pl.ds(cc, z.targets, stride=z.strings), :] = total
            return carry

        if z.share == 1:
            lax.fori_loop(0, n_tiles, one_tile, 0)
        else:
            part = part_ref[0]
            mine = (n_tiles - part + z.share - 1) // z.share
            lax.fori_loop(0, mine, lambda n, carry: one_tile(n * z.share + part, carry), 0)

    most = z.tiles // chunk_tiles
    lower = 0
    for depth in sorted({min(d, most) for d in (2, 3, 4, most)}):
        pl.when((count > lower) & (count <= depth * SPAN // z.block))(
            functools.partial(run, depth)
        )
        lower = depth * SPAN // z.block

    wide = z.src * z.strings
    lane_out = lax.broadcasted_iota(jnp.int32, (z.targets * z.strings, LANES), 1)
    for w in range(z.tiles):
        sides = []
        for at_side in range(2):
            rank = rank_ref[2 * w + at_side]
            spot = jnp.maximum(rank, 0)
            shift = ((spot + at_side) % 2) * half_block
            moved = pltpu.roll(result[spot // 2], shift, 1)
            here = rank >= 0
            if z.share > 1:
                here = here & ((spot // 2) % z.share == part_ref[0])
            sides.append(jnp.where(here, moved, 0.0))
        both = jnp.where(lane_out < half_block, sides[0], sides[1])
        for j in range(z.n_beta):
            device = w // z.halves * z.n_beta + j
            out_ref[device, w % z.halves] = both[j * wide : (j + 1) * wide]


def finish_kernel(z, irrep_ref, rx_ref, diag_ref, coef_ref, out_ref):
    wide = z.src * z.strings
    stride = z.share * z.halves * wide

    def column(first):
        rows = [
            rx_ref[pl.ds(part * z.halves * wide + first, z.sets, stride=stride), :]
            for part in range(z.share)
        ]
        return functools.reduce(jnp.add, rows)

    columns = []
    for t in range(z.src):
        for cc in range(z.strings):
            firsts = [h * wide + t * z.strings + cc for h in range(z.halves)]
            columns.append(jnp.concatenate([column(first) for first in firsts], axis=1))
    added = jnp.concatenate(columns, axis=0).T
    total = diag_ref[...] * coef_ref[...].astype(jnp.float32) + added
    for b in range(z.own):
        at = slice(b * z.block, (b + 1) * z.block)
        out_ref[at, :] = jnp.where(irrep_ref[b] == 0, total[at], 0.0)


def on_device(
    coefficients, diagonal, integrals, alpha_row, alpha_sign, beta_block, beta_sign, block_irrep
):
    z = Sizes(coefficients, integrals, alpha_row, beta_sign, block_irrep)
    f32, i32, bf16 = jnp.float32, jnp.int32, jnp.bfloat16
    alpha_rank = lax.axis_index("alpha")
    params = pltpu.CompilerParams(vmem_limit_bytes=56 * 1024 * 1024)

    first = jnp.minimum(alpha_rank, z.senders - 1) * z.per
    own_signs = lax.dynamic_slice_in_dim(beta_sign, first, z.per, 0)
    own_blocks = lax.dynamic_slice_in_dim(beta_block, first, z.per, 0)
    code = own_signs.reshape(z.per, z.pairs, z.block) * (own_blocks + 1)[:, :, None]
    packed = pl.pallas_call(
        functools.partial(pack_kernel, z),
        out_shape=jax.ShapeDtypeStruct((z.devices * z.pack, LANES), bf16),
        in_specs=[VMEM, VMEM],
        out_specs=VMEM,
        scratch_shapes=[pltpu.VMEM((z.devices * z.pack, LANES), f32)],
        compiler_params=params,
    )(coefficients, code.astype(f32))
    arrived = lax.all_to_all(
        packed.reshape(z.devices, z.pack, LANES), ("alpha", "beta"), 0, 0, tiled=True
    ).reshape(z.devices * z.pack, LANES)

    pad = z.pair_lanes - z.pairs
    wide = z.src * z.strings
    part = (alpha_rank * z.n_beta + lax.axis_index("beta")) % z.share
    integ = jnp.pad(integrals, ((0, pad), (0, pad)))
    terms = pl.pallas_call(
        functools.partial(main_kernel, z),
        out_shape=jax.ShapeDtypeStruct((z.devices, z.halves, wide, LANES), f32),
        in_specs=[SMEM, SMEM, VMEM, VMEM, VMEM, VMEM],
        out_specs=VMEM,
        scratch_shapes=[
            pltpu.VMEM((z.devices * z.pack, LANES), f32),
            pltpu.VMEM((z.tiles, z.lists, LANES), f32),
            pltpu.VMEM((z.tiles * LANES // SPAN * z.lists, SPAN), bf16),
            pltpu.VMEM((z.pair_tiles, z.lists, LANES), f32),
            pltpu.VMEM((z.pair_rows * z.targets, LANES), f32),
            pltpu.VMEM((z.chunks, LANES, DEPTH), bf16),
            pltpu.VMEM((z.tiles, z.pair_rows, LANES), f32),
            pltpu.VMEM((z.tiles, z.pair_rows, LANES), f32),
            pltpu.VMEM((z.tiles, z.pair_rows, LANES), f32),
            pltpu.VMEM((z.strings, 2 * z.targets, LANES), f32),
            pltpu.VMEM((DEPTH, z.strings * LANES), bf16),
            pltpu.VMEM((z.tiles, z.targets * z.strings, LANES), f32),
            pltpu.SMEM((z.blocks,), i32),
            pltpu.SMEM((z.blocks + 8,), i32),
        ],
        compiler_params=params,
    )(block_irrep, part.astype(i32)[None], arrived, integ, alpha_row, alpha_sign)

    back = lax.all_to_all(terms, ("alpha", "beta"), 0, 0, tiled=True).reshape(-1, LANES)
    own_irrep = lax.dynamic_slice_in_dim(block_irrep, alpha_rank * z.own, z.own, 0)
    return pl.pallas_call(
        functools.partial(finish_kernel, z),
        out_shape=jax.ShapeDtypeStruct((z.rows, z.cols), f32),
        in_specs=[SMEM, VMEM, VMEM, VMEM],
        out_specs=VMEM,
        compiler_params=params,
    )(own_irrep, back, diagonal, coefficients)


def solution(mesh):
    return jax.shard_map(
        on_device,
        mesh=mesh,
        in_specs=(
            P("alpha", "beta"),
            P("alpha", "beta"),
            P(),
            P(),
            P(),
            P("beta", None),
            P("beta", None),
            P(),
        ),
        out_specs=P("alpha", "beta"),
        check_vma=False,
    )
```

```python
import functools

import jax
import jax.numpy as jnp
from jax import lax
from jax.experimental import pallas as pl
from jax.experimental.pallas import tpu as pltpu
from jax.sharding import PartitionSpec as P

LANES = 128
DEPTH = 512
SPAN = 256
VMEM = pl.BlockSpec(memory_space=pltpu.VMEM)
SMEM = pl.BlockSpec(memory_space=pltpu.SMEM)


def round_up(size, step):
    return -(-size // step) * step


class Sizes:
    def __init__(self, coefficients, integrals, alpha_row, beta_sign, block_irrep):
        self.n_alpha = lax.axis_size("alpha")
        self.n_beta = lax.axis_size("beta")
        self.devices = self.n_alpha * self.n_beta
        self.rows, self.cols = coefficients.shape
        self.pairs = integrals.shape[0]
        self.block = beta_sign.shape[1] // self.pairs
        self.src = self.cols // self.block
        self.targets = self.n_beta * self.src
        self.all_rows = alpha_row.shape[1]
        self.blocks = block_irrep.shape[0]
        self.own = self.rows // self.block
        self.share = max(1, self.devices // self.block)
        self.sets = self.devices // self.share
        self.strings = self.block // self.sets
        self.halves = self.rows // LANES
        self.tiles = self.all_rows // LANES
        self.per = max(1, self.src // self.n_alpha)
        self.senders = self.src // self.per
        self.group = self.src * self.strings
        self.lists = self.n_beta * self.group
        self.chunk_pairs = DEPTH // self.targets
        self.pair_rows = round_up(self.pairs, self.chunk_pairs)
        self.chunks = self.pair_rows // self.chunk_pairs
        self.pair_lanes = round_up(self.pairs, LANES)
        self.pair_tiles = self.pair_lanes // LANES
        self.coef_rows = self.halves * self.group
        self.sign_rows = self.per * self.strings * self.pair_tiles
        self.pack = round_up(self.coef_rows + self.sign_rows, 8)


def pack_kernel(z, coef_ref, sign_ref, out_ref, scratch):
    scratch[...] = jnp.zeros_like(scratch)
    turned = coef_ref[...].astype(jnp.float32).T
    for half in range(z.halves):
        for g in range(z.group):
            row = half * z.group + g
            for part in range(z.share):
                scratch[pl.ds(row + part * z.pack, z.sets, stride=z.share * z.pack), :] = turned[
                    g * z.sets : (g + 1) * z.sets, half * LANES : (half + 1) * LANES
                ]
    for s in range(z.per):
        code = sign_ref[s].T
        code = jnp.concatenate(
            [code, jnp.zeros((z.block, z.pair_lanes - z.pairs), jnp.float32)], axis=1
        )
        for cc in range(z.strings):
            for k in range(z.pair_tiles):
                row = z.coef_rows + (s * z.strings + cc) * z.pair_tiles + k
                for part in range(z.share):
                    scratch[pl.ds(row + part * z.pack, z.sets, stride=z.share * z.pack), :] = code[
                        cc * z.sets : (cc + 1) * z.sets, k * LANES : (k + 1) * LANES
                    ]
    out_ref[...] = scratch[...].astype(jnp.bfloat16)


def live_blocks(z, irrep_ref, rank_ref, list_ref):
    count = jnp.int32(0)
    lane_row = lax.broadcasted_iota(jnp.int32, (1, LANES), 1)
    ranks = jnp.full((1, LANES), -1, jnp.int32)
    for g in range(z.blocks):
        live = irrep_ref[g] == 0
        rank = jnp.where(live, count, -1)
        rank_ref[g] = rank
        list_ref[count] = g
        ranks = jnp.where(lane_row == g, rank, ranks)
        count = count + live.astype(jnp.int32)
    for extra in range(4):
        list_ref[count + extra] = 0
    return count, ranks


def index_kernel(z, irrep_ref, row_ref, sign_ref, out_ref, rank_ref, list_ref):
    count, ranks = live_blocks(z, irrep_ref, rank_ref, list_ref)
    lane_pair = lax.broadcasted_iota(jnp.int32, (z.pairs, LANES), 1)
    tail = z.pairs // 8 * 8

    def compact_step(u, carry):
        first, second = list_ref[2 * u], list_ref[2 * u + 1]
        left_shift = (first % 2) * z.block
        right_shift = (1 - second % 2) * z.block

        def merged(ref):
            at_first = pl.ds(pl.multiple_of(first // 2 * LANES, LANES), LANES)
            at_second = pl.ds(pl.multiple_of(second // 2 * LANES, LANES), LANES)
            return jnp.where(
                lane_pair < z.block,
                pltpu.roll(ref[:, at_first], left_shift, 1),
                pltpu.roll(ref[:, at_second], right_shift, 1),
            )

        source = merged(row_ref)
        signs = merged(sign_ref)
        block = source // z.block
        rank = jnp.take_along_axis(
            jnp.broadcast_to(ranks, (z.pairs, LANES)), block, axis=1, mode="promise_in_bounds"
        )
        spot = rank * z.block + (source & (z.block - 1))
        inside = (lane_pair < z.block) | (2 * u + 1 < count)
        out_ref[u, tail : z.pair_rows, :] = jnp.zeros((z.pair_rows - tail, LANES), jnp.int32)
        out_ref[u, 0 : z.pairs, :] = jnp.where((rank >= 0) & inside, signs * (spot + 1), 0)
        return carry

    lax.fori_loop(0, (count + 1) // 2, compact_step, 0)


def main_kernel(
    z,
    irrep_ref,
    part_ref,
    rx_ref,
    integ_ref,
    spot_ref,
    out_ref,
    rxf,
    full,
    table,
    codes,
    tall,
    acc,
    held,
    result,
    rank_ref,
    list_ref,
):
    f32, bf16 = jnp.float32, jnp.bfloat16
    half_block = z.block
    count, _ = live_blocks(z, irrep_ref, rank_ref, list_ref)
    n_tiles = (count + 1) // 2

    rxf[...] = rx_ref[...].astype(f32)
    for i in range(z.n_alpha):
        base = i * z.n_beta * z.pack
        for half in range(z.halves):
            for s in range(z.src):
                for cc in range(z.strings):
                    source = base + half * z.group + s * z.strings + cc
                    dest = cc * z.targets + s
                    full[i * z.halves + half, pl.ds(dest, z.n_beta, stride=z.src), :] = rxf[
                        pl.ds(source, z.n_beta, stride=z.pack), :
                    ]
        for s in range(z.per if i < z.senders else 0):
            for cc in range(z.strings):
                for k in range(z.pair_tiles):
                    source = base + z.coef_rows + (s * z.strings + cc) * z.pair_tiles + k
                    dest = (i * z.per + s) * z.strings + cc
                    codes[k, pl.ds(dest, z.n_beta, stride=z.group), :] = rxf[
                        pl.ds(source, z.n_beta, stride=z.pack), :
                    ]

    step = 4
    target = (lax.broadcasted_iota(jnp.int32, (z.targets, z.pair_lanes), 0) + 1).astype(f32)

    def weight_step(n, carry):
        parts = []
        for m in range(step * z.strings):
            code = jnp.concatenate(
                [codes[k, pl.ds(n * step * z.strings + m, 1), :] for k in range(z.pair_tiles)],
                axis=1,
            )
            hit = jnp.where(code == target, 1.0, 0.0) - jnp.where(code == -target, 1.0, 0.0)
            parts.append(hit)
        hits = jnp.concatenate(parts, axis=0).astype(bf16)
        found = jnp.dot(hits, integ_ref[...], preferred_element_type=f32)
        high = found.astype(bf16).astype(f32)
        low = found - high
        for m in range(step):
            rows = []
            for cc in range(z.strings):
                at = (m * z.strings + cc) * z.targets
                rows += [high[at : at + z.targets], low[at : at + z.targets]]
            turned = jnp.concatenate(rows, axis=0).T
            tall[pl.ds(n * step + m, z.pair_rows, stride=z.targets), :] = turned[0 : z.pair_rows]
        return carry

    lax.fori_loop(0, z.targets // step, weight_step, 0)

    lane_list = lax.broadcasted_iota(jnp.int32, (z.lists, LANES), 1)
    chunk_tiles = SPAN // LANES

    def compact_step(u, carry):
        first, second = list_ref[2 * u], list_ref[2 * u + 1]
        left_shift = (first % 2) * half_block
        right_shift = (1 - second % 2) * half_block
        left = pltpu.roll(full[first // 2], left_shift, 1)
        right = pltpu.roll(full[second // 2], right_shift, 1)
        left = jnp.where(2 * u < count, left, 0.0)
        right = jnp.where(2 * u + 1 < count, right, 0.0)
        at_list = pl.ds(pl.multiple_of(u // chunk_tiles * z.lists, z.lists), z.lists)
        at_lane = pl.ds(pl.multiple_of(u % chunk_tiles * LANES, LANES), LANES)
        table[at_list, at_lane] = jnp.where(lane_list < half_block, left, right).astype(bf16)
        return carry

    lax.fori_loop(0, (n_tiles + chunk_tiles - 1) // chunk_tiles * chunk_tiles, compact_step, 0)

    local = lax.broadcasted_iota(jnp.int32, (SPAN, LANES), 0).astype(f32).astype(bf16)
    nothing = jnp.zeros((SPAN, LANES), bf16)
    side = 2 * z.targets

    def tall_row(few):
        return jnp.concatenate([few.astype(f32).astype(bf16)] * (SPAN // 16), axis=0)

    def run(depth):
        def one_tile(u, carry):
            acc[...] = jnp.zeros_like(acc)
            held[...] = jnp.zeros_like(held)

            def spread(n):
                at = pl.multiple_of(n * DEPTH, DEPTH)
                weights = tall[pl.ds(at, DEPTH), :].T.astype(bf16)
                total = jnp.dot(weights, held[...], preferred_element_type=f32)
                for cc in range(z.strings):
                    acc[cc] += total[
                        cc * side : (cc + 1) * side, cc * LANES : (cc + 1) * LANES
                    ]

            def one_chunk(n, inner):
                spread(jnp.maximum(n - 1, 0))
                picks, chunk = [], []
                for q in range(z.chunk_pairs):
                    at = pl.ds(n * z.chunk_pairs + q, 1)
                    code = jnp.broadcast_to(spot_ref[u, at, :], (16, LANES))
                    spot = jnp.abs(code) - 1
                    sign = jnp.clip(code, -1, 1)
                    hit = local == tall_row(spot & (SPAN - 1))
                    picks.append(jnp.where(hit, tall_row(sign), nothing))
                    chunk.append(lax.shift_right_arithmetic(spot[0:8], SPAN.bit_length() - 1))
                pick = jnp.concatenate(picks, axis=1)
                found = jnp.dot(
                    table[0 : depth * z.lists, :], pick, preferred_element_type=f32
                )
                for q in range(z.chunk_pairs):
                    lanes = slice(q * LANES, (q + 1) * LANES)
                    value = found[0 : z.lists, lanes]
                    for m in range(1, depth):
                        other = found[m * z.lists : (m + 1) * z.lists, lanes]
                        here = jnp.concatenate([chunk[q] == m] * (z.lists // 8), axis=0)
                        value = jnp.where(here, other, value)
                    value = value.astype(bf16)
                    for cc in range(z.strings):
                        held[
                            q * z.targets : (q + 1) * z.targets, cc * LANES : (cc + 1) * LANES
                        ] = value[cc * z.targets : (cc + 1) * z.targets]
                return inner

            lax.fori_loop(0, z.chunks, one_chunk, 0)
            spread(z.chunks - 1)
            for cc in range(z.strings):
                total = acc[cc, 0 : z.targets, :] + acc[cc, z.targets : 2 * z.targets, :]
                result[u, pl.ds(cc, z.targets, stride=z.strings), :] = total
            return carry

        if z.share == 1:
            lax.fori_loop(0, n_tiles, one_tile, 0)
        else:
            part = part_ref[0]
            mine = (n_tiles - part + z.share - 1) // z.share
            lax.fori_loop(0, mine, lambda n, carry: one_tile(n * z.share + part, carry), 0)

    most = z.tiles // chunk_tiles
    lower = 0
    for depth in sorted({min(d, most) for d in (2, 3, 4, most)}):
        pl.when((count > lower) & (count <= depth * SPAN // z.block))(
            functools.partial(run, depth)
        )
        lower = depth * SPAN // z.block

    wide = z.src * z.strings
    lane_out = lax.broadcasted_iota(jnp.int32, (z.targets * z.strings, LANES), 1)
    for w in range(z.tiles):
        sides = []
        for at_side in range(2):
            rank = rank_ref[2 * w + at_side]
            spot = jnp.maximum(rank, 0)
            shift = ((spot + at_side) % 2) * half_block
            moved = pltpu.roll(result[spot // 2], shift, 1)
            here = rank >= 0
            if z.share > 1:
                here = here & ((spot // 2) % z.share == part_ref[0])
            sides.append(jnp.where(here, moved, 0.0))
        both = jnp.where(lane_out < half_block, sides[0], sides[1])
        for j in range(z.n_beta):
            device = w // z.halves * z.n_beta + j
            out_ref[device, w % z.halves] = both[j * wide : (j + 1) * wide]


def finish_kernel(z, irrep_ref, rx_ref, diag_ref, coef_ref, out_ref):
    wide = z.src * z.strings
    stride = z.share * z.halves * wide

    def column(first):
        rows = [
            rx_ref[pl.ds(part * z.halves * wide + first, z.sets, stride=stride), :]
            for part in range(z.share)
        ]
        return functools.reduce(jnp.add, rows)

    columns = []
    for t in range(z.src):
        for cc in range(z.strings):
            firsts = [h * wide + t * z.strings + cc for h in range(z.halves)]
            columns.append(jnp.concatenate([column(first) for first in firsts], axis=1))
    added = jnp.concatenate(columns, axis=0).T
    total = diag_ref[...] * coef_ref[...].astype(jnp.float32) + added
    for b in range(z.own):
        at = slice(b * z.block, (b + 1) * z.block)
        out_ref[at, :] = jnp.where(irrep_ref[b] == 0, total[at], 0.0)


def on_device(
    coefficients, diagonal, integrals, alpha_row, alpha_sign, beta_block, beta_sign, block_irrep
):
    z = Sizes(coefficients, integrals, alpha_row, beta_sign, block_irrep)
    f32, i32, bf16 = jnp.float32, jnp.int32, jnp.bfloat16
    alpha_rank = lax.axis_index("alpha")
    params = pltpu.CompilerParams(vmem_limit_bytes=32 * 1024 * 1024)

    first = jnp.minimum(alpha_rank, z.senders - 1) * z.per
    own_signs = lax.dynamic_slice_in_dim(beta_sign, first, z.per, 0)
    own_blocks = lax.dynamic_slice_in_dim(beta_block, first, z.per, 0)
    code = own_signs.reshape(z.per, z.pairs, z.block) * (own_blocks + 1)[:, :, None]
    packed = pl.pallas_call(
        functools.partial(pack_kernel, z),
        out_shape=jax.ShapeDtypeStruct((z.devices * z.pack, LANES), bf16),
        in_specs=[VMEM, VMEM],
        out_specs=VMEM,
        scratch_shapes=[pltpu.VMEM((z.devices * z.pack, LANES), f32)],
        compiler_params=params,
    )(coefficients, code.astype(f32))
    arrived = lax.all_to_all(
        packed.reshape(z.devices, z.pack, LANES), ("alpha", "beta"), 0, 0, tiled=True
    ).reshape(z.devices * z.pack, LANES)

    pad = z.pair_lanes - z.pairs
    wide = z.src * z.strings
    part = (alpha_rank * z.n_beta + lax.axis_index("beta")) % z.share
    integ = jnp.pad(integrals, ((0, pad), (0, pad)))
    lists = [pltpu.SMEM((z.blocks,), i32), pltpu.SMEM((z.blocks + 8,), i32)]
    spots = pl.pallas_call(
        functools.partial(index_kernel, z),
        out_shape=jax.ShapeDtypeStruct((z.tiles, z.pair_rows, LANES), i32),
        in_specs=[SMEM, VMEM, VMEM],
        out_specs=VMEM,
        scratch_shapes=lists,
        compiler_params=pltpu.CompilerParams(vmem_limit_bytes=16 * 1024 * 1024),
        cost_estimate=pl.CostEstimate(
            flops=50 * z.pairs * z.all_rows,
            bytes_accessed=12 * z.pairs * z.all_rows,
            transcendentals=0,
        ),
    )(block_irrep, alpha_row, alpha_sign)
    terms = pl.pallas_call(
        functools.partial(main_kernel, z),
        out_shape=jax.ShapeDtypeStruct((z.devices, z.halves, wide, LANES), f32),
        in_specs=[SMEM, SMEM, VMEM, VMEM, VMEM],
        out_specs=VMEM,
        scratch_shapes=[
            pltpu.VMEM((z.devices * z.pack, LANES), f32),
            pltpu.VMEM((z.tiles, z.lists, LANES), f32),
            pltpu.VMEM((z.tiles * LANES // SPAN * z.lists, SPAN), bf16),
            pltpu.VMEM((z.pair_tiles, z.lists, LANES), f32),
            pltpu.VMEM((z.pair_rows * z.targets, LANES), f32),
            pltpu.VMEM((z.strings, 2 * z.targets, LANES), f32),
            pltpu.VMEM((DEPTH, z.strings * LANES), bf16),
            pltpu.VMEM((z.tiles, z.targets * z.strings, LANES), f32),
        ]
        + lists,
        compiler_params=params,
    )(block_irrep, part.astype(i32)[None], arrived, integ, spots)

    back = lax.all_to_all(terms, ("alpha", "beta"), 0, 0, tiled=True).reshape(-1, LANES)
    own_irrep = lax.dynamic_slice_in_dim(block_irrep, alpha_rank * z.own, z.own, 0)
    return pl.pallas_call(
        functools.partial(finish_kernel, z),
        out_shape=jax.ShapeDtypeStruct((z.rows, z.cols), f32),
        in_specs=[SMEM, VMEM, VMEM, VMEM],
        out_specs=VMEM,
        compiler_params=params,
    )(own_irrep, back, diagonal, coefficients)


def solution(mesh):
    return jax.shard_map(
        on_device,
        mesh=mesh,
        in_specs=(
            P("alpha", "beta"),
            P("alpha", "beta"),
            P(),
            P(),
            P(),
            P("beta", None),
            P("beta", None),
            P(),
        ),
        out_specs=P("alpha", "beta"),
        check_vma=False,
    )
```

```python
import functools

import jax
import jax.numpy as jnp
from jax import lax
from jax.experimental import pallas as pl
from jax.experimental.pallas import tpu as pltpu
from jax.sharding import PartitionSpec as P

LANES = 128
DEPTH = 256
SPAN = 256
VMEM = pl.BlockSpec(memory_space=pltpu.VMEM)
SMEM = pl.BlockSpec(memory_space=pltpu.SMEM)


def round_up(size, step):
    return -(-size // step) * step


class Sizes:
    def __init__(self, coefficients, integrals, alpha_row, beta_sign, block_irrep):
        self.n_alpha = lax.axis_size("alpha")
        self.n_beta = lax.axis_size("beta")
        self.devices = self.n_alpha * self.n_beta
        self.rows, self.cols = coefficients.shape
        self.pairs = integrals.shape[0]
        self.block = beta_sign.shape[1] // self.pairs
        self.src = self.cols // self.block
        self.targets = self.n_beta * self.src
        self.all_rows = alpha_row.shape[1]
        self.blocks = block_irrep.shape[0]
        self.own = self.rows // self.block
        self.share = max(1, self.devices // self.block)
        self.sets = self.devices // self.share
        self.strings = self.block // self.sets
        self.halves = self.rows // LANES
        self.tiles = self.all_rows // LANES
        self.per = max(1, self.src // self.n_alpha)
        self.senders = self.src // self.per
        self.group = self.src * self.strings
        self.lists = self.n_beta * self.group
        self.chunk_pairs = DEPTH // self.targets
        self.pair_rows = round_up(self.pairs, 2 * self.chunk_pairs)
        self.chunks = self.pair_rows // self.chunk_pairs
        self.pair_lanes = round_up(self.pairs, LANES)
        self.pair_tiles = self.pair_lanes // LANES
        self.coef_rows = self.halves * self.group
        self.sign_rows = self.per * self.strings * self.pair_tiles
        self.pack = round_up(self.coef_rows + self.sign_rows, 8)


def pack_kernel(z, first_ref, coef_ref, sign_ref, block_ref, out_ref, scratch):
    scratch[...] = jnp.zeros_like(scratch)
    turned = coef_ref[...].astype(jnp.float32).T
    for half in range(z.halves):
        for g in range(z.group):
            row = half * z.group + g
            for part in range(z.share):
                scratch[pl.ds(row + part * z.pack, z.sets, stride=z.share * z.pack), :] = turned[
                    g * z.sets : (g + 1) * z.sets, half * LANES : (half + 1) * LANES
                ]
    for s in range(z.per):
        number = block_ref[pl.ds(first_ref[0] + s, 1), :] + 1
        code = sign_ref[s].astype(jnp.float32).T * number.astype(jnp.float32)
        code = jnp.concatenate(
            [code, jnp.zeros((z.block, z.pair_lanes - z.pairs), jnp.float32)], axis=1
        )
        for cc in range(z.strings):
            for k in range(z.pair_tiles):
                row = z.coef_rows + (s * z.strings + cc) * z.pair_tiles + k
                for part in range(z.share):
                    scratch[pl.ds(row + part * z.pack, z.sets, stride=z.share * z.pack), :] = code[
                        cc * z.sets : (cc + 1) * z.sets, k * LANES : (k + 1) * LANES
                    ]
    out_ref[...] = scratch[...].astype(jnp.bfloat16)


def live_blocks(z, irrep_ref, rank_ref, list_ref):
    count = jnp.int32(0)
    lane_row = lax.broadcasted_iota(jnp.int32, (1, LANES), 1)
    ranks = jnp.full((1, LANES), -1, jnp.int32)
    for g in range(z.blocks):
        live = irrep_ref[g] == 0
        rank = jnp.where(live, count, -1)
        rank_ref[g] = rank
        list_ref[count] = g
        ranks = jnp.where(lane_row == g, rank, ranks)
        count = count + live.astype(jnp.int32)
    for extra in range(4):
        list_ref[count + extra] = 0
    return count, ranks


def index_kernel(z, irrep_ref, row_ref, sign_ref, out_ref, rank_ref, list_ref):
    count, ranks = live_blocks(z, irrep_ref, rank_ref, list_ref)
    lane_pair = lax.broadcasted_iota(jnp.int32, (z.pairs, LANES), 1)
    tail = z.pairs // 8 * 8

    def compact_step(u, carry):
        first, second = list_ref[2 * u], list_ref[2 * u + 1]
        left_shift = (first % 2) * z.block
        right_shift = (1 - second % 2) * z.block

        def merged(ref):
            at_first = pl.ds(pl.multiple_of(first // 2 * LANES, LANES), LANES)
            at_second = pl.ds(pl.multiple_of(second // 2 * LANES, LANES), LANES)
            return jnp.where(
                lane_pair < z.block,
                pltpu.roll(ref[:, at_first], left_shift, 1),
                pltpu.roll(ref[:, at_second], right_shift, 1),
            )

        source = merged(row_ref)
        signs = merged(sign_ref)
        block = source // z.block
        rank = jnp.take_along_axis(
            jnp.broadcast_to(ranks, (z.pairs, LANES)), block, axis=1, mode="promise_in_bounds"
        )
        spot = rank * z.block + (source & (z.block - 1))
        inside = (lane_pair < z.block) | (2 * u + 1 < count)
        out_ref[u, tail : z.pair_rows, :] = jnp.zeros((z.pair_rows - tail, LANES), jnp.int32)
        out_ref[u, 0 : z.pairs, :] = jnp.where((rank >= 0) & inside, signs * (spot + 1), 0)
        return carry

    lax.fori_loop(0, (count + 1) // 2, compact_step, 0)


def main_kernel(
    z,
    irrep_ref,
    part_ref,
    rx_ref,
    integ_ref,
    spot_ref,
    out_ref,
    rxf,
    full,
    table,
    codes,
    tall,
    acc,
    pick_a,
    pick_b,
    held_a,
    held_b,
    result,
    rank_ref,
    list_ref,
):
    f32, bf16 = jnp.float32, jnp.bfloat16
    half_block = z.block
    count, _ = live_blocks(z, irrep_ref, rank_ref, list_ref)
    n_tiles = (count + 1) // 2

    rxf[...] = rx_ref[...].astype(f32)
    for i in range(z.n_alpha):
        base = i * z.n_beta * z.pack
        for half in range(z.halves):
            for s in range(z.src):
                for cc in range(z.strings):
                    source = base + half * z.group + s * z.strings + cc
                    dest = cc * z.targets + s
                    full[i * z.halves + half, pl.ds(dest, z.n_beta, stride=z.src), :] = rxf[
                        pl.ds(source, z.n_beta, stride=z.pack), :
                    ]
        for s in range(z.per if i < z.senders else 0):
            for cc in range(z.strings):
                for k in range(z.pair_tiles):
                    source = base + z.coef_rows + (s * z.strings + cc) * z.pair_tiles + k
                    dest = (i * z.per + s) * z.strings + cc
                    codes[k, pl.ds(dest, z.n_beta, stride=z.group), :] = rxf[
                        pl.ds(source, z.n_beta, stride=z.pack), :
                    ]

    step = 4
    target = (lax.broadcasted_iota(jnp.int32, (z.targets, z.pair_lanes), 0) + 1).astype(f32)

    def weight_step(n, carry):
        parts = []
        for m in range(step * z.strings):
            code = jnp.concatenate(
                [codes[k, pl.ds(n * step * z.strings + m, 1), :] for k in range(z.pair_tiles)],
                axis=1,
            )
            hit = jnp.where(code == target, 1.0, 0.0) - jnp.where(code == -target, 1.0, 0.0)
            parts.append(hit)
        hits = jnp.concatenate(parts, axis=0).astype(bf16)
        found = jnp.dot(hits, integ_ref[...], preferred_element_type=f32)
        high = found.astype(bf16).astype(f32)
        low = found - high
        for m in range(step):
            rows = []
            for cc in range(z.strings):
                at = (m * z.strings + cc) * z.targets
                rows += [high[at : at + z.targets], low[at : at + z.targets]]
            turned = jnp.concatenate(rows, axis=0).T
            tall[pl.ds(n * step + m, z.pair_rows, stride=z.targets), :] = turned[0 : z.pair_rows]
        return carry

    lax.fori_loop(0, z.targets // step, weight_step, 0)

    lane_list = lax.broadcasted_iota(jnp.int32, (z.lists, LANES), 1)
    chunk_tiles = SPAN // LANES

    def compact_step(u, carry):
        first, second = list_ref[2 * u], list_ref[2 * u + 1]
        left_shift = (first % 2) * half_block
        right_shift = (1 - second % 2) * half_block
        left = pltpu.roll(full[first // 2], left_shift, 1)
        right = pltpu.roll(full[second // 2], right_shift, 1)
        left = jnp.where(2 * u < count, left, 0.0)
        right = jnp.where(2 * u + 1 < count, right, 0.0)
        at_list = pl.ds(pl.multiple_of(u // chunk_tiles * z.lists, z.lists), z.lists)
        at_lane = pl.ds(pl.multiple_of(u % chunk_tiles * LANES, LANES), LANES)
        table[at_list, at_lane] = jnp.where(lane_list < half_block, left, right).astype(bf16)
        return carry

    lax.fori_loop(0, (n_tiles + chunk_tiles - 1) // chunk_tiles * chunk_tiles, compact_step, 0)

    local = lax.broadcasted_iota(jnp.int32, (SPAN, LANES), 0).astype(f32).astype(bf16)
    nothing = jnp.zeros((SPAN, LANES), bf16)
    side = 2 * z.targets

    def tall_row(few):
        return jnp.concatenate([few.astype(f32).astype(bf16)] * (SPAN // 16), axis=0)

    def run(depth):
        def one_tile(u, carry):
            acc[...] = jnp.zeros_like(acc)
            held_b[...] = jnp.zeros_like(held_b)

            def code_row(n, q, rows):
                at = pl.ds(n * z.chunk_pairs + q, 1)
                return jnp.broadcast_to(spot_ref[u, at, :], (rows, LANES))

            def build(n, pick_ref):
                for q in range(z.chunk_pairs):
                    code = code_row(n, q, 16)
                    hit = local == tall_row((jnp.abs(code) - 1) & (SPAN - 1))
                    pick_ref[:, q * LANES : (q + 1) * LANES] = jnp.where(
                        hit, tall_row(jnp.clip(code, -1, 1)), nothing
                    )

            def spread(n, held_ref):
                at = pl.multiple_of(n * DEPTH, DEPTH)
                weights = tall[pl.ds(at, DEPTH), :].T.astype(bf16)
                total = jnp.dot(weights, held_ref[...], preferred_element_type=f32)
                for cc in range(z.strings):
                    acc[cc] += total[
                        cc * side : (cc + 1) * side, cc * LANES : (cc + 1) * LANES
                    ]

            def choose(n, found, held_ref):
                for q in range(z.chunk_pairs):
                    lanes = slice(q * LANES, (q + 1) * LANES)
                    spot = jnp.abs(code_row(n, q, 8)) - 1
                    chunk = lax.shift_right_arithmetic(spot, SPAN.bit_length() - 1)
                    value = found[0 : z.lists, lanes]
                    for m in range(1, depth):
                        other = found[m * z.lists : (m + 1) * z.lists, lanes]
                        here = jnp.concatenate([chunk == m] * (z.lists // 8), axis=0)
                        value = jnp.where(here, other, value)
                    value = value.astype(bf16)
                    for cc in range(z.strings):
                        held_ref[
                            q * z.targets : (q + 1) * z.targets, cc * LANES : (cc + 1) * LANES
                        ] = value[cc * z.targets : (cc + 1) * z.targets]

            def stage(n, pick_ref, next_ref, held_ref, before_ref):
                found = jnp.dot(
                    table[0 : depth * z.lists, :], pick_ref[...], preferred_element_type=f32
                )
                build(jnp.minimum(n + 1, z.chunks - 1), next_ref)
                spread(jnp.maximum(n - 1, 0), before_ref)
                choose(n, found, held_ref)

            def two_chunks(n, inner):
                stage(2 * n, pick_a, pick_b, held_a, held_b)
                stage(2 * n + 1, pick_b, pick_a, held_b, held_a)
                return inner

            build(0, pick_a)
            lax.fori_loop(0, z.chunks // 2, two_chunks, 0)
            spread(z.chunks - 1, held_b)
            for cc in range(z.strings):
                total = acc[cc, 0 : z.targets, :] + acc[cc, z.targets : 2 * z.targets, :]
                result[u, pl.ds(cc, z.targets, stride=z.strings), :] = total
            return carry

        if z.share == 1:
            lax.fori_loop(0, n_tiles, one_tile, 0)
        else:
            part = part_ref[0]
            mine = (n_tiles - part + z.share - 1) // z.share
            lax.fori_loop(0, mine, lambda n, carry: one_tile(n * z.share + part, carry), 0)

    most = z.tiles // chunk_tiles
    lower = 0
    for depth in sorted({min(d, most) for d in (2, 3, 4, most)}):
        pl.when((count > lower) & (count <= depth * SPAN // z.block))(
            functools.partial(run, depth)
        )
        lower = depth * SPAN // z.block

    wide = z.src * z.strings
    lane_out = lax.broadcasted_iota(jnp.int32, (z.targets * z.strings, LANES), 1)
    for w in range(z.tiles):
        sides = []
        for at_side in range(2):
            rank = rank_ref[2 * w + at_side]
            spot = jnp.maximum(rank, 0)
            shift = ((spot + at_side) % 2) * half_block
            moved = pltpu.roll(result[spot // 2], shift, 1)
            here = rank >= 0
            if z.share > 1:
                here = here & ((spot // 2) % z.share == part_ref[0])
            sides.append(jnp.where(here, moved, 0.0))
        both = jnp.where(lane_out < half_block, sides[0], sides[1])
        for j in range(z.n_beta):
            device = w // z.halves * z.n_beta + j
            out_ref[device, w % z.halves] = both[j * wide : (j + 1) * wide]


def finish_kernel(z, irrep_ref, rx_ref, diag_ref, coef_ref, out_ref):
    wide = z.src * z.strings
    stride = z.share * z.halves * wide

    def column(first):
        rows = [
            rx_ref[pl.ds(part * z.halves * wide + first, z.sets, stride=stride), :]
            for part in range(z.share)
        ]
        return functools.reduce(jnp.add, rows)

    columns = []
    for t in range(z.src):
        for cc in range(z.strings):
            firsts = [h * wide + t * z.strings + cc for h in range(z.halves)]
            columns.append(jnp.concatenate([column(first) for first in firsts], axis=1))
    added = jnp.concatenate(columns, axis=0).T
    total = diag_ref[...] * coef_ref[...].astype(jnp.float32) + added
    for b in range(z.own):
        at = slice(b * z.block, (b + 1) * z.block)
        out_ref[at, :] = jnp.where(irrep_ref[b] == 0, total[at], 0.0)


def on_device(
    coefficients, diagonal, integrals, alpha_row, alpha_sign, beta_block, beta_sign, block_irrep
):
    z = Sizes(coefficients, integrals, alpha_row, beta_sign, block_irrep)
    f32, i32, bf16 = jnp.float32, jnp.int32, jnp.bfloat16
    alpha_rank = lax.axis_index("alpha")
    params = pltpu.CompilerParams(vmem_limit_bytes=32 * 1024 * 1024)

    first = jnp.minimum(alpha_rank, z.senders - 1) * z.per
    own_signs = lax.dynamic_slice_in_dim(beta_sign, first, z.per, 0)
    packed = pl.pallas_call(
        functools.partial(pack_kernel, z),
        out_shape=jax.ShapeDtypeStruct((z.devices * z.pack, LANES), bf16),
        in_specs=[SMEM, VMEM, VMEM, VMEM],
        out_specs=VMEM,
        scratch_shapes=[pltpu.VMEM((z.devices * z.pack, LANES), f32)],
        compiler_params=params,
    )(
        first.astype(i32)[None],
        coefficients,
        own_signs.reshape(z.per, z.pairs, z.block),
        beta_block,
    )
    arrived = lax.all_to_all(
        packed.reshape(z.devices, z.pack, LANES), ("alpha", "beta"), 0, 0, tiled=True
    ).reshape(z.devices * z.pack, LANES)

    pad = z.pair_lanes - z.pairs
    wide = z.src * z.strings
    part = (alpha_rank * z.n_beta + lax.axis_index("beta")) % z.share
    integ = jnp.pad(integrals, ((0, pad), (0, pad)))
    lists = [pltpu.SMEM((z.blocks,), i32), pltpu.SMEM((z.blocks + 8,), i32)]
    spots = pl.pallas_call(
        functools.partial(index_kernel, z),
        out_shape=jax.ShapeDtypeStruct((z.tiles, z.pair_rows, LANES), i32),
        in_specs=[SMEM, VMEM, VMEM],
        out_specs=VMEM,
        scratch_shapes=lists,
        compiler_params=pltpu.CompilerParams(vmem_limit_bytes=16 * 1024 * 1024),
        cost_estimate=pl.CostEstimate(
            flops=50 * z.pairs * z.all_rows,
            bytes_accessed=12 * z.pairs * z.all_rows,
            transcendentals=0,
        ),
    )(block_irrep, alpha_row, alpha_sign)
    terms = pl.pallas_call(
        functools.partial(main_kernel, z),
        out_shape=jax.ShapeDtypeStruct((z.devices, z.halves, wide, LANES), f32),
        in_specs=[SMEM, SMEM, VMEM, VMEM, VMEM],
        out_specs=VMEM,
        scratch_shapes=[
            pltpu.VMEM((z.devices * z.pack, LANES), f32),
            pltpu.VMEM((z.tiles, z.lists, LANES), f32),
            pltpu.VMEM((z.tiles * LANES // SPAN * z.lists, SPAN), bf16),
            pltpu.VMEM((z.pair_tiles, z.lists, LANES), f32),
            pltpu.VMEM((z.pair_rows * z.targets, LANES), f32),
            pltpu.VMEM((z.strings, 2 * z.targets, LANES), f32),
            pltpu.VMEM((SPAN, z.chunk_pairs * LANES), bf16),
            pltpu.VMEM((SPAN, z.chunk_pairs * LANES), bf16),
            pltpu.VMEM((DEPTH, z.strings * LANES), bf16),
            pltpu.VMEM((DEPTH, z.strings * LANES), bf16),
            pltpu.VMEM((z.tiles, z.targets * z.strings, LANES), f32),
        ]
        + lists,
        compiler_params=params,
    )(block_irrep, part.astype(i32)[None], arrived, integ, spots)

    back = lax.all_to_all(terms, ("alpha", "beta"), 0, 0, tiled=True).reshape(-1, LANES)
    own_irrep = lax.dynamic_slice_in_dim(block_irrep, alpha_rank * z.own, z.own, 0)
    return pl.pallas_call(
        functools.partial(finish_kernel, z),
        out_shape=jax.ShapeDtypeStruct((z.rows, z.cols), f32),
        in_specs=[SMEM, VMEM, VMEM, VMEM],
        out_specs=VMEM,
        compiler_params=params,
    )(own_irrep, back, diagonal, coefficients)


def solution(mesh):
    return jax.shard_map(
        on_device,
        mesh=mesh,
        in_specs=(
            P("alpha", "beta"),
            P("alpha", "beta"),
            P(),
            P(),
            P(),
            P("beta", None),
            P("beta", None),
            P(),
        ),
        out_specs=P("alpha", "beta"),
        check_vma=False,
    )
```

```python
import functools

import jax
import jax.numpy as jnp
from jax import lax
from jax.experimental import pallas as pl
from jax.experimental.pallas import tpu as pltpu
from jax.sharding import PartitionSpec as P

LANES = 128
DEPTH = 512
SPAN = 256
VMEM = pl.BlockSpec(memory_space=pltpu.VMEM)
SMEM = pl.BlockSpec(memory_space=pltpu.SMEM)


def round_up(size, step):
    return -(-size // step) * step


class Sizes:
    def __init__(self, coefficients, integrals, alpha_row, beta_sign, block_irrep):
        self.n_alpha = lax.axis_size("alpha")
        self.n_beta = lax.axis_size("beta")
        self.devices = self.n_alpha * self.n_beta
        self.rows, self.cols = coefficients.shape
        self.pairs = integrals.shape[0]
        self.block = beta_sign.shape[1] // self.pairs
        self.src = self.cols // self.block
        self.targets = self.n_beta * self.src
        self.all_rows = alpha_row.shape[1]
        self.blocks = block_irrep.shape[0]
        self.own = self.rows // self.block
        self.share = max(1, self.devices // self.block)
        self.sets = self.devices // self.share
        self.strings = self.block // self.sets
        self.halves = self.rows // LANES
        self.tiles = self.all_rows // LANES
        self.per = max(1, self.src // self.n_alpha)
        self.senders = self.src // self.per
        self.group = self.src * self.strings
        self.lists = self.n_beta * self.group
        self.chunk_pairs = DEPTH // self.targets
        self.pair_rows = round_up(self.pairs, self.chunk_pairs)
        self.chunks = self.pair_rows // self.chunk_pairs
        self.pair_lanes = round_up(self.pairs, LANES)
        self.pair_tiles = self.pair_lanes // LANES
        self.coef_rows = self.halves * self.group
        self.sign_rows = self.per * self.strings * self.pair_tiles
        self.pack = round_up(self.coef_rows + self.sign_rows, 8)


def pack_kernel(z, coef_ref, sign_ref, out_ref, scratch):
    scratch[...] = jnp.zeros_like(scratch)
    turned = coef_ref[...].astype(jnp.float32).T
    for half in range(z.halves):
        for g in range(z.group):
            row = half * z.group + g
            for part in range(z.share):
                scratch[pl.ds(row + part * z.pack, z.sets, stride=z.share * z.pack), :] = turned[
                    g * z.sets : (g + 1) * z.sets, half * LANES : (half + 1) * LANES
                ]
    for s in range(z.per):
        code = sign_ref[s].T
        code = jnp.concatenate(
            [code, jnp.zeros((z.block, z.pair_lanes - z.pairs), jnp.float32)], axis=1
        )
        for cc in range(z.strings):
            for k in range(z.pair_tiles):
                row = z.coef_rows + (s * z.strings + cc) * z.pair_tiles + k
                for part in range(z.share):
                    scratch[pl.ds(row + part * z.pack, z.sets, stride=z.share * z.pack), :] = code[
                        cc * z.sets : (cc + 1) * z.sets, k * LANES : (k + 1) * LANES
                    ]
    out_ref[...] = scratch[...].astype(jnp.bfloat16)


def live_blocks(z, irrep_ref, rank_ref, list_ref):
    count = jnp.int32(0)
    lane_row = lax.broadcasted_iota(jnp.int32, (1, LANES), 1)
    ranks = jnp.full((1, LANES), -1, jnp.int32)
    for g in range(z.blocks):
        live = irrep_ref[g] == 0
        rank = jnp.where(live, count, -1)
        rank_ref[g] = rank
        list_ref[count] = g
        ranks = jnp.where(lane_row == g, rank, ranks)
        count = count + live.astype(jnp.int32)
    for extra in range(4):
        list_ref[count + extra] = 0
    return count, ranks


def index_kernel(z, irrep_ref, row_ref, sign_ref, out_ref, rank_ref, list_ref):
    count, ranks = live_blocks(z, irrep_ref, rank_ref, list_ref)
    lane_pair = lax.broadcasted_iota(jnp.int32, (z.pairs, LANES), 1)
    tail = z.pairs // 8 * 8

    def compact_step(u, carry):
        first, second = list_ref[2 * u], list_ref[2 * u + 1]
        left_shift = (first % 2) * z.block
        right_shift = (1 - second % 2) * z.block

        def merged(ref):
            at_first = pl.ds(pl.multiple_of(first // 2 * LANES, LANES), LANES)
            at_second = pl.ds(pl.multiple_of(second // 2 * LANES, LANES), LANES)
            return jnp.where(
                lane_pair < z.block,
                pltpu.roll(ref[:, at_first], left_shift, 1),
                pltpu.roll(ref[:, at_second], right_shift, 1),
            )

        source = merged(row_ref)
        signs = merged(sign_ref)
        block = source // z.block
        rank = jnp.take_along_axis(
            jnp.broadcast_to(ranks, (z.pairs, LANES)), block, axis=1, mode="promise_in_bounds"
        )
        spot = rank * z.block + (source & (z.block - 1))
        inside = (lane_pair < z.block) | (2 * u + 1 < count)
        out_ref[u, tail : z.pair_rows, :] = jnp.zeros((z.pair_rows - tail, LANES), jnp.int32)
        out_ref[u, 0 : z.pairs, :] = jnp.where((rank >= 0) & inside, signs * (spot + 1), 0)
        return carry

    lax.fori_loop(0, (count + 1) // 2, compact_step, 0)


def main_kernel(
    z,
    irrep_ref,
    part_ref,
    rx_ref,
    integ_ref,
    spot_ref,
    out_ref,
    rxf,
    full,
    table,
    codes,
    tall,
    acc,
    held,
    result,
    rank_ref,
    list_ref,
):
    f32, bf16 = jnp.float32, jnp.bfloat16
    half_block = z.block
    count, _ = live_blocks(z, irrep_ref, rank_ref, list_ref)
    n_tiles = (count + 1) // 2

    rxf[...] = rx_ref[...].astype(f32)
    for i in range(z.n_alpha):
        base = i * z.n_beta * z.pack
        for half in range(z.halves):
            for s in range(z.src):
                for cc in range(z.strings):
                    source = base + half * z.group + s * z.strings + cc
                    dest = cc * z.targets + s
                    full[i * z.halves + half, pl.ds(dest, z.n_beta, stride=z.src), :] = rxf[
                        pl.ds(source, z.n_beta, stride=z.pack), :
                    ]
        for s in range(z.per if i < z.senders else 0):
            for cc in range(z.strings):
                for k in range(z.pair_tiles):
                    source = base + z.coef_rows + (s * z.strings + cc) * z.pair_tiles + k
                    dest = (i * z.per + s) * z.strings + cc
                    codes[k, pl.ds(dest, z.n_beta, stride=z.group), :] = rxf[
                        pl.ds(source, z.n_beta, stride=z.pack), :
                    ]

    step = 4
    target = (lax.broadcasted_iota(jnp.int32, (z.targets, z.pair_lanes), 0) + 1).astype(f32)

    def weight_step(n, carry):
        parts = []
        for m in range(step * z.strings):
            code = jnp.concatenate(
                [codes[k, pl.ds(n * step * z.strings + m, 1), :] for k in range(z.pair_tiles)],
                axis=1,
            )
            hit = jnp.where(code == target, 1.0, 0.0) - jnp.where(code == -target, 1.0, 0.0)
            parts.append(hit)
        hits = jnp.concatenate(parts, axis=0).astype(bf16)
        found = jnp.dot(hits, integ_ref[...], preferred_element_type=f32)
        high = found.astype(bf16).astype(f32)
        low = found - high
        for m in range(step):
            rows = []
            for cc in range(z.strings):
                at = (m * z.strings + cc) * z.targets
                rows += [high[at : at + z.targets], low[at : at + z.targets]]
            turned = jnp.concatenate(rows, axis=0).T
            tall[pl.ds(n * step + m, z.pair_rows, stride=z.targets), :] = turned[0 : z.pair_rows]
        return carry

    lax.fori_loop(0, z.targets // step, weight_step, 0)

    lane_list = lax.broadcasted_iota(jnp.int32, (z.lists, LANES), 1)
    chunk_tiles = SPAN // LANES

    def compact_step(u, carry):
        first, second = list_ref[2 * u], list_ref[2 * u + 1]
        left_shift = (first % 2) * half_block
        right_shift = (1 - second % 2) * half_block
        left = pltpu.roll(full[first // 2], left_shift, 1)
        right = pltpu.roll(full[second // 2], right_shift, 1)
        left = jnp.where(2 * u < count, left, 0.0)
        right = jnp.where(2 * u + 1 < count, right, 0.0)
        at_list = pl.ds(pl.multiple_of(u // chunk_tiles * z.lists, z.lists), z.lists)
        at_lane = pl.ds(pl.multiple_of(u % chunk_tiles * LANES, LANES), LANES)
        table[at_list, at_lane] = jnp.where(lane_list < half_block, left, right).astype(bf16)
        return carry

    lax.fori_loop(0, (n_tiles + chunk_tiles - 1) // chunk_tiles * chunk_tiles, compact_step, 0)

    local = lax.broadcasted_iota(jnp.int32, (SPAN, LANES), 0).astype(f32).astype(bf16)
    nothing = jnp.zeros((SPAN, LANES), bf16)
    side = 2 * z.targets

    def tall_row(few):
        return jnp.concatenate([few.astype(f32).astype(bf16)] * (SPAN // 16), axis=0)

    def run(depth):
        def one_tile(u, carry):
            acc[...] = jnp.zeros_like(acc)
            held[...] = jnp.zeros_like(held)

            def spread(n):
                at = pl.multiple_of(n * DEPTH, DEPTH)
                weights = tall[pl.ds(at, DEPTH), :].T.astype(bf16)
                total = jnp.dot(weights, held[...], preferred_element_type=f32)
                for cc in range(z.strings):
                    acc[cc] += total[
                        cc * side : (cc + 1) * side, cc * LANES : (cc + 1) * LANES
                    ]

            def one_chunk(n, inner):
                spread(jnp.maximum(n - 1, 0))
                for start in range(0, z.chunk_pairs, 4):
                    picks, chunk = [], []
                    for q in range(start, start + 4):
                        at = pl.ds(n * z.chunk_pairs + q, 1)
                        code = jnp.broadcast_to(spot_ref[u, at, :], (16, LANES))
                        spot = jnp.abs(code) - 1
                        sign = jnp.clip(code, -1, 1)
                        hit = local == tall_row(spot & (SPAN - 1))
                        picks.append(jnp.where(hit, tall_row(sign), nothing))
                        chunk.append(lax.shift_right_arithmetic(spot[0:8], SPAN.bit_length() - 1))
                    pick = jnp.concatenate(picks, axis=1)
                    found = jnp.dot(
                        table[0 : depth * z.lists, :], pick, preferred_element_type=f32
                    )
                    for k in range(4):
                        lanes = slice(k * LANES, (k + 1) * LANES)
                        value = found[0 : z.lists, lanes]
                        for m in range(1, depth):
                            other = found[m * z.lists : (m + 1) * z.lists, lanes]
                            here = jnp.concatenate([chunk[k] == m] * (z.lists // 8), axis=0)
                            value = jnp.where(here, other, value)
                        value = value.astype(bf16)
                        row = (start + k) * z.targets
                        for cc in range(z.strings):
                            held[row : row + z.targets, cc * LANES : (cc + 1) * LANES] = value[
                                cc * z.targets : (cc + 1) * z.targets
                            ]
                return inner

            lax.fori_loop(0, z.chunks, one_chunk, 0)
            spread(z.chunks - 1)
            for cc in range(z.strings):
                total = acc[cc, 0 : z.targets, :] + acc[cc, z.targets : 2 * z.targets, :]
                result[u, pl.ds(cc, z.targets, stride=z.strings), :] = total
            return carry

        if z.share == 1:
            lax.fori_loop(0, n_tiles, one_tile, 0)
        else:
            part = part_ref[0]
            mine = (n_tiles - part + z.share - 1) // z.share
            lax.fori_loop(0, mine, lambda n, carry: one_tile(n * z.share + part, carry), 0)

    most = z.tiles // chunk_tiles
    lower = 0
    for depth in sorted({min(d, most) for d in (2, 3, 4, most)}):
        pl.when((count > lower) & (count <= depth * SPAN // z.block))(
            functools.partial(run, depth)
        )
        lower = depth * SPAN // z.block

    wide = z.src * z.strings
    lane_out = lax.broadcasted_iota(jnp.int32, (z.targets * z.strings, LANES), 1)
    for w in range(z.tiles):
        sides = []
        for at_side in range(2):
            rank = rank_ref[2 * w + at_side]
            spot = jnp.maximum(rank, 0)
            shift = ((spot + at_side) % 2) * half_block
            moved = pltpu.roll(result[spot // 2], shift, 1)
            here = rank >= 0
            if z.share > 1:
                here = here & ((spot // 2) % z.share == part_ref[0])
            sides.append(jnp.where(here, moved, 0.0))
        both = jnp.where(lane_out < half_block, sides[0], sides[1])
        for j in range(z.n_beta):
            device = w // z.halves * z.n_beta + j
            out_ref[device, w % z.halves] = both[j * wide : (j + 1) * wide]


def finish_kernel(z, irrep_ref, rx_ref, diag_ref, coef_ref, out_ref):
    wide = z.src * z.strings
    stride = z.share * z.halves * wide

    def column(first):
        rows = [
            rx_ref[pl.ds(part * z.halves * wide + first, z.sets, stride=stride), :]
            for part in range(z.share)
        ]
        return functools.reduce(jnp.add, rows)

    columns = []
    for t in range(z.src):
        for cc in range(z.strings):
            firsts = [h * wide + t * z.strings + cc for h in range(z.halves)]
            columns.append(jnp.concatenate([column(first) for first in firsts], axis=1))
    added = jnp.concatenate(columns, axis=0).T
    total = diag_ref[...] * coef_ref[...].astype(jnp.float32) + added
    for b in range(z.own):
        at = slice(b * z.block, (b + 1) * z.block)
        out_ref[at, :] = jnp.where(irrep_ref[b] == 0, total[at], 0.0)


def on_device(
    coefficients, diagonal, integrals, alpha_row, alpha_sign, beta_block, beta_sign, block_irrep
):
    z = Sizes(coefficients, integrals, alpha_row, beta_sign, block_irrep)
    f32, i32, bf16 = jnp.float32, jnp.int32, jnp.bfloat16
    alpha_rank = lax.axis_index("alpha")
    params = pltpu.CompilerParams(vmem_limit_bytes=32 * 1024 * 1024)

    first = jnp.minimum(alpha_rank, z.senders - 1) * z.per
    own_signs = lax.dynamic_slice_in_dim(beta_sign, first, z.per, 0)
    own_blocks = lax.dynamic_slice_in_dim(beta_block, first, z.per, 0)
    code = own_signs.reshape(z.per, z.pairs, z.block) * (own_blocks + 1)[:, :, None]
    packed = pl.pallas_call(
        functools.partial(pack_kernel, z),
        out_shape=jax.ShapeDtypeStruct((z.devices * z.pack, LANES), bf16),
        in_specs=[VMEM, VMEM],
        out_specs=VMEM,
        scratch_shapes=[pltpu.VMEM((z.devices * z.pack, LANES), f32)],
        compiler_params=params,
    )(coefficients, code.astype(f32))
    arrived = lax.all_to_all(
        packed.reshape(z.devices, z.pack, LANES), ("alpha", "beta"), 0, 0, tiled=True
    ).reshape(z.devices * z.pack, LANES)

    pad = z.pair_lanes - z.pairs
    wide = z.src * z.strings
    part = (alpha_rank * z.n_beta + lax.axis_index("beta")) % z.share
    integ = jnp.pad(integrals, ((0, pad), (0, pad)))
    lists = [pltpu.SMEM((z.blocks,), i32), pltpu.SMEM((z.blocks + 8,), i32)]
    spots = pl.pallas_call(
        functools.partial(index_kernel, z),
        out_shape=jax.ShapeDtypeStruct((z.tiles, z.pair_rows, LANES), i32),
        in_specs=[SMEM, VMEM, VMEM],
        out_specs=VMEM,
        scratch_shapes=lists,
        compiler_params=pltpu.CompilerParams(vmem_limit_bytes=16 * 1024 * 1024),
        cost_estimate=pl.CostEstimate(
            flops=50 * z.pairs * z.all_rows,
            bytes_accessed=12 * z.pairs * z.all_rows,
            transcendentals=0,
        ),
    )(block_irrep, alpha_row, alpha_sign)
    terms = pl.pallas_call(
        functools.partial(main_kernel, z),
        out_shape=jax.ShapeDtypeStruct((z.devices, z.halves, wide, LANES), f32),
        in_specs=[SMEM, SMEM, VMEM, VMEM, VMEM],
        out_specs=VMEM,
        scratch_shapes=[
            pltpu.VMEM((z.devices * z.pack, LANES), f32),
            pltpu.VMEM((z.tiles, z.lists, LANES), f32),
            pltpu.VMEM((z.tiles * LANES // SPAN * z.lists, SPAN), bf16),
            pltpu.VMEM((z.pair_tiles, z.lists, LANES), f32),
            pltpu.VMEM((z.pair_rows * z.targets, LANES), f32),
            pltpu.VMEM((z.strings, 2 * z.targets, LANES), f32),
            pltpu.VMEM((DEPTH, z.strings * LANES), bf16),
            pltpu.VMEM((z.tiles, z.targets * z.strings, LANES), f32),
        ]
        + lists,
        compiler_params=params,
    )(block_irrep, part.astype(i32)[None], arrived, integ, spots)

    back = lax.all_to_all(terms, ("alpha", "beta"), 0, 0, tiled=True).reshape(-1, LANES)
    own_irrep = lax.dynamic_slice_in_dim(block_irrep, alpha_rank * z.own, z.own, 0)
    return pl.pallas_call(
        functools.partial(finish_kernel, z),
        out_shape=jax.ShapeDtypeStruct((z.rows, z.cols), f32),
        in_specs=[SMEM, VMEM, VMEM, VMEM],
        out_specs=VMEM,
        compiler_params=params,
    )(own_irrep, back, diagonal, coefficients)


def solution(mesh):
    return jax.shard_map(
        on_device,
        mesh=mesh,
        in_specs=(
            P("alpha", "beta"),
            P("alpha", "beta"),
            P(),
            P(),
            P(),
            P("beta", None),
            P("beta", None),
            P(),
        ),
        out_specs=P("alpha", "beta"),
        check_vma=False,
    )
```

```python
import functools

import jax
import jax.numpy as jnp
from jax import lax
from jax.experimental import pallas as pl
from jax.experimental.pallas import tpu as pltpu
from jax.sharding import PartitionSpec as P

LANES = 128
DEPTH = 512
SPAN = 256
GATHERED = 4
VMEM = pl.BlockSpec(memory_space=pltpu.VMEM)
SMEM = pl.BlockSpec(memory_space=pltpu.SMEM)


def round_up(size, step):
    return -(-size // step) * step


class Sizes:
    def __init__(self, coefficients, integrals, alpha_row, beta_sign, block_irrep):
        self.n_alpha = lax.axis_size("alpha")
        self.n_beta = lax.axis_size("beta")
        self.devices = self.n_alpha * self.n_beta
        self.rows, self.cols = coefficients.shape
        self.pairs = integrals.shape[0]
        self.block = beta_sign.shape[1] // self.pairs
        self.src = self.cols // self.block
        self.targets = self.n_beta * self.src
        self.all_rows = alpha_row.shape[1]
        self.blocks = block_irrep.shape[0]
        self.own = self.rows // self.block
        self.share = max(1, self.devices // self.block)
        self.sets = self.devices // self.share
        self.strings = self.block // self.sets
        self.halves = self.rows // LANES
        self.tiles = self.all_rows // LANES
        self.per = max(1, self.src // self.n_alpha)
        self.senders = self.src // self.per
        self.group = self.src * self.strings
        self.lists = self.n_beta * self.group
        self.chunk_pairs = DEPTH // self.targets
        self.pair_rows = round_up(self.pairs, self.chunk_pairs)
        self.chunks = self.pair_rows // self.chunk_pairs
        self.pair_lanes = round_up(self.pairs, LANES)
        self.pair_tiles = self.pair_lanes // LANES
        self.coef_rows = self.halves * self.group
        self.sign_rows = self.per * self.strings * self.pair_tiles
        self.pack = round_up(self.coef_rows + self.sign_rows, 8)


def pack_kernel(z, coef_ref, sign_ref, out_ref, scratch):
    scratch[...] = jnp.zeros_like(scratch)
    turned = coef_ref[...].astype(jnp.float32).T
    for half in range(z.halves):
        for g in range(z.group):
            row = half * z.group + g
            for part in range(z.share):
                scratch[pl.ds(row + part * z.pack, z.sets, stride=z.share * z.pack), :] = turned[
                    g * z.sets : (g + 1) * z.sets, half * LANES : (half + 1) * LANES
                ]
    for s in range(z.per):
        code = sign_ref[s].T
        code = jnp.concatenate(
            [code, jnp.zeros((z.block, z.pair_lanes - z.pairs), jnp.float32)], axis=1
        )
        for cc in range(z.strings):
            for k in range(z.pair_tiles):
                row = z.coef_rows + (s * z.strings + cc) * z.pair_tiles + k
                for part in range(z.share):
                    scratch[pl.ds(row + part * z.pack, z.sets, stride=z.share * z.pack), :] = code[
                        cc * z.sets : (cc + 1) * z.sets, k * LANES : (k + 1) * LANES
                    ]
    out_ref[...] = scratch[...].astype(jnp.bfloat16)


def live_blocks(z, irrep_ref, rank_ref, list_ref):
    count = jnp.int32(0)
    lane_row = lax.broadcasted_iota(jnp.int32, (1, LANES), 1)
    ranks = jnp.full((1, LANES), -1, jnp.int32)
    for g in range(z.blocks):
        live = irrep_ref[g] == 0
        rank = jnp.where(live, count, -1)
        rank_ref[g] = rank
        list_ref[count] = g
        ranks = jnp.where(lane_row == g, rank, ranks)
        count = count + live.astype(jnp.int32)
    for extra in range(4):
        list_ref[count + extra] = 0
    return count, ranks


def index_kernel(z, irrep_ref, row_ref, sign_ref, out_ref, rank_ref, list_ref):
    count, ranks = live_blocks(z, irrep_ref, rank_ref, list_ref)
    lane_pair = lax.broadcasted_iota(jnp.int32, (z.pairs, LANES), 1)
    tail = z.pairs // 8 * 8

    def compact_step(u, carry):
        first, second = list_ref[2 * u], list_ref[2 * u + 1]
        left_shift = (first % 2) * z.block
        right_shift = (1 - second % 2) * z.block

        def merged(ref):
            at_first = pl.ds(pl.multiple_of(first // 2 * LANES, LANES), LANES)
            at_second = pl.ds(pl.multiple_of(second // 2 * LANES, LANES), LANES)
            return jnp.where(
                lane_pair < z.block,
                pltpu.roll(ref[:, at_first], left_shift, 1),
                pltpu.roll(ref[:, at_second], right_shift, 1),
            )

        source = merged(row_ref)
        signs = merged(sign_ref)
        block = source // z.block
        rank = jnp.take_along_axis(
            jnp.broadcast_to(ranks, (z.pairs, LANES)), block, axis=1, mode="promise_in_bounds"
        )
        spot = rank * z.block + (source & (z.block - 1))
        inside = (lane_pair < z.block) | (2 * u + 1 < count)
        out_ref[u, tail : z.pair_rows, :] = jnp.zeros((z.pair_rows - tail, LANES), jnp.int32)
        out_ref[u, 0 : z.pairs, :] = jnp.where((rank >= 0) & inside, signs * (spot + 1), 0)
        return carry

    lax.fori_loop(0, (count + 1) // 2, compact_step, 0)


def main_kernel(
    z,
    irrep_ref,
    part_ref,
    rx_ref,
    integ_ref,
    spot_ref,
    out_ref,
    rxf,
    full,
    tabf,
    table,
    codes,
    tall,
    acc,
    held,
    result,
    rank_ref,
    list_ref,
):
    f32, bf16 = jnp.float32, jnp.bfloat16
    half_block = z.block
    count, _ = live_blocks(z, irrep_ref, rank_ref, list_ref)
    n_tiles = (count + 1) // 2

    rxf[...] = rx_ref[...].astype(f32)
    for i in range(z.n_alpha):
        base = i * z.n_beta * z.pack
        for half in range(z.halves):
            for s in range(z.src):
                for cc in range(z.strings):
                    source = base + half * z.group + s * z.strings + cc
                    dest = cc * z.targets + s
                    full[i * z.halves + half, pl.ds(dest, z.n_beta, stride=z.src), :] = rxf[
                        pl.ds(source, z.n_beta, stride=z.pack), :
                    ]
        for s in range(z.per if i < z.senders else 0):
            for cc in range(z.strings):
                for k in range(z.pair_tiles):
                    source = base + z.coef_rows + (s * z.strings + cc) * z.pair_tiles + k
                    dest = (i * z.per + s) * z.strings + cc
                    codes[k, pl.ds(dest, z.n_beta, stride=z.group), :] = rxf[
                        pl.ds(source, z.n_beta, stride=z.pack), :
                    ]

    step = 4
    target = (lax.broadcasted_iota(jnp.int32, (z.targets, z.pair_lanes), 0) + 1).astype(f32)

    def weight_step(n, carry):
        parts = []
        for m in range(step * z.strings):
            code = jnp.concatenate(
                [codes[k, pl.ds(n * step * z.strings + m, 1), :] for k in range(z.pair_tiles)],
                axis=1,
            )
            hit = jnp.where(code == target, 1.0, 0.0) - jnp.where(code == -target, 1.0, 0.0)
            parts.append(hit)
        hits = jnp.concatenate(parts, axis=0).astype(bf16)
        found = jnp.dot(hits, integ_ref[...], preferred_element_type=f32)
        high = found.astype(bf16).astype(f32)
        low = found - high
        for m in range(step):
            rows = []
            for cc in range(z.strings):
                at = (m * z.strings + cc) * z.targets
                rows += [high[at : at + z.targets], low[at : at + z.targets]]
            turned = jnp.concatenate(rows, axis=0).T
            tall[pl.ds(n * step + m, z.pair_rows, stride=z.targets), :] = turned[0 : z.pair_rows]
        return carry

    lax.fori_loop(0, z.targets // step, weight_step, 0, unroll=2)

    lane_list = lax.broadcasted_iota(jnp.int32, (z.lists, LANES), 1)
    chunk_tiles = SPAN // LANES

    def compact_step(u, carry):
        first, second = list_ref[2 * u], list_ref[2 * u + 1]
        left_shift = (first % 2) * half_block
        right_shift = (1 - second % 2) * half_block
        left = pltpu.roll(full[first // 2], left_shift, 1)
        right = pltpu.roll(full[second // 2], right_shift, 1)
        left = jnp.where(2 * u < count, left, 0.0)
        right = jnp.where(2 * u + 1 < count, right, 0.0)
        at_list = pl.ds(pl.multiple_of(u // chunk_tiles * z.lists, z.lists), z.lists)
        at_lane = pl.ds(pl.multiple_of(u % chunk_tiles * LANES, LANES), LANES)
        both = jnp.where(lane_list < half_block, left, right)
        tabf[u] = both
        table[at_list, at_lane] = both.astype(bf16)
        return carry

    lax.fori_loop(0, (n_tiles + chunk_tiles - 1) // chunk_tiles * chunk_tiles, compact_step, 0)

    local = lax.broadcasted_iota(jnp.int32, (SPAN, LANES), 0).astype(f32).astype(bf16)
    nothing = jnp.zeros((SPAN, LANES), bf16)
    side = 2 * z.targets

    def tall_row(few):
        return jnp.concatenate([few.astype(f32).astype(bf16)] * (SPAN // 16), axis=0)

    def run(tiles):
        depth = (tiles * LANES + SPAN - 1) // SPAN

        def one_tile(u, carry):
            acc[...] = jnp.zeros_like(acc)
            held[...] = jnp.zeros_like(held)

            def spread(n):
                at = pl.multiple_of(n * DEPTH, DEPTH)
                weights = tall[pl.ds(at, DEPTH), :].T.astype(bf16)
                total = jnp.dot(weights, held[...], preferred_element_type=f32)
                for cc in range(z.strings):
                    acc[cc] += total[
                        cc * side : (cc + 1) * side, cc * LANES : (cc + 1) * LANES
                    ]

            def keep(q, value):
                value = value.astype(bf16)
                for cc in range(z.strings):
                    held[q * z.targets : (q + 1) * z.targets, cc * LANES : (cc + 1) * LANES] = (
                        value[cc * z.targets : (cc + 1) * z.targets]
                    )

            def gather(q, spot, sign):
                lanes = spot & (LANES - 1)
                tile = lax.shift_right_arithmetic(spot, LANES.bit_length() - 1)
                hits = [tile == k for k in range(tiles)]
                parts = []
                for row in range(0, z.lists, 8):
                    value = jnp.zeros((8, LANES), f32)
                    for k in range(tiles):
                        taken = jnp.take_along_axis(
                            tabf[k, row : row + 8, :], lanes, axis=1, mode="promise_in_bounds"
                        )
                        value = jnp.where(hits[k], taken, value)
                    parts.append(value * sign)
                keep(q, jnp.concatenate(parts, axis=0))

            def one_chunk(n, inner):
                spread(jnp.maximum(n - 1, 0))
                picks, chunk, chosen = [], [], []
                for q in range(z.chunk_pairs):
                    at = pl.ds(n * z.chunk_pairs + q, 1)
                    code = jnp.broadcast_to(spot_ref[u, at, :], (16, LANES))
                    spot = jnp.abs(code) - 1
                    sign = jnp.clip(code, -1, 1)
                    if q % GATHERED == GATHERED - 1:
                        gather(q, spot[0:8], sign[0:8].astype(f32))
                        continue
                    chosen.append(q)
                    hit = local == tall_row(spot & (SPAN - 1))
                    picks.append(jnp.where(hit, tall_row(sign), nothing))
                    chunk.append(lax.shift_right_arithmetic(spot[0:8], SPAN.bit_length() - 1))
                pick = jnp.concatenate(picks, axis=1)
                found = jnp.dot(
                    table[0 : depth * z.lists, :], pick, preferred_element_type=f32
                )
                for k, q in enumerate(chosen):
                    lanes = slice(k * LANES, (k + 1) * LANES)
                    value = found[0 : z.lists, lanes]
                    for m in range(1, depth):
                        other = found[m * z.lists : (m + 1) * z.lists, lanes]
                        here = jnp.concatenate([chunk[k] == m] * (z.lists // 8), axis=0)
                        value = jnp.where(here, other, value)
                    keep(q, value)
                return inner

            lax.fori_loop(0, z.chunks, one_chunk, 0)
            spread(z.chunks - 1)
            for cc in range(z.strings):
                total = acc[cc, 0 : z.targets, :] + acc[cc, z.targets : 2 * z.targets, :]
                result[u, pl.ds(cc, z.targets, stride=z.strings), :] = total
            return carry

        if z.share == 1:
            lax.fori_loop(0, n_tiles, one_tile, 0)
        else:
            part = part_ref[0]
            mine = (n_tiles - part + z.share - 1) // z.share
            lax.fori_loop(0, mine, lambda n, carry: one_tile(n * z.share + part, carry), 0)

    lower = 0
    for tiles in sorted({min(tiles, z.tiles) for tiles in (4, 5, 6, 8, z.tiles)}):
        pl.when((n_tiles > lower) & (n_tiles <= tiles))(functools.partial(run, tiles))
        lower = tiles

    wide = z.src * z.strings
    lane_out = lax.broadcasted_iota(jnp.int32, (z.targets * z.strings, LANES), 1)
    for w in range(z.tiles):
        sides = []
        for at_side in range(2):
            rank = rank_ref[2 * w + at_side]
            spot = jnp.maximum(rank, 0)
            shift = ((spot + at_side) % 2) * half_block
            moved = pltpu.roll(result[spot // 2], shift, 1)
            here = rank >= 0
            if z.share > 1:
                here = here & ((spot // 2) % z.share == part_ref[0])
            sides.append(jnp.where(here, moved, 0.0))
        both = jnp.where(lane_out < half_block, sides[0], sides[1])
        for j in range(z.n_beta):
            device = w // z.halves * z.n_beta + j
            out_ref[device, w % z.halves] = both[j * wide : (j + 1) * wide]


def finish_kernel(z, irrep_ref, rx_ref, diag_ref, coef_ref, out_ref):
    wide = z.src * z.strings
    stride = z.share * z.halves * wide

    def column(first):
        rows = [
            rx_ref[pl.ds(part * z.halves * wide + first, z.sets, stride=stride), :]
            for part in range(z.share)
        ]
        return functools.reduce(jnp.add, rows)

    columns = []
    for t in range(z.src):
        for cc in range(z.strings):
            firsts = [h * wide + t * z.strings + cc for h in range(z.halves)]
            columns.append(jnp.concatenate([column(first) for first in firsts], axis=1))
    added = jnp.concatenate(columns, axis=0).T
    total = diag_ref[...] * coef_ref[...].astype(jnp.float32) + added
    for b in range(z.own):
        at = slice(b * z.block, (b + 1) * z.block)
        out_ref[at, :] = jnp.where(irrep_ref[b] == 0, total[at], 0.0)


def on_device(
    coefficients, diagonal, integrals, alpha_row, alpha_sign, beta_block, beta_sign, block_irrep
):
    z = Sizes(coefficients, integrals, alpha_row, beta_sign, block_irrep)
    f32, i32, bf16 = jnp.float32, jnp.int32, jnp.bfloat16
    alpha_rank = lax.axis_index("alpha")
    params = pltpu.CompilerParams(vmem_limit_bytes=32 * 1024 * 1024)

    first = jnp.minimum(alpha_rank, z.senders - 1) * z.per
    own_signs = lax.dynamic_slice_in_dim(beta_sign, first, z.per, 0)
    own_blocks = lax.dynamic_slice_in_dim(beta_block, first, z.per, 0)
    code = own_signs.reshape(z.per, z.pairs, z.block) * (own_blocks + 1)[:, :, None]
    packed = pl.pallas_call(
        functools.partial(pack_kernel, z),
        out_shape=jax.ShapeDtypeStruct((z.devices * z.pack, LANES), bf16),
        in_specs=[VMEM, VMEM],
        out_specs=VMEM,
        scratch_shapes=[pltpu.VMEM((z.devices * z.pack, LANES), f32)],
        compiler_params=params,
    )(coefficients, code.astype(f32))
    arrived = lax.all_to_all(
        packed.reshape(z.devices, z.pack, LANES), ("alpha", "beta"), 0, 0, tiled=True
    ).reshape(z.devices * z.pack, LANES)

    pad = z.pair_lanes - z.pairs
    wide = z.src * z.strings
    part = (alpha_rank * z.n_beta + lax.axis_index("beta")) % z.share
    integ = jnp.pad(integrals, ((0, pad), (0, pad)))
    lists = [pltpu.SMEM((z.blocks,), i32), pltpu.SMEM((z.blocks + 8,), i32)]
    spots = pl.pallas_call(
        functools.partial(index_kernel, z),
        out_shape=jax.ShapeDtypeStruct((z.tiles, z.pair_rows, LANES), i32),
        in_specs=[SMEM, VMEM, VMEM],
        out_specs=VMEM,
        scratch_shapes=lists,
        compiler_params=pltpu.CompilerParams(vmem_limit_bytes=16 * 1024 * 1024),
        cost_estimate=pl.CostEstimate(
            flops=50 * z.pairs * z.all_rows,
            bytes_accessed=12 * z.pairs * z.all_rows,
            transcendentals=0,
        ),
    )(block_irrep, alpha_row, alpha_sign)
    terms = pl.pallas_call(
        functools.partial(main_kernel, z),
        out_shape=jax.ShapeDtypeStruct((z.devices, z.halves, wide, LANES), f32),
        in_specs=[SMEM, SMEM, VMEM, VMEM, VMEM],
        out_specs=VMEM,
        scratch_shapes=[
            pltpu.VMEM((z.devices * z.pack, LANES), f32),
            pltpu.VMEM((z.tiles, z.lists, LANES), f32),
            pltpu.VMEM((z.tiles, z.lists, LANES), f32),
            pltpu.VMEM((z.tiles * LANES // SPAN * z.lists, SPAN), bf16),
            pltpu.VMEM((z.pair_tiles, z.lists, LANES), f32),
            pltpu.VMEM((z.pair_rows * z.targets, LANES), f32),
            pltpu.VMEM((z.strings, 2 * z.targets, LANES), f32),
            pltpu.VMEM((DEPTH, z.strings * LANES), bf16),
            pltpu.VMEM((z.tiles, z.targets * z.strings, LANES), f32),
        ]
        + lists,
        compiler_params=params,
    )(block_irrep, part.astype(i32)[None], arrived, integ, spots)

    back = lax.all_to_all(terms, ("alpha", "beta"), 0, 0, tiled=True).reshape(-1, LANES)
    own_irrep = lax.dynamic_slice_in_dim(block_irrep, alpha_rank * z.own, z.own, 0)
    return pl.pallas_call(
        functools.partial(finish_kernel, z),
        out_shape=jax.ShapeDtypeStruct((z.rows, z.cols), f32),
        in_specs=[SMEM, VMEM, VMEM, VMEM],
        out_specs=VMEM,
        compiler_params=params,
    )(own_irrep, back, diagonal, coefficients)


def solution(mesh):
    return jax.shard_map(
        on_device,
        mesh=mesh,
        in_specs=(
            P("alpha", "beta"),
            P("alpha", "beta"),
            P(),
            P(),
            P(),
            P("beta", None),
            P("beta", None),
            P(),
        ),
        out_specs=P("alpha", "beta"),
        check_vma=False,
    )
```

```python
import functools

import jax
import jax.numpy as jnp
from jax import lax
from jax.experimental import pallas as pl
from jax.experimental.pallas import tpu as pltpu
from jax.sharding import PartitionSpec as P

LANES = 128
DEPTH = 512
SPAN = 256
GATHERED = 4
VMEM = pl.BlockSpec(memory_space=pltpu.VMEM)
SMEM = pl.BlockSpec(memory_space=pltpu.SMEM)


def round_up(size, step):
    return -(-size // step) * step


class Sizes:
    def __init__(self, coefficients, integrals, alpha_row, beta_sign, block_irrep):
        self.n_alpha = lax.axis_size("alpha")
        self.n_beta = lax.axis_size("beta")
        self.devices = self.n_alpha * self.n_beta
        self.rows, self.cols = coefficients.shape
        self.pairs = integrals.shape[0]
        self.block = beta_sign.shape[1] // self.pairs
        self.src = self.cols // self.block
        self.targets = self.n_beta * self.src
        self.all_rows = alpha_row.shape[1]
        self.blocks = block_irrep.shape[0]
        self.own = self.rows // self.block
        self.share = max(1, self.devices // self.block)
        self.sets = self.devices // self.share
        self.strings = self.block // self.sets
        self.halves = self.rows // LANES
        self.tiles = self.all_rows // LANES
        self.per = max(1, self.src // self.n_alpha)
        self.senders = self.src // self.per
        self.group = self.src * self.strings
        self.lists = self.n_beta * self.group
        self.chunk_pairs = DEPTH // self.targets
        self.pair_rows = round_up(self.pairs, self.chunk_pairs)
        self.chunks = self.pair_rows // self.chunk_pairs
        self.pair_lanes = round_up(self.pairs, LANES)
        self.pair_tiles = self.pair_lanes // LANES
        self.coef_rows = self.halves * self.group
        self.sign_rows = self.per * self.strings * self.pair_tiles
        self.pack = round_up(self.coef_rows + self.sign_rows, 8)


def pack_kernel(z, coef_ref, sign_ref, out_ref, scratch):
    scratch[...] = jnp.zeros_like(scratch)
    turned = coef_ref[...].astype(jnp.float32).T
    for half in range(z.halves):
        for g in range(z.group):
            row = half * z.group + g
            for part in range(z.share):
                scratch[pl.ds(row + part * z.pack, z.sets, stride=z.share * z.pack), :] = turned[
                    g * z.sets : (g + 1) * z.sets, half * LANES : (half + 1) * LANES
                ]
    for s in range(z.per):
        code = sign_ref[s].T
        code = jnp.concatenate(
            [code, jnp.zeros((z.block, z.pair_lanes - z.pairs), jnp.float32)], axis=1
        )
        for cc in range(z.strings):
            for k in range(z.pair_tiles):
                row = z.coef_rows + (s * z.strings + cc) * z.pair_tiles + k
                for part in range(z.share):
                    scratch[pl.ds(row + part * z.pack, z.sets, stride=z.share * z.pack), :] = code[
                        cc * z.sets : (cc + 1) * z.sets, k * LANES : (k + 1) * LANES
                    ]
    out_ref[...] = scratch[...].astype(jnp.bfloat16)


def live_blocks(z, irrep_ref, rank_ref, list_ref):
    count = jnp.int32(0)
    lane_row = lax.broadcasted_iota(jnp.int32, (1, LANES), 1)
    ranks = jnp.full((1, LANES), -1, jnp.int32)
    for g in range(z.blocks):
        live = irrep_ref[g] == 0
        rank = jnp.where(live, count, -1)
        rank_ref[g] = rank
        list_ref[count] = g
        ranks = jnp.where(lane_row == g, rank, ranks)
        count = count + live.astype(jnp.int32)
    for extra in range(4):
        list_ref[count + extra] = 0
    return count, ranks


def index_kernel(z, irrep_ref, row_ref, sign_ref, out_ref, rank_ref, list_ref):
    count, ranks = live_blocks(z, irrep_ref, rank_ref, list_ref)
    lane_pair = lax.broadcasted_iota(jnp.int32, (z.pairs, LANES), 1)
    tail = z.pairs // 8 * 8

    def compact_step(u, carry):
        first, second = list_ref[2 * u], list_ref[2 * u + 1]
        left_shift = (first % 2) * z.block
        right_shift = (1 - second % 2) * z.block

        def merged(ref):
            at_first = pl.ds(pl.multiple_of(first // 2 * LANES, LANES), LANES)
            at_second = pl.ds(pl.multiple_of(second // 2 * LANES, LANES), LANES)
            return jnp.where(
                lane_pair < z.block,
                pltpu.roll(ref[:, at_first], left_shift, 1),
                pltpu.roll(ref[:, at_second], right_shift, 1),
            )

        source = merged(row_ref)
        signs = merged(sign_ref)
        block = source // z.block
        rank = jnp.take_along_axis(
            jnp.broadcast_to(ranks, (z.pairs, LANES)), block, axis=1, mode="promise_in_bounds"
        )
        spot = rank * z.block + (source & (z.block - 1))
        inside = (lane_pair < z.block) | (2 * u + 1 < count)
        out_ref[u, tail : z.pair_rows, :] = jnp.zeros((z.pair_rows - tail, LANES), jnp.int32)
        out_ref[u, 0 : z.pairs, :] = jnp.where((rank >= 0) & inside, signs * (spot + 1), 0)
        return carry

    lax.fori_loop(0, (count + 1) // 2, compact_step, 0)


def main_kernel(
    z,
    irrep_ref,
    part_ref,
    rx_ref,
    integ_ref,
    spot_ref,
    out_ref,
    rxf,
    full,
    tabf,
    table,
    codes,
    tall,
    weights,
    acc,
    held,
    result,
    rank_ref,
    list_ref,
):
    f32, bf16 = jnp.float32, jnp.bfloat16
    half_block = z.block
    count, _ = live_blocks(z, irrep_ref, rank_ref, list_ref)
    n_tiles = (count + 1) // 2

    rxf[...] = rx_ref[...].astype(f32)
    for i in range(z.n_alpha):
        base = i * z.n_beta * z.pack
        for half in range(z.halves):
            for s in range(z.src):
                for cc in range(z.strings):
                    source = base + half * z.group + s * z.strings + cc
                    dest = cc * z.targets + s
                    full[i * z.halves + half, pl.ds(dest, z.n_beta, stride=z.src), :] = rxf[
                        pl.ds(source, z.n_beta, stride=z.pack), :
                    ]
        for s in range(z.per if i < z.senders else 0):
            for cc in range(z.strings):
                for k in range(z.pair_tiles):
                    source = base + z.coef_rows + (s * z.strings + cc) * z.pair_tiles + k
                    dest = (i * z.per + s) * z.strings + cc
                    codes[k, pl.ds(dest, z.n_beta, stride=z.group), :] = rxf[
                        pl.ds(source, z.n_beta, stride=z.pack), :
                    ]

    step = 4
    target = (lax.broadcasted_iota(jnp.int32, (z.targets, z.pair_lanes), 0) + 1).astype(f32)

    def weight_step(n, carry):
        parts = []
        for m in range(step * z.strings):
            code = jnp.concatenate(
                [codes[k, pl.ds(n * step * z.strings + m, 1), :] for k in range(z.pair_tiles)],
                axis=1,
            )
            hit = jnp.where(code == target, 1.0, 0.0) - jnp.where(code == -target, 1.0, 0.0)
            parts.append(hit)
        hits = jnp.concatenate(parts, axis=0).astype(bf16)
        found = jnp.dot(hits, integ_ref[...], preferred_element_type=f32)
        high = found.astype(bf16).astype(f32)
        low = found - high
        for m in range(step):
            rows = []
            for cc in range(z.strings):
                at = (m * z.strings + cc) * z.targets
                rows += [high[at : at + z.targets], low[at : at + z.targets]]
            turned = jnp.concatenate(rows, axis=0).T
            tall[pl.ds(n * step + m, z.pair_rows, stride=z.targets), :] = turned[0 : z.pair_rows]
        return carry

    lax.fori_loop(0, z.targets // step, weight_step, 0, unroll=2)

    lane_list = lax.broadcasted_iota(jnp.int32, (z.lists, LANES), 1)
    chunk_tiles = SPAN // LANES

    def compact_step(u, carry):
        first, second = list_ref[2 * u], list_ref[2 * u + 1]
        left_shift = (first % 2) * half_block
        right_shift = (1 - second % 2) * half_block
        left = pltpu.roll(full[first // 2], left_shift, 1)
        right = pltpu.roll(full[second // 2], right_shift, 1)
        left = jnp.where(2 * u < count, left, 0.0)
        right = jnp.where(2 * u + 1 < count, right, 0.0)
        at_list = pl.ds(pl.multiple_of(u // chunk_tiles * z.lists, z.lists), z.lists)
        at_lane = pl.ds(pl.multiple_of(u % chunk_tiles * LANES, LANES), LANES)
        both = jnp.where(lane_list < half_block, left, right)
        tabf[u] = both
        table[at_list, at_lane] = both.astype(bf16)
        return carry

    lax.fori_loop(0, (n_tiles + chunk_tiles - 1) // chunk_tiles * chunk_tiles, compact_step, 0)

    local = lax.broadcasted_iota(jnp.int32, (SPAN, LANES), 0).astype(f32).astype(bf16)
    nothing = jnp.zeros((SPAN, LANES), bf16)
    side = 2 * z.targets

    def tall_row(few):
        return jnp.concatenate([few.astype(f32).astype(bf16)] * (SPAN // 16), axis=0)

    def run(tiles):
        depth = (tiles * LANES + SPAN - 1) // SPAN

        def one_tile(u, carry, turn=False):
            acc[...] = jnp.zeros_like(acc)
            held[...] = jnp.zeros_like(held)

            def spread(n):
                if turn:
                    at = pl.multiple_of(n * DEPTH, DEPTH)
                    turned = tall[pl.ds(at, DEPTH), :].T.astype(bf16)
                    weights[n] = turned
                else:
                    turned = weights[n]
                total = jnp.dot(turned, held[...], preferred_element_type=f32)
                for cc in range(z.strings):
                    acc[cc] += total[
                        cc * side : (cc + 1) * side, cc * LANES : (cc + 1) * LANES
                    ]

            def keep(q, value):
                value = value.astype(bf16)
                for cc in range(z.strings):
                    held[q * z.targets : (q + 1) * z.targets, cc * LANES : (cc + 1) * LANES] = (
                        value[cc * z.targets : (cc + 1) * z.targets]
                    )

            def gather(q, spot, sign):
                lanes = spot & (LANES - 1)
                tile = lax.shift_right_arithmetic(spot, LANES.bit_length() - 1)
                hits = [tile == k for k in range(tiles)]
                parts = []
                for row in range(0, z.lists, 8):
                    value = jnp.zeros((8, LANES), f32)
                    for k in range(tiles):
                        taken = jnp.take_along_axis(
                            tabf[k, row : row + 8, :], lanes, axis=1, mode="promise_in_bounds"
                        )
                        value = jnp.where(hits[k], taken, value)
                    parts.append(value * sign)
                keep(q, jnp.concatenate(parts, axis=0))

            def one_chunk(n, inner):
                spread(jnp.maximum(n - 1, 0))
                picks, chunk, chosen = [], [], []
                for q in range(z.chunk_pairs):
                    at = pl.ds(n * z.chunk_pairs + q, 1)
                    code = jnp.broadcast_to(spot_ref[u, at, :], (16, LANES))
                    spot = jnp.abs(code) - 1
                    sign = jnp.clip(code, -1, 1)
                    if q % GATHERED == GATHERED - 1:
                        gather(q, spot[0:8], sign[0:8].astype(f32))
                        continue
                    chosen.append(q)
                    hit = local == tall_row(spot & (SPAN - 1))
                    picks.append(jnp.where(hit, tall_row(sign), nothing))
                    chunk.append(lax.shift_right_arithmetic(spot[0:8], SPAN.bit_length() - 1))
                pick = jnp.concatenate(picks, axis=1)
                found = jnp.dot(
                    table[0 : depth * z.lists, :], pick, preferred_element_type=f32
                )
                for k, q in enumerate(chosen):
                    lanes = slice(k * LANES, (k + 1) * LANES)
                    value = found[0 : z.lists, lanes]
                    for m in range(1, depth):
                        other = found[m * z.lists : (m + 1) * z.lists, lanes]
                        here = jnp.concatenate([chunk[k] == m] * (z.lists // 8), axis=0)
                        value = jnp.where(here, other, value)
                    keep(q, value)
                return inner

            lax.fori_loop(0, z.chunks, one_chunk, 0)
            spread(z.chunks - 1)
            for cc in range(z.strings):
                total = acc[cc, 0 : z.targets, :] + acc[cc, z.targets : 2 * z.targets, :]
                result[u, pl.ds(cc, z.targets, stride=z.strings), :] = total
            return carry

        if z.share == 1:
            one_tile(0, 0, turn=True)
            lax.fori_loop(1, n_tiles, one_tile, 0)
        else:
            part = part_ref[0]
            mine = (n_tiles - part + z.share - 1) // z.share
            lax.fori_loop(0, mine, lambda n, carry: one_tile(n * z.share + part, carry, True), 0)

    lower = 0
    for tiles in sorted({min(tiles, z.tiles) for tiles in (4, 5, 6, 8, z.tiles)}):
        pl.when((n_tiles > lower) & (n_tiles <= tiles))(functools.partial(run, tiles))
        lower = tiles

    wide = z.src * z.strings
    lane_out = lax.broadcasted_iota(jnp.int32, (z.targets * z.strings, LANES), 1)
    for w in range(z.tiles):
        sides = []
        for at_side in range(2):
            rank = rank_ref[2 * w + at_side]
            spot = jnp.maximum(rank, 0)
            shift = ((spot + at_side) % 2) * half_block
            moved = pltpu.roll(result[spot // 2], shift, 1)
            here = rank >= 0
            if z.share > 1:
                here = here & ((spot // 2) % z.share == part_ref[0])
            sides.append(jnp.where(here, moved, 0.0))
        both = jnp.where(lane_out < half_block, sides[0], sides[1])
        for j in range(z.n_beta):
            device = w // z.halves * z.n_beta + j
            out_ref[device, w % z.halves] = both[j * wide : (j + 1) * wide]


def finish_kernel(z, irrep_ref, rx_ref, diag_ref, coef_ref, out_ref):
    wide = z.src * z.strings
    stride = z.share * z.halves * wide

    def column(first):
        rows = [
            rx_ref[pl.ds(part * z.halves * wide + first, z.sets, stride=stride), :]
            for part in range(z.share)
        ]
        return functools.reduce(jnp.add, rows)

    columns = []
    for t in range(z.src):
        for cc in range(z.strings):
            firsts = [h * wide + t * z.strings + cc for h in range(z.halves)]
            columns.append(jnp.concatenate([column(first) for first in firsts], axis=1))
    added = jnp.concatenate(columns, axis=0).T
    total = diag_ref[...] * coef_ref[...].astype(jnp.float32) + added
    for b in range(z.own):
        at = slice(b * z.block, (b + 1) * z.block)
        out_ref[at, :] = jnp.where(irrep_ref[b] == 0, total[at], 0.0)


def on_device(
    coefficients, diagonal, integrals, alpha_row, alpha_sign, beta_block, beta_sign, block_irrep
):
    z = Sizes(coefficients, integrals, alpha_row, beta_sign, block_irrep)
    f32, i32, bf16 = jnp.float32, jnp.int32, jnp.bfloat16
    alpha_rank = lax.axis_index("alpha")
    params = pltpu.CompilerParams(vmem_limit_bytes=32 * 1024 * 1024)

    first = jnp.minimum(alpha_rank, z.senders - 1) * z.per
    own_signs = lax.dynamic_slice_in_dim(beta_sign, first, z.per, 0)
    own_blocks = lax.dynamic_slice_in_dim(beta_block, first, z.per, 0)
    code = own_signs.reshape(z.per, z.pairs, z.block) * (own_blocks + 1)[:, :, None]
    packed = pl.pallas_call(
        functools.partial(pack_kernel, z),
        out_shape=jax.ShapeDtypeStruct((z.devices * z.pack, LANES), bf16),
        in_specs=[VMEM, VMEM],
        out_specs=VMEM,
        scratch_shapes=[pltpu.VMEM((z.devices * z.pack, LANES), f32)],
        compiler_params=params,
    )(coefficients, code.astype(f32))
    arrived = lax.all_to_all(
        packed.reshape(z.devices, z.pack, LANES), ("alpha", "beta"), 0, 0, tiled=True
    ).reshape(z.devices * z.pack, LANES)

    pad = z.pair_lanes - z.pairs
    wide = z.src * z.strings
    part = (alpha_rank * z.n_beta + lax.axis_index("beta")) % z.share
    integ = jnp.pad(integrals, ((0, pad), (0, pad)))
    lists = [pltpu.SMEM((z.blocks,), i32), pltpu.SMEM((z.blocks + 8,), i32)]
    spots = pl.pallas_call(
        functools.partial(index_kernel, z),
        out_shape=jax.ShapeDtypeStruct((z.tiles, z.pair_rows, LANES), i32),
        in_specs=[SMEM, VMEM, VMEM],
        out_specs=VMEM,
        scratch_shapes=lists,
        compiler_params=pltpu.CompilerParams(vmem_limit_bytes=16 * 1024 * 1024),
        cost_estimate=pl.CostEstimate(
            flops=50 * z.pairs * z.all_rows,
            bytes_accessed=12 * z.pairs * z.all_rows,
            transcendentals=0,
        ),
    )(block_irrep, alpha_row, alpha_sign)
    terms = pl.pallas_call(
        functools.partial(main_kernel, z),
        out_shape=jax.ShapeDtypeStruct((z.devices, z.halves, wide, LANES), f32),
        in_specs=[SMEM, SMEM, VMEM, VMEM, VMEM],
        out_specs=VMEM,
        scratch_shapes=[
            pltpu.VMEM((z.devices * z.pack, LANES), f32),
            pltpu.VMEM((z.tiles, z.lists, LANES), f32),
            pltpu.VMEM((z.tiles, z.lists, LANES), f32),
            pltpu.VMEM((z.tiles * LANES // SPAN * z.lists, SPAN), bf16),
            pltpu.VMEM((z.pair_tiles, z.lists, LANES), f32),
            pltpu.VMEM((z.pair_rows * z.targets, LANES), f32),
            pltpu.VMEM((z.chunks, LANES, DEPTH), bf16),
            pltpu.VMEM((z.strings, 2 * z.targets, LANES), f32),
            pltpu.VMEM((DEPTH, z.strings * LANES), bf16),
            pltpu.VMEM((z.tiles, z.targets * z.strings, LANES), f32),
        ]
        + lists,
        compiler_params=params,
    )(block_irrep, part.astype(i32)[None], arrived, integ, spots)

    back = lax.all_to_all(terms, ("alpha", "beta"), 0, 0, tiled=True).reshape(-1, LANES)
    own_irrep = lax.dynamic_slice_in_dim(block_irrep, alpha_rank * z.own, z.own, 0)
    return pl.pallas_call(
        functools.partial(finish_kernel, z),
        out_shape=jax.ShapeDtypeStruct((z.rows, z.cols), f32),
        in_specs=[SMEM, VMEM, VMEM, VMEM],
        out_specs=VMEM,
        compiler_params=params,
    )(own_irrep, back, diagonal, coefficients)


def solution(mesh):
    return jax.shard_map(
        on_device,
        mesh=mesh,
        in_specs=(
            P("alpha", "beta"),
            P("alpha", "beta"),
            P(),
            P(),
            P(),
            P("beta", None),
            P("beta", None),
            P(),
        ),
        out_specs=P("alpha", "beta"),
        check_vma=False,
    )
```

```python
import functools

import jax
import jax.numpy as jnp
from jax import lax
from jax.experimental import pallas as pl
from jax.experimental.pallas import tpu as pltpu
from jax.sharding import PartitionSpec as P

LANES = 128
DEPTH = 512
WIDE = 256
GATHERED = 3
VMEM = pl.BlockSpec(memory_space=pltpu.VMEM)
SMEM = pl.BlockSpec(memory_space=pltpu.SMEM)


def round_up(size, step):
    return -(-size // step) * step


class Sizes:
    def __init__(self, coefficients, integrals, alpha_row, beta_sign, block_irrep):
        self.n_alpha = lax.axis_size("alpha")
        self.n_beta = lax.axis_size("beta")
        self.devices = self.n_alpha * self.n_beta
        self.rows, self.cols = coefficients.shape
        self.pairs = integrals.shape[0]
        self.block = beta_sign.shape[1] // self.pairs
        self.src = self.cols // self.block
        self.targets = self.n_beta * self.src
        self.all_rows = alpha_row.shape[1]
        self.blocks = block_irrep.shape[0]
        self.own = self.rows // self.block
        self.share = max(1, self.devices // self.block)
        self.sets = self.devices // self.share
        self.strings = self.block // self.sets
        self.halves = self.rows // LANES
        self.tiles = self.all_rows // LANES
        self.per = max(1, self.src // self.n_alpha)
        self.senders = self.src // self.per
        self.group = self.src * self.strings
        self.lists = self.n_beta * self.group
        self.chunk_pairs = DEPTH // self.targets
        self.pair_rows = round_up(self.pairs, self.chunk_pairs)
        self.chunks = self.pair_rows // self.chunk_pairs
        self.pair_lanes = round_up(self.pairs, LANES)
        self.pair_tiles = self.pair_lanes // LANES
        self.coef_rows = self.halves * self.group
        self.sign_rows = self.per * self.strings * self.pair_tiles
        self.pack = round_up(self.coef_rows + self.sign_rows, 8)


def pack_kernel(z, coef_ref, sign_ref, out_ref, scratch):
    scratch[...] = jnp.zeros_like(scratch)
    turned = coef_ref[...].astype(jnp.float32).T
    for half in range(z.halves):
        for g in range(z.group):
            row = half * z.group + g
            for part in range(z.share):
                scratch[pl.ds(row + part * z.pack, z.sets, stride=z.share * z.pack), :] = turned[
                    g * z.sets : (g + 1) * z.sets, half * LANES : (half + 1) * LANES
                ]
    for s in range(z.per):
        code = sign_ref[s].T
        code = jnp.concatenate(
            [code, jnp.zeros((z.block, z.pair_lanes - z.pairs), jnp.float32)], axis=1
        )
        for cc in range(z.strings):
            for k in range(z.pair_tiles):
                row = z.coef_rows + (s * z.strings + cc) * z.pair_tiles + k
                for part in range(z.share):
                    scratch[pl.ds(row + part * z.pack, z.sets, stride=z.share * z.pack), :] = code[
                        cc * z.sets : (cc + 1) * z.sets, k * LANES : (k + 1) * LANES
                    ]
    out_ref[...] = scratch[...].astype(jnp.bfloat16)


def live_blocks(z, irrep_ref, rank_ref, list_ref):
    count = jnp.int32(0)
    lane_row = lax.broadcasted_iota(jnp.int32, (1, LANES), 1)
    ranks = jnp.full((1, LANES), -1, jnp.int32)
    for extra in range(z.blocks + 8):
        list_ref[extra] = 0
    for g in range(z.blocks):
        live = irrep_ref[g] == 0
        rank = jnp.where(live, count, -1)
        rank_ref[g] = rank
        list_ref[count] = g
        ranks = jnp.where(lane_row == g, rank, ranks)
        count = count + live.astype(jnp.int32)
    for extra in range(4):
        list_ref[count + extra] = 0
    return count, ranks


def index_kernel(z, irrep_ref, row_ref, sign_ref, out_ref, rank_ref, list_ref):
    count, ranks = live_blocks(z, irrep_ref, rank_ref, list_ref)
    lane_pair = lax.broadcasted_iota(jnp.int32, (z.pairs, LANES), 1)
    tail = z.pairs // 8 * 8

    def compact_step(u, carry):
        first, second = list_ref[2 * u], list_ref[2 * u + 1]
        left_shift = (first % 2) * z.block
        right_shift = (1 - second % 2) * z.block

        def merged(ref):
            at_first = pl.ds(pl.multiple_of(first // 2 * LANES, LANES), LANES)
            at_second = pl.ds(pl.multiple_of(second // 2 * LANES, LANES), LANES)
            return jnp.where(
                lane_pair < z.block,
                pltpu.roll(ref[:, at_first], left_shift, 1),
                pltpu.roll(ref[:, at_second], right_shift, 1),
            )

        source = merged(row_ref)
        signs = merged(sign_ref)
        block = source // z.block
        rank = jnp.take_along_axis(
            jnp.broadcast_to(ranks, (z.pairs, LANES)), block, axis=1, mode="promise_in_bounds"
        )
        spot = rank * z.block + (source & (z.block - 1))
        inside = (lane_pair < z.block) | (2 * u + 1 < count)
        out_ref[u, tail : z.pair_rows, :] = jnp.zeros((z.pair_rows - tail, LANES), jnp.int32)
        out_ref[u, 0 : z.pairs, :] = jnp.where((rank >= 0) & inside, signs * (spot + 1), 0)
        return carry

    lax.fori_loop(0, (count + 1) // 2, compact_step, 0)


def main_kernel(
    z,
    irrep_ref,
    part_ref,
    rx_ref,
    integ_ref,
    spot_ref,
    out_ref,
    rxf,
    full,
    tabf,
    table,
    codes,
    tall,
    weights,
    acc,
    held,
    result,
    rank_ref,
    list_ref,
):
    f32, bf16 = jnp.float32, jnp.bfloat16
    half_block = z.block
    count, _ = live_blocks(z, irrep_ref, rank_ref, list_ref)
    n_tiles = (count + 1) // 2

    rxf[...] = rx_ref[...].astype(f32)
    for i in range(z.n_alpha):
        base = i * z.n_beta * z.pack
        for half in range(z.halves):
            for s in range(z.src):
                for cc in range(z.strings):
                    source = base + half * z.group + s * z.strings + cc
                    dest = cc * z.targets + s
                    full[i * z.halves + half, pl.ds(dest, z.n_beta, stride=z.src), :] = rxf[
                        pl.ds(source, z.n_beta, stride=z.pack), :
                    ]
        for s in range(z.per if i < z.senders else 0):
            for cc in range(z.strings):
                for k in range(z.pair_tiles):
                    source = base + z.coef_rows + (s * z.strings + cc) * z.pair_tiles + k
                    dest = (i * z.per + s) * z.strings + cc
                    codes[k, pl.ds(dest, z.n_beta, stride=z.group), :] = rxf[
                        pl.ds(source, z.n_beta, stride=z.pack), :
                    ]

    step = 4
    target = (lax.broadcasted_iota(jnp.int32, (z.targets, z.pair_lanes), 0) + 1).astype(f32)

    def weight_step(n, carry):
        parts = []
        for m in range(step * z.strings):
            code = jnp.concatenate(
                [codes[k, pl.ds(n * step * z.strings + m, 1), :] for k in range(z.pair_tiles)],
                axis=1,
            )
            hit = jnp.where(code == target, 1.0, 0.0) - jnp.where(code == -target, 1.0, 0.0)
            parts.append(hit)
        hits = jnp.concatenate(parts, axis=0).astype(bf16)
        found = jnp.dot(hits, integ_ref[...], preferred_element_type=f32)
        high = found.astype(bf16).astype(f32)
        low = found - high
        for m in range(step):
            rows = []
            for cc in range(z.strings):
                at = (m * z.strings + cc) * z.targets
                rows += [high[at : at + z.targets], low[at : at + z.targets]]
            turned = jnp.concatenate(rows, axis=0).T
            tall[pl.ds(n * step + m, z.pair_rows, stride=z.targets), :] = turned[0 : z.pair_rows]
        return carry

    lax.fori_loop(0, z.targets // step, weight_step, 0, unroll=2)

    lane_list = lax.broadcasted_iota(jnp.int32, (z.lists, LANES), 1)

    def compact_step(u, carry):
        first, second = list_ref[2 * u], list_ref[2 * u + 1]
        left_shift = (first % 2) * half_block
        right_shift = (1 - second % 2) * half_block
        left = pltpu.roll(full[first // 2], left_shift, 1)
        right = pltpu.roll(full[second // 2], right_shift, 1)
        left = jnp.where(2 * u < count, left, 0.0)
        right = jnp.where(2 * u + 1 < count, right, 0.0)
        tabf[u] = jnp.where(lane_list < half_block, left, right)
        return carry

    lax.fori_loop(0, z.tiles, compact_step, 0)

    side = 2 * z.targets

    def run(blocks, span):
        depth = (blocks * z.block + span - 1) // span
        tiles = (blocks + 1) // 2
        local = lax.broadcasted_iota(jnp.int32, (span, LANES), 0).astype(f32).astype(bf16)
        nothing = jnp.zeros((span, LANES), bf16)

        def tall_row(few):
            return jnp.concatenate([few.astype(f32).astype(bf16)] * (span // 16), axis=0)

        def chunk_of(spot):
            if span & (span - 1) == 0:
                return lax.shift_right_arithmetic(spot, span.bit_length() - 1)
            return sum((spot >= span * m).astype(jnp.int32) for m in range(1, depth))

        for m in range(depth):
            for k in range(0, span, LANES):
                block = (m * span + k) // z.block
                left, right = tabf[min(block // 2, z.tiles - 1)], jnp.zeros((z.lists, LANES), f32)
                if block % 2:
                    left = pltpu.roll(left, half_block, 1)
                    if block // 2 + 1 < z.tiles:
                        right = pltpu.roll(tabf[block // 2 + 1], half_block, 1)
                    left = jnp.where(lane_list < half_block, left, right)
                table[m * z.lists : (m + 1) * z.lists, k : k + LANES] = left.astype(bf16)

        def one_tile(u, carry, turn=False):
            acc[...] = jnp.zeros_like(acc)
            held[...] = jnp.zeros_like(held)

            def spread(n):
                if turn:
                    at = pl.multiple_of(n * DEPTH, DEPTH)
                    turned = tall[pl.ds(at, DEPTH), :].T.astype(bf16)
                    weights[n] = turned
                else:
                    turned = weights[n]
                total = jnp.dot(turned, held[...], preferred_element_type=f32)
                for cc in range(z.strings):
                    acc[cc] += total[
                        cc * side : (cc + 1) * side, cc * LANES : (cc + 1) * LANES
                    ]

            def keep(q, value):
                value = value.astype(bf16)
                for cc in range(z.strings):
                    held[q * z.targets : (q + 1) * z.targets, cc * LANES : (cc + 1) * LANES] = (
                        value[cc * z.targets : (cc + 1) * z.targets]
                    )

            def gather(q, spot, sign):
                lanes = spot & (LANES - 1)
                tile = lax.shift_right_arithmetic(spot, LANES.bit_length() - 1)
                hits = [tile == k for k in range(tiles)]
                parts = []
                for row in range(0, z.lists, 8):
                    value = jnp.zeros((8, LANES), f32)
                    for k in range(tiles):
                        taken = jnp.take_along_axis(
                            tabf[k, row : row + 8, :], lanes, axis=1, mode="promise_in_bounds"
                        )
                        value = jnp.where(hits[k], taken, value)
                    parts.append(value * sign)
                keep(q, jnp.concatenate(parts, axis=0))

            def one_chunk(n, inner):
                spread(jnp.maximum(n - 1, 0))
                picks, chunk, chosen = [], [], []
                for q in range(z.chunk_pairs):
                    at = pl.ds(n * z.chunk_pairs + q, 1)
                    code = jnp.broadcast_to(spot_ref[u, at, :], (16, LANES))
                    spot = jnp.abs(code) - 1
                    sign = jnp.clip(code, -1, 1)
                    if q % GATHERED == GATHERED - 1:
                        gather(q, spot[0:8], sign[0:8].astype(f32))
                        continue
                    chosen.append(q)
                    part = chunk_of(spot)
                    hit = local == tall_row(spot - part * span)
                    picks.append(jnp.where(hit, tall_row(sign), nothing))
                    chunk.append(part[0:8])
                pick = jnp.concatenate(picks, axis=1)
                found = jnp.dot(
                    table[0 : depth * z.lists, 0:span], pick, preferred_element_type=f32
                )
                for k, q in enumerate(chosen):
                    lanes = slice(k * LANES, (k + 1) * LANES)
                    value = found[0 : z.lists, lanes]
                    for m in range(1, depth):
                        other = found[m * z.lists : (m + 1) * z.lists, lanes]
                        here = jnp.concatenate([chunk[k] == m] * (z.lists // 8), axis=0)
                        value = jnp.where(here, other, value)
                    keep(q, value)
                return inner

            lax.fori_loop(0, z.chunks, one_chunk, 0)
            spread(z.chunks - 1)
            for cc in range(z.strings):
                total = acc[cc, 0 : z.targets, :] + acc[cc, z.targets : 2 * z.targets, :]
                result[u, pl.ds(cc, z.targets, stride=z.strings), :] = total
            return carry

        if z.share == 1:
            one_tile(0, 0, turn=True)
            lax.fori_loop(1, n_tiles, one_tile, 0)
        else:
            part = part_ref[0]
            mine = (n_tiles - part + z.share - 1) // z.share
            lax.fori_loop(0, mine, lambda n, carry: one_tile(n * z.share + part, carry, True), 0)

    lower = 0
    cases = [(6, 192), (8, WIDE), (9, 192), (10, WIDE), (12, WIDE), (16, WIDE), (z.blocks, WIDE)]
    for blocks, span in cases:
        if lower < blocks <= z.blocks:
            pl.when((count > lower) & (count <= blocks))(functools.partial(run, blocks, span))
            lower = blocks

    wide = z.src * z.strings
    lane_out = lax.broadcasted_iota(jnp.int32, (z.targets * z.strings, LANES), 1)
    for w in range(z.tiles):
        sides = []
        for at_side in range(2):
            rank = rank_ref[2 * w + at_side]
            spot = jnp.maximum(rank, 0)
            shift = ((spot + at_side) % 2) * half_block
            moved = pltpu.roll(result[spot // 2], shift, 1)
            here = rank >= 0
            if z.share > 1:
                here = here & ((spot // 2) % z.share == part_ref[0])
            sides.append(jnp.where(here, moved, 0.0))
        both = jnp.where(lane_out < half_block, sides[0], sides[1])
        for j in range(z.n_beta):
            device = w // z.halves * z.n_beta + j
            out_ref[device, w % z.halves] = both[j * wide : (j + 1) * wide]


def finish_kernel(z, irrep_ref, rx_ref, diag_ref, coef_ref, out_ref):
    wide = z.src * z.strings
    stride = z.share * z.halves * wide

    def column(first):
        rows = [
            rx_ref[pl.ds(part * z.halves * wide + first, z.sets, stride=stride), :]
            for part in range(z.share)
        ]
        return functools.reduce(jnp.add, rows)

    columns = []
    for t in range(z.src):
        for cc in range(z.strings):
            firsts = [h * wide + t * z.strings + cc for h in range(z.halves)]
            columns.append(jnp.concatenate([column(first) for first in firsts], axis=1))
    added = jnp.concatenate(columns, axis=0).T
    total = diag_ref[...] * coef_ref[...].astype(jnp.float32) + added
    for b in range(z.own):
        at = slice(b * z.block, (b + 1) * z.block)
        out_ref[at, :] = jnp.where(irrep_ref[b] == 0, total[at], 0.0)


def on_device(
    coefficients, diagonal, integrals, alpha_row, alpha_sign, beta_block, beta_sign, block_irrep
):
    z = Sizes(coefficients, integrals, alpha_row, beta_sign, block_irrep)
    f32, i32, bf16 = jnp.float32, jnp.int32, jnp.bfloat16
    alpha_rank = lax.axis_index("alpha")
    params = pltpu.CompilerParams(vmem_limit_bytes=32 * 1024 * 1024)

    first = jnp.minimum(alpha_rank, z.senders - 1) * z.per
    own_signs = lax.dynamic_slice_in_dim(beta_sign, first, z.per, 0)
    own_blocks = lax.dynamic_slice_in_dim(beta_block, first, z.per, 0)
    code = own_signs.reshape(z.per, z.pairs, z.block) * (own_blocks + 1)[:, :, None]
    packed = pl.pallas_call(
        functools.partial(pack_kernel, z),
        out_shape=jax.ShapeDtypeStruct((z.devices * z.pack, LANES), bf16),
        in_specs=[VMEM, VMEM],
        out_specs=VMEM,
        scratch_shapes=[pltpu.VMEM((z.devices * z.pack, LANES), f32)],
        compiler_params=params,
    )(coefficients, code.astype(f32))
    arrived = lax.all_to_all(
        packed.reshape(z.devices, z.pack, LANES), ("alpha", "beta"), 0, 0, tiled=True
    ).reshape(z.devices * z.pack, LANES)

    pad = z.pair_lanes - z.pairs
    wide = z.src * z.strings
    part = (alpha_rank * z.n_beta + lax.axis_index("beta")) % z.share
    integ = jnp.pad(integrals, ((0, pad), (0, pad)))
    lists = [pltpu.SMEM((z.blocks,), i32), pltpu.SMEM((z.blocks + 8,), i32)]
    spots = pl.pallas_call(
        functools.partial(index_kernel, z),
        out_shape=jax.ShapeDtypeStruct((z.tiles, z.pair_rows, LANES), i32),
        in_specs=[SMEM, VMEM, VMEM],
        out_specs=VMEM,
        scratch_shapes=lists,
        compiler_params=pltpu.CompilerParams(vmem_limit_bytes=16 * 1024 * 1024),
        cost_estimate=pl.CostEstimate(
            flops=50 * z.pairs * z.all_rows,
            bytes_accessed=12 * z.pairs * z.all_rows,
            transcendentals=0,
        ),
    )(block_irrep, alpha_row, alpha_sign)
    terms = pl.pallas_call(
        functools.partial(main_kernel, z),
        out_shape=jax.ShapeDtypeStruct((z.devices, z.halves, wide, LANES), f32),
        in_specs=[SMEM, SMEM, VMEM, VMEM, VMEM],
        out_specs=VMEM,
        scratch_shapes=[
            pltpu.VMEM((z.devices * z.pack, LANES), f32),
            pltpu.VMEM((z.tiles, z.lists, LANES), f32),
            pltpu.VMEM((z.tiles, z.lists, LANES), f32),
            pltpu.VMEM((round_up(z.all_rows, WIDE) // WIDE * z.lists, WIDE), bf16),
            pltpu.VMEM((z.pair_tiles, z.lists, LANES), f32),
            pltpu.VMEM((z.pair_rows * z.targets, LANES), f32),
            pltpu.VMEM((z.chunks, LANES, DEPTH), bf16),
            pltpu.VMEM((z.strings, 2 * z.targets, LANES), f32),
            pltpu.VMEM((DEPTH, z.strings * LANES), bf16),
            pltpu.VMEM((z.tiles, z.targets * z.strings, LANES), f32),
        ]
        + lists,
        compiler_params=params,
    )(block_irrep, part.astype(i32)[None], arrived, integ, spots)

    back = lax.all_to_all(terms, ("alpha", "beta"), 0, 0, tiled=True).reshape(-1, LANES)
    own_irrep = lax.dynamic_slice_in_dim(block_irrep, alpha_rank * z.own, z.own, 0)
    return pl.pallas_call(
        functools.partial(finish_kernel, z),
        out_shape=jax.ShapeDtypeStruct((z.rows, z.cols), f32),
        in_specs=[SMEM, VMEM, VMEM, VMEM],
        out_specs=VMEM,
        compiler_params=params,
    )(own_irrep, back, diagonal, coefficients)


def solution(mesh):
    return jax.shard_map(
        on_device,
        mesh=mesh,
        in_specs=(
            P("alpha", "beta"),
            P("alpha", "beta"),
            P(),
            P(),
            P(),
            P("beta", None),
            P("beta", None),
            P(),
        ),
        out_specs=P("alpha", "beta"),
        check_vma=False,
    )
```

```python
import functools

import jax
import jax.numpy as jnp
from jax import lax
from jax.experimental import pallas as pl
from jax.experimental.pallas import tpu as pltpu
from jax.sharding import PartitionSpec as P

LANES = 128
DEPTH = 512
WIDE = 256
GATHERED = 4
VMEM = pl.BlockSpec(memory_space=pltpu.VMEM)
SMEM = pl.BlockSpec(memory_space=pltpu.SMEM)


def round_up(size, step):
    return -(-size // step) * step


class Sizes:
    def __init__(self, coefficients, integrals, alpha_row, beta_sign, block_irrep):
        self.n_alpha = lax.axis_size("alpha")
        self.n_beta = lax.axis_size("beta")
        self.devices = self.n_alpha * self.n_beta
        self.rows, self.cols = coefficients.shape
        self.pairs = integrals.shape[0]
        self.block = beta_sign.shape[1] // self.pairs
        self.src = self.cols // self.block
        self.targets = self.n_beta * self.src
        self.all_rows = alpha_row.shape[1]
        self.blocks = block_irrep.shape[0]
        self.own = self.rows // self.block
        self.share = max(1, self.devices // self.block)
        self.sets = self.devices // self.share
        self.strings = self.block // self.sets
        self.halves = self.rows // LANES
        self.tiles = self.all_rows // LANES
        self.per = max(1, self.src // self.n_alpha)
        self.senders = self.src // self.per
        self.group = self.src * self.strings
        self.lists = self.n_beta * self.group
        self.chunk_pairs = DEPTH // self.targets
        self.pair_rows = round_up(self.pairs, self.chunk_pairs)
        self.chunks = self.pair_rows // self.chunk_pairs
        self.pair_lanes = round_up(self.pairs, LANES)
        self.pair_tiles = self.pair_lanes // LANES
        self.coef_rows = self.halves * self.group
        self.sign_rows = self.per * self.strings * self.pair_tiles
        self.pack = round_up(self.coef_rows + self.sign_rows, 8)


def pack_kernel(z, coef_ref, sign_ref, out_ref, scratch):
    scratch[...] = jnp.zeros_like(scratch)
    turned = coef_ref[...].astype(jnp.float32).T
    for half in range(z.halves):
        for g in range(z.group):
            row = half * z.group + g
            for part in range(z.share):
                scratch[pl.ds(row + part * z.pack, z.sets, stride=z.share * z.pack), :] = turned[
                    g * z.sets : (g + 1) * z.sets, half * LANES : (half + 1) * LANES
                ]
    for s in range(z.per):
        code = sign_ref[s].T
        code = jnp.concatenate(
            [code, jnp.zeros((z.block, z.pair_lanes - z.pairs), jnp.float32)], axis=1
        )
        for cc in range(z.strings):
            for k in range(z.pair_tiles):
                row = z.coef_rows + (s * z.strings + cc) * z.pair_tiles + k
                for part in range(z.share):
                    scratch[pl.ds(row + part * z.pack, z.sets, stride=z.share * z.pack), :] = code[
                        cc * z.sets : (cc + 1) * z.sets, k * LANES : (k + 1) * LANES
                    ]
    out_ref[...] = scratch[...].astype(jnp.bfloat16)


def live_blocks(z, irrep_ref, rank_ref, list_ref):
    count = jnp.int32(0)
    lane_row = lax.broadcasted_iota(jnp.int32, (1, LANES), 1)
    ranks = jnp.full((1, LANES), -1, jnp.int32)
    for extra in range(z.blocks + 8):
        list_ref[extra] = 0
    for g in range(z.blocks):
        live = irrep_ref[g] == 0
        rank = jnp.where(live, count, -1)
        rank_ref[g] = rank
        list_ref[count] = g
        ranks = jnp.where(lane_row == g, rank, ranks)
        count = count + live.astype(jnp.int32)
    for extra in range(4):
        list_ref[count + extra] = 0
    return count, ranks


def index_kernel(z, irrep_ref, row_ref, sign_ref, out_ref, rank_ref, list_ref):
    count, ranks = live_blocks(z, irrep_ref, rank_ref, list_ref)
    lane_pair = lax.broadcasted_iota(jnp.int32, (z.pairs, LANES), 1)
    tail = z.pairs // 8 * 8

    def compact_step(u, carry):
        first, second = list_ref[2 * u], list_ref[2 * u + 1]
        left_shift = (first % 2) * z.block
        right_shift = (1 - second % 2) * z.block

        def merged(ref):
            at_first = pl.ds(pl.multiple_of(first // 2 * LANES, LANES), LANES)
            at_second = pl.ds(pl.multiple_of(second // 2 * LANES, LANES), LANES)
            return jnp.where(
                lane_pair < z.block,
                pltpu.roll(ref[:, at_first], left_shift, 1),
                pltpu.roll(ref[:, at_second], right_shift, 1),
            )

        source = merged(row_ref)
        signs = merged(sign_ref)
        block = source // z.block
        rank = jnp.take_along_axis(
            jnp.broadcast_to(ranks, (z.pairs, LANES)), block, axis=1, mode="promise_in_bounds"
        )
        spot = rank * z.block + (source & (z.block - 1))
        inside = (lane_pair < z.block) | (2 * u + 1 < count)
        out_ref[u, tail : z.pair_rows, :] = jnp.zeros((z.pair_rows - tail, LANES), jnp.int32)
        out_ref[u, 0 : z.pairs, :] = jnp.where((rank >= 0) & inside, signs * (spot + 1), 0)
        return carry

    lax.fori_loop(0, (count + 1) // 2, compact_step, 0)

    @pl.when(count % 2 == 1)
    def _():
        u = count // 2
        half = z.pair_rows // 2
        even = out_ref[u, pl.ds(0, half, stride=2), :]
        odd = out_ref[u, pl.ds(1, half, stride=2), :]
        out_ref[u, 0:half, :] = even + pltpu.roll(odd, z.block, 1)


def main_kernel(
    z,
    irrep_ref,
    part_ref,
    rx_ref,
    integ_ref,
    spot_ref,
    out_ref,
    rxf,
    full,
    tabf,
    table,
    codes,
    tall,
    weights,
    acc,
    held,
    result,
    rank_ref,
    list_ref,
):
    f32, bf16 = jnp.float32, jnp.bfloat16
    half_block = z.block
    count, _ = live_blocks(z, irrep_ref, rank_ref, list_ref)
    n_tiles = (count + 1) // 2

    rxf[...] = rx_ref[...].astype(f32)
    for i in range(z.n_alpha):
        base = i * z.n_beta * z.pack
        for half in range(z.halves):
            for s in range(z.src):
                for cc in range(z.strings):
                    source = base + half * z.group + s * z.strings + cc
                    dest = cc * z.targets + s
                    full[i * z.halves + half, pl.ds(dest, z.n_beta, stride=z.src), :] = rxf[
                        pl.ds(source, z.n_beta, stride=z.pack), :
                    ]
        for s in range(z.per if i < z.senders else 0):
            for cc in range(z.strings):
                for k in range(z.pair_tiles):
                    source = base + z.coef_rows + (s * z.strings + cc) * z.pair_tiles + k
                    dest = (i * z.per + s) * z.strings + cc
                    codes[k, pl.ds(dest, z.n_beta, stride=z.group), :] = rxf[
                        pl.ds(source, z.n_beta, stride=z.pack), :
                    ]

    step = 4
    target = (lax.broadcasted_iota(jnp.int32, (z.targets, z.pair_lanes), 0) + 1).astype(f32)

    def weight_step(n, carry):
        parts = []
        for m in range(step * z.strings):
            code = jnp.concatenate(
                [codes[k, pl.ds(n * step * z.strings + m, 1), :] for k in range(z.pair_tiles)],
                axis=1,
            )
            hit = jnp.where(code == target, 1.0, 0.0) - jnp.where(code == -target, 1.0, 0.0)
            parts.append(hit)
        hits = jnp.concatenate(parts, axis=0).astype(bf16)
        found = jnp.dot(hits, integ_ref[...], preferred_element_type=f32)
        high = found.astype(bf16).astype(f32)
        low = found - high
        for m in range(step):
            rows = []
            for cc in range(z.strings):
                at = (m * z.strings + cc) * z.targets
                rows += [high[at : at + z.targets], low[at : at + z.targets]]
            turned = jnp.concatenate(rows, axis=0).T
            tall[pl.ds(n * step + m, z.pair_rows, stride=z.targets), :] = turned[0 : z.pair_rows]
        return carry

    lax.fori_loop(0, z.targets // step, weight_step, 0, unroll=2)

    lane_list = lax.broadcasted_iota(jnp.int32, (z.lists, LANES), 1)

    def compact_step(u, carry):
        first, second = list_ref[2 * u], list_ref[2 * u + 1]
        left_shift = (first % 2) * half_block
        right_shift = (1 - second % 2) * half_block
        left = pltpu.roll(full[first // 2], left_shift, 1)
        right = pltpu.roll(full[second // 2], right_shift, 1)
        left = jnp.where(2 * u < count, left, 0.0)
        right = jnp.where(2 * u + 1 < count, right, 0.0)
        tabf[u] = jnp.where(lane_list < half_block, left, right)
        return carry

    lax.fori_loop(0, z.tiles, compact_step, 0)

    side = 2 * z.targets

    def run(blocks, span):
        depth = (blocks * z.block + span - 1) // span
        tiles = (blocks + 1) // 2
        local = lax.broadcasted_iota(jnp.int32, (span, LANES), 0).astype(f32).astype(bf16)
        nothing = jnp.zeros((span, LANES), bf16)

        def tall_row(few):
            return jnp.concatenate([few.astype(f32).astype(bf16)] * (span // 16), axis=0)

        def chunk_of(spot):
            if span & (span - 1) == 0:
                return lax.shift_right_arithmetic(spot, span.bit_length() - 1)
            return sum((spot >= span * m).astype(jnp.int32) for m in range(1, depth))

        for m in range(depth):
            for k in range(0, span, LANES):
                block = (m * span + k) // z.block
                left, right = tabf[min(block // 2, z.tiles - 1)], jnp.zeros((z.lists, LANES), f32)
                if block % 2:
                    left = pltpu.roll(left, half_block, 1)
                    if block // 2 + 1 < z.tiles:
                        right = pltpu.roll(tabf[block // 2 + 1], half_block, 1)
                    left = jnp.where(lane_list < half_block, left, right)
                table[m * z.lists : (m + 1) * z.lists, k : k + LANES] = left.astype(bf16)

        def one_tile(u, carry, turn=False, half=False):
            columns = z.chunk_pairs // 2 if half else z.chunk_pairs
            acc[...] = jnp.zeros_like(acc)
            held[...] = jnp.zeros_like(held)

            def spread(n):
                if turn:
                    at = pl.multiple_of(n * DEPTH, DEPTH)
                    turned = tall[pl.ds(at, DEPTH), :].T.astype(bf16)
                    weights[n] = turned
                else:
                    turned = weights[n]
                total = jnp.dot(turned, held[...], preferred_element_type=f32)
                for cc in range(z.strings):
                    acc[cc] += total[
                        cc * side : (cc + 1) * side, cc * LANES : (cc + 1) * LANES
                    ]

            def keep(q, value):
                sides = [value]
                if half:
                    left = lane_list < half_block
                    sides = [jnp.where(left, value, 0.0), jnp.where(left, 0.0, value)]
                for one, side_value in enumerate(sides):
                    side_value = side_value.astype(bf16)
                    row = (q * len(sides) + one) * z.targets
                    for cc in range(z.strings):
                        held[row : row + z.targets, cc * LANES : (cc + 1) * LANES] = side_value[
                            cc * z.targets : (cc + 1) * z.targets
                        ]

            def gather(q, spot, sign):
                lanes = spot & (LANES - 1)
                tile = lax.shift_right_arithmetic(spot, LANES.bit_length() - 1)
                hits = [tile == k for k in range(tiles)]
                parts = []
                for row in range(0, z.lists, 8):
                    value = jnp.zeros((8, LANES), f32)
                    for k in range(tiles):
                        taken = jnp.take_along_axis(
                            tabf[k, row : row + 8, :], lanes, axis=1, mode="promise_in_bounds"
                        )
                        value = jnp.where(hits[k], taken, value)
                    parts.append(value * sign)
                keep(q, jnp.concatenate(parts, axis=0))

            def one_chunk(n, inner):
                spread(jnp.maximum(n - 1, 0))
                picks, chunk, chosen = [], [], []
                for q in range(columns):
                    at = pl.ds(n * columns + q, 1)
                    code = jnp.broadcast_to(spot_ref[u, at, :], (16, LANES))
                    spot = jnp.abs(code) - 1
                    sign = jnp.clip(code, -1, 1)
                    if q % GATHERED == GATHERED - 1:
                        gather(q, spot[0:8], sign[0:8].astype(f32))
                        continue
                    chosen.append(q)
                    part = chunk_of(spot)
                    hit = local == tall_row(spot - part * span)
                    picks.append(jnp.where(hit, tall_row(sign), nothing))
                    chunk.append(part[0:8])
                pick = jnp.concatenate(picks, axis=1)
                found = jnp.dot(
                    table[0 : depth * z.lists, 0:span], pick, preferred_element_type=f32
                )
                for k, q in enumerate(chosen):
                    lanes = slice(k * LANES, (k + 1) * LANES)
                    value = found[0 : z.lists, lanes]
                    for m in range(1, depth):
                        other = found[m * z.lists : (m + 1) * z.lists, lanes]
                        here = jnp.concatenate([chunk[k] == m] * (z.lists // 8), axis=0)
                        value = jnp.where(here, other, value)
                    keep(q, value)
                return inner

            lax.fori_loop(0, z.chunks, one_chunk, 0)
            spread(z.chunks - 1)
            for cc in range(z.strings):
                total = acc[cc, 0 : z.targets, :] + acc[cc, z.targets : 2 * z.targets, :]
                if half:
                    total = total + pltpu.roll(total, half_block, 1)
                result[u, pl.ds(cc, z.targets, stride=z.strings), :] = total
            return carry

        whole = count // 2
        last_here = count % 2 == 1
        if z.share == 1:
            one_tile(0, 0, turn=True)
            lax.fori_loop(1, whole, one_tile, 0)
        else:
            part = part_ref[0]
            mine = (whole - part + z.share - 1) // z.share
            lax.fori_loop(0, mine, lambda n, carry: one_tile(n * z.share + part, carry, True), 0)
            last_here = last_here & (whole % z.share == part)

        @pl.when(last_here)
        def _():
            one_tile(whole, 0, turn=z.share > 1, half=True)

    lower = 0
    cases = [(6, 192), (8, WIDE), (9, 192), (10, WIDE), (12, WIDE), (16, WIDE), (z.blocks, WIDE)]
    for blocks, span in cases:
        if lower < blocks <= z.blocks:
            pl.when((count > lower) & (count <= blocks))(functools.partial(run, blocks, span))
            lower = blocks

    wide = z.src * z.strings
    lane_out = lax.broadcasted_iota(jnp.int32, (z.targets * z.strings, LANES), 1)
    for w in range(z.tiles):
        sides = []
        for at_side in range(2):
            rank = rank_ref[2 * w + at_side]
            spot = jnp.maximum(rank, 0)
            shift = ((spot + at_side) % 2) * half_block
            moved = pltpu.roll(result[spot // 2], shift, 1)
            here = rank >= 0
            if z.share > 1:
                here = here & ((spot // 2) % z.share == part_ref[0])
            sides.append(jnp.where(here, moved, 0.0))
        both = jnp.where(lane_out < half_block, sides[0], sides[1])
        for j in range(z.n_beta):
            device = w // z.halves * z.n_beta + j
            out_ref[device, w % z.halves] = both[j * wide : (j + 1) * wide]


def finish_kernel(z, irrep_ref, rx_ref, diag_ref, coef_ref, out_ref):
    wide = z.src * z.strings
    stride = z.share * z.halves * wide

    def column(first):
        rows = [
            rx_ref[pl.ds(part * z.halves * wide + first, z.sets, stride=stride), :]
            for part in range(z.share)
        ]
        return functools.reduce(jnp.add, rows)

    columns = []
    for t in range(z.src):
        for cc in range(z.strings):
            firsts = [h * wide + t * z.strings + cc for h in range(z.halves)]
            columns.append(jnp.concatenate([column(first) for first in firsts], axis=1))
    added = jnp.concatenate(columns, axis=0).T
    total = diag_ref[...] * coef_ref[...].astype(jnp.float32) + added
    for b in range(z.own):
        at = slice(b * z.block, (b + 1) * z.block)
        out_ref[at, :] = jnp.where(irrep_ref[b] == 0, total[at], 0.0)


def on_device(
    coefficients, diagonal, integrals, alpha_row, alpha_sign, beta_block, beta_sign, block_irrep
):
    z = Sizes(coefficients, integrals, alpha_row, beta_sign, block_irrep)
    f32, i32, bf16 = jnp.float32, jnp.int32, jnp.bfloat16
    alpha_rank = lax.axis_index("alpha")
    params = pltpu.CompilerParams(vmem_limit_bytes=32 * 1024 * 1024)

    first = jnp.minimum(alpha_rank, z.senders - 1) * z.per
    own_signs = lax.dynamic_slice_in_dim(beta_sign, first, z.per, 0)
    own_blocks = lax.dynamic_slice_in_dim(beta_block, first, z.per, 0)
    code = own_signs.reshape(z.per, z.pairs, z.block) * (own_blocks + 1)[:, :, None]
    packed = pl.pallas_call(
        functools.partial(pack_kernel, z),
        out_shape=jax.ShapeDtypeStruct((z.devices * z.pack, LANES), bf16),
        in_specs=[VMEM, VMEM],
        out_specs=VMEM,
        scratch_shapes=[pltpu.VMEM((z.devices * z.pack, LANES), f32)],
        compiler_params=params,
    )(coefficients, code.astype(f32))
    arrived = lax.all_to_all(
        packed.reshape(z.devices, z.pack, LANES), ("alpha", "beta"), 0, 0, tiled=True
    ).reshape(z.devices * z.pack, LANES)

    pad = z.pair_lanes - z.pairs
    wide = z.src * z.strings
    part = (alpha_rank * z.n_beta + lax.axis_index("beta")) % z.share
    integ = jnp.pad(integrals, ((0, pad), (0, pad)))
    lists = [pltpu.SMEM((z.blocks,), i32), pltpu.SMEM((z.blocks + 8,), i32)]
    spots = pl.pallas_call(
        functools.partial(index_kernel, z),
        out_shape=jax.ShapeDtypeStruct((z.tiles, z.pair_rows, LANES), i32),
        in_specs=[SMEM, VMEM, VMEM],
        out_specs=VMEM,
        scratch_shapes=lists,
        compiler_params=pltpu.CompilerParams(vmem_limit_bytes=16 * 1024 * 1024),
        cost_estimate=pl.CostEstimate(
            flops=50 * z.pairs * z.all_rows,
            bytes_accessed=12 * z.pairs * z.all_rows,
            transcendentals=0,
        ),
    )(block_irrep, alpha_row, alpha_sign)
    terms = pl.pallas_call(
        functools.partial(main_kernel, z),
        out_shape=jax.ShapeDtypeStruct((z.devices, z.halves, wide, LANES), f32),
        in_specs=[SMEM, SMEM, VMEM, VMEM, VMEM],
        out_specs=VMEM,
        scratch_shapes=[
            pltpu.VMEM((z.devices * z.pack, LANES), f32),
            pltpu.VMEM((z.tiles, z.lists, LANES), f32),
            pltpu.VMEM((z.tiles, z.lists, LANES), f32),
            pltpu.VMEM((round_up(z.all_rows, WIDE) // WIDE * z.lists, WIDE), bf16),
            pltpu.VMEM((z.pair_tiles, z.lists, LANES), f32),
            pltpu.VMEM((z.pair_rows * z.targets, LANES), f32),
            pltpu.VMEM((z.chunks, LANES, DEPTH), bf16),
            pltpu.VMEM((z.strings, 2 * z.targets, LANES), f32),
            pltpu.VMEM((DEPTH, z.strings * LANES), bf16),
            pltpu.VMEM((z.tiles, z.targets * z.strings, LANES), f32),
        ]
        + lists,
        compiler_params=params,
    )(block_irrep, part.astype(i32)[None], arrived, integ, spots)

    back = lax.all_to_all(terms, ("alpha", "beta"), 0, 0, tiled=True).reshape(-1, LANES)
    own_irrep = lax.dynamic_slice_in_dim(block_irrep, alpha_rank * z.own, z.own, 0)
    return pl.pallas_call(
        functools.partial(finish_kernel, z),
        out_shape=jax.ShapeDtypeStruct((z.rows, z.cols), f32),
        in_specs=[SMEM, VMEM, VMEM, VMEM],
        out_specs=VMEM,
        compiler_params=params,
    )(own_irrep, back, diagonal, coefficients)


def solution(mesh):
    return jax.shard_map(
        on_device,
        mesh=mesh,
        in_specs=(
            P("alpha", "beta"),
            P("alpha", "beta"),
            P(),
            P(),
            P(),
            P("beta", None),
            P("beta", None),
            P(),
        ),
        out_specs=P("alpha", "beta"),
        check_vma=False,
    )
```

```python
import functools

import jax
import jax.numpy as jnp
from jax import lax
from jax.experimental import pallas as pl
from jax.experimental.pallas import tpu as pltpu
from jax.sharding import PartitionSpec as P

LANES = 128
DEPTH = 512
WIDE = 256
GATHERED = 4
VMEM = pl.BlockSpec(memory_space=pltpu.VMEM)
SMEM = pl.BlockSpec(memory_space=pltpu.SMEM)


def round_up(size, step):
    return -(-size // step) * step


class Sizes:
    def __init__(self, coefficients, integrals, alpha_row, beta_sign, block_irrep):
        self.n_alpha = lax.axis_size("alpha")
        self.n_beta = lax.axis_size("beta")
        self.devices = self.n_alpha * self.n_beta
        self.rows, self.cols = coefficients.shape
        self.pairs = integrals.shape[0]
        self.block = beta_sign.shape[1] // self.pairs
        self.src = self.cols // self.block
        self.targets = self.n_beta * self.src
        self.all_rows = alpha_row.shape[1]
        self.blocks = block_irrep.shape[0]
        self.own = self.rows // self.block
        self.share = max(1, self.devices // self.block)
        self.sets = self.devices // self.share
        self.strings = self.block // self.sets
        self.halves = self.rows // LANES
        self.tiles = self.all_rows // LANES
        self.per = max(1, self.src // self.n_alpha)
        self.senders = self.src // self.per
        self.group = self.src * self.strings
        self.lists = self.n_beta * self.group
        self.chunk_pairs = DEPTH // self.targets
        self.pair_rows = round_up(self.pairs, self.chunk_pairs)
        self.chunks = self.pair_rows // self.chunk_pairs
        self.whole_chunks = self.pairs // self.chunk_pairs
        self.tail_pairs = round_up(self.pairs % self.chunk_pairs, 2)
        self.pair_lanes = round_up(self.pairs, LANES)
        self.pair_tiles = self.pair_lanes // LANES
        self.coef_rows = self.halves * self.group
        self.sign_rows = self.per * self.strings * self.pair_tiles
        self.pack = round_up(self.coef_rows + self.sign_rows, 8)


def pack_kernel(z, coef_ref, sign_ref, out_ref, scratch):
    scratch[...] = jnp.zeros_like(scratch)
    turned = coef_ref[...].astype(jnp.float32).T
    for half in range(z.halves):
        for g in range(z.group):
            row = half * z.group + g
            for part in range(z.share):
                scratch[pl.ds(row + part * z.pack, z.sets, stride=z.share * z.pack), :] = turned[
                    g * z.sets : (g + 1) * z.sets, half * LANES : (half + 1) * LANES
                ]
    for s in range(z.per):
        code = sign_ref[s].T
        code = jnp.concatenate(
            [code, jnp.zeros((z.block, z.pair_lanes - z.pairs), jnp.float32)], axis=1
        )
        for cc in range(z.strings):
            for k in range(z.pair_tiles):
                row = z.coef_rows + (s * z.strings + cc) * z.pair_tiles + k
                for part in range(z.share):
                    scratch[pl.ds(row + part * z.pack, z.sets, stride=z.share * z.pack), :] = code[
                        cc * z.sets : (cc + 1) * z.sets, k * LANES : (k + 1) * LANES
                    ]
    out_ref[...] = scratch[...].astype(jnp.bfloat16)


def live_blocks(z, irrep_ref, rank_ref, list_ref):
    count = jnp.int32(0)
    lane_row = lax.broadcasted_iota(jnp.int32, (1, LANES), 1)
    ranks = jnp.full((1, LANES), -1, jnp.int32)
    for extra in range(z.blocks + 8):
        list_ref[extra] = 0
    for g in range(z.blocks):
        live = irrep_ref[g] == 0
        rank = jnp.where(live, count, -1)
        rank_ref[g] = rank
        list_ref[count] = g
        ranks = jnp.where(lane_row == g, rank, ranks)
        count = count + live.astype(jnp.int32)
    for extra in range(4):
        list_ref[count + extra] = 0
    return count, ranks


def index_kernel(z, irrep_ref, row_ref, sign_ref, out_ref, rank_ref, list_ref):
    count, ranks = live_blocks(z, irrep_ref, rank_ref, list_ref)
    lane_pair = lax.broadcasted_iota(jnp.int32, (z.pairs, LANES), 1)
    tail = z.pairs // 8 * 8

    def compact_step(u, carry):
        first, second = list_ref[2 * u], list_ref[2 * u + 1]
        left_shift = (first % 2) * z.block
        right_shift = (1 - second % 2) * z.block

        def merged(ref):
            at_first = pl.ds(pl.multiple_of(first // 2 * LANES, LANES), LANES)
            at_second = pl.ds(pl.multiple_of(second // 2 * LANES, LANES), LANES)
            return jnp.where(
                lane_pair < z.block,
                pltpu.roll(ref[:, at_first], left_shift, 1),
                pltpu.roll(ref[:, at_second], right_shift, 1),
            )

        source = merged(row_ref)
        signs = merged(sign_ref)
        block = source // z.block
        rank = jnp.take_along_axis(
            jnp.broadcast_to(ranks, (z.pairs, LANES)), block, axis=1, mode="promise_in_bounds"
        )
        spot = rank * z.block + (source & (z.block - 1))
        inside = (lane_pair < z.block) | (2 * u + 1 < count)
        out_ref[u, tail : z.pair_rows, :] = jnp.zeros((z.pair_rows - tail, LANES), jnp.int32)
        out_ref[u, 0 : z.pairs, :] = jnp.where((rank >= 0) & inside, signs * (spot + 1), 0)
        return carry

    lax.fori_loop(0, (count + 1) // 2, compact_step, 0)

    @pl.when(count % 2 == 1)
    def _():
        u = count // 2
        half = z.pair_rows // 2
        even = out_ref[u, pl.ds(0, half, stride=2), :]
        odd = out_ref[u, pl.ds(1, half, stride=2), :]
        out_ref[u, 0:half, :] = even + pltpu.roll(odd, z.block, 1)


def main_kernel(
    z,
    irrep_ref,
    part_ref,
    rx_ref,
    integ_ref,
    spot_ref,
    out_ref,
    rxf,
    full,
    tabf,
    table,
    codes,
    tall,
    weights,
    acc,
    held,
    result,
    rank_ref,
    list_ref,
):
    f32, bf16 = jnp.float32, jnp.bfloat16
    half_block = z.block
    count, _ = live_blocks(z, irrep_ref, rank_ref, list_ref)
    n_tiles = (count + 1) // 2

    rxf[...] = rx_ref[...].astype(f32)
    for i in range(z.n_alpha):
        base = i * z.n_beta * z.pack
        for half in range(z.halves):
            for s in range(z.src):
                for cc in range(z.strings):
                    source = base + half * z.group + s * z.strings + cc
                    dest = cc * z.targets + s
                    full[i * z.halves + half, pl.ds(dest, z.n_beta, stride=z.src), :] = rxf[
                        pl.ds(source, z.n_beta, stride=z.pack), :
                    ]
        for s in range(z.per if i < z.senders else 0):
            for cc in range(z.strings):
                for k in range(z.pair_tiles):
                    source = base + z.coef_rows + (s * z.strings + cc) * z.pair_tiles + k
                    dest = (i * z.per + s) * z.strings + cc
                    codes[k, pl.ds(dest, z.n_beta, stride=z.group), :] = rxf[
                        pl.ds(source, z.n_beta, stride=z.pack), :
                    ]

    step = 4
    target = (lax.broadcasted_iota(jnp.int32, (z.targets, z.pair_lanes), 0) + 1).astype(f32)

    def weight_step(n, carry):
        parts = []
        for m in range(step * z.strings):
            code = jnp.concatenate(
                [codes[k, pl.ds(n * step * z.strings + m, 1), :] for k in range(z.pair_tiles)],
                axis=1,
            )
            hit = jnp.where(code == target, 1.0, 0.0) - jnp.where(code == -target, 1.0, 0.0)
            parts.append(hit)
        hits = jnp.concatenate(parts, axis=0).astype(bf16)
        found = jnp.dot(hits, integ_ref[...], preferred_element_type=f32)
        high = found.astype(bf16).astype(f32)
        low = found - high
        for m in range(step):
            rows = []
            for cc in range(z.strings):
                at = (m * z.strings + cc) * z.targets
                rows += [high[at : at + z.targets], low[at : at + z.targets]]
            turned = jnp.concatenate(rows, axis=0).T
            tall[pl.ds(n * step + m, z.pair_rows, stride=z.targets), :] = turned[0 : z.pair_rows]
        return carry

    lax.fori_loop(0, z.targets // step, weight_step, 0, unroll=min(8, z.targets // step))

    lane_list = lax.broadcasted_iota(jnp.int32, (z.lists, LANES), 1)

    def compact_step(u, carry):
        first, second = list_ref[2 * u], list_ref[2 * u + 1]
        left_shift = (first % 2) * half_block
        right_shift = (1 - second % 2) * half_block
        left = pltpu.roll(full[first // 2], left_shift, 1)
        right = pltpu.roll(full[second // 2], right_shift, 1)
        left = jnp.where(2 * u < count, left, 0.0)
        right = jnp.where(2 * u + 1 < count, right, 0.0)
        tabf[u] = jnp.where(lane_list < half_block, left, right)
        return carry

    lax.fori_loop(0, z.tiles, compact_step, 0)

    side = 2 * z.targets

    def run(blocks, span):
        depth = (blocks * z.block + span - 1) // span
        tiles = (blocks + 1) // 2
        local = lax.broadcasted_iota(jnp.int32, (span, LANES), 0).astype(f32).astype(bf16)
        nothing = jnp.zeros((span, LANES), bf16)

        def tall_row(few):
            return jnp.concatenate([few.astype(f32).astype(bf16)] * (span // 16), axis=0)

        def chunk_of(spot):
            if span & (span - 1) == 0:
                return lax.shift_right_arithmetic(spot, span.bit_length() - 1)
            return sum((spot >= span * m).astype(jnp.int32) for m in range(1, depth))

        for m in range(depth):
            for k in range(0, span, LANES):
                block = (m * span + k) // z.block
                left, right = tabf[min(block // 2, z.tiles - 1)], jnp.zeros((z.lists, LANES), f32)
                if block % 2:
                    left = pltpu.roll(left, half_block, 1)
                    if block // 2 + 1 < z.tiles:
                        right = pltpu.roll(tabf[block // 2 + 1], half_block, 1)
                    left = jnp.where(lane_list < half_block, left, right)
                table[m * z.lists : (m + 1) * z.lists, k : k + LANES] = left.astype(bf16)

        def one_tile(u, carry, turn=False, half=False):
            acc[...] = jnp.zeros_like(acc)
            held[...] = jnp.zeros_like(held)

            def spread(n, rows=DEPTH):
                if turn:
                    at = pl.multiple_of(n * DEPTH, DEPTH)
                    turned = tall[pl.ds(at, DEPTH), :].T.astype(bf16)
                    weights[n] = turned
                else:
                    turned = weights[n]
                total = jnp.dot(
                    turned[:, 0:rows], held[0:rows, :], preferred_element_type=f32
                )
                for cc in range(z.strings):
                    acc[cc] += total[
                        cc * side : (cc + 1) * side, cc * LANES : (cc + 1) * LANES
                    ]

            def keep(q, value):
                sides = [value]
                if half:
                    left = lane_list < half_block
                    sides = [jnp.where(left, value, 0.0), jnp.where(left, 0.0, value)]
                for one, side_value in enumerate(sides):
                    side_value = side_value.astype(bf16)
                    row = (q * len(sides) + one) * z.targets
                    for cc in range(z.strings):
                        held[row : row + z.targets, cc * LANES : (cc + 1) * LANES] = side_value[
                            cc * z.targets : (cc + 1) * z.targets
                        ]

            def gather(q, spot, sign):
                lanes = spot & (LANES - 1)
                tile = lax.shift_right_arithmetic(spot, LANES.bit_length() - 1)
                hits = [tile == k for k in range(tiles)]
                parts = []
                for row in range(0, z.lists, 8):
                    value = jnp.zeros((8, LANES), f32)
                    for k in range(tiles):
                        taken = jnp.take_along_axis(
                            tabf[k, row : row + 8, :], lanes, axis=1, mode="promise_in_bounds"
                        )
                        value = jnp.where(hits[k], taken, value)
                    parts.append(value * sign)
                keep(q, jnp.concatenate(parts, axis=0))

            def one_chunk(n, inner, pairs=z.chunk_pairs):
                spread(jnp.maximum(n - 1, 0))
                columns = pairs // 2 if half else pairs
                short = pairs < z.chunk_pairs
                first = n * (z.chunk_pairs // 2 if half else z.chunk_pairs)
                picks, chunk, chosen = [], [], []
                for q in range(columns):
                    at = pl.ds(first + q, 1)
                    code = jnp.broadcast_to(spot_ref[u, at, :], (16, LANES))
                    spot = jnp.abs(code) - 1
                    sign = jnp.clip(code, -1, 1)
                    if q % GATHERED == GATHERED - 1 and not short:
                        gather(q, spot[0:8], sign[0:8].astype(f32))
                        continue
                    chosen.append(q)
                    part = chunk_of(spot)
                    hit = local == tall_row(spot - part * span)
                    picks.append(jnp.where(hit, tall_row(sign), nothing))
                    chunk.append(part[0:8])
                pick = jnp.concatenate(picks, axis=1)
                found = jnp.dot(
                    table[0 : depth * z.lists, 0:span], pick, preferred_element_type=f32
                )
                for k, q in enumerate(chosen):
                    lanes = slice(k * LANES, (k + 1) * LANES)
                    value = found[0 : z.lists, lanes]
                    for m in range(1, depth):
                        other = found[m * z.lists : (m + 1) * z.lists, lanes]
                        here = jnp.concatenate([chunk[k] == m] * (z.lists // 8), axis=0)
                        value = jnp.where(here, other, value)
                    keep(q, value)
                return inner

            lax.fori_loop(0, z.whole_chunks, one_chunk, 0)
            if z.tail_pairs:
                one_chunk(z.whole_chunks, 0, z.tail_pairs)
                spread(z.whole_chunks, z.tail_pairs * z.targets)
            else:
                spread(z.whole_chunks - 1)
            for cc in range(z.strings):
                total = acc[cc, 0 : z.targets, :] + acc[cc, z.targets : 2 * z.targets, :]
                if half:
                    total = total + pltpu.roll(total, half_block, 1)
                result[u, pl.ds(cc, z.targets, stride=z.strings), :] = total
            return carry

        whole = count // 2
        last_here = count % 2 == 1
        if z.share == 1:
            one_tile(0, 0, turn=True)
            lax.fori_loop(1, whole, one_tile, 0)
        else:
            part = part_ref[0]
            mine = (whole - part + z.share - 1) // z.share
            lax.fori_loop(0, mine, lambda n, carry: one_tile(n * z.share + part, carry, True), 0)
            last_here = last_here & (whole % z.share == part)

        @pl.when(last_here)
        def _():
            one_tile(whole, 0, turn=z.share > 1, half=True)

    lower = 0
    cases = [(6, 192), (8, WIDE), (9, 192), (10, WIDE), (12, WIDE), (16, WIDE), (z.blocks, WIDE)]
    for blocks, span in cases:
        if lower < blocks <= z.blocks:
            pl.when((count > lower) & (count <= blocks))(functools.partial(run, blocks, span))
            lower = blocks

    wide = z.src * z.strings
    lane_out = lax.broadcasted_iota(jnp.int32, (z.targets * z.strings, LANES), 1)
    for w in range(z.tiles):
        sides = []
        for at_side in range(2):
            rank = rank_ref[2 * w + at_side]
            spot = jnp.maximum(rank, 0)
            shift = ((spot + at_side) % 2) * half_block
            moved = pltpu.roll(result[spot // 2], shift, 1)
            here = rank >= 0
            if z.share > 1:
                here = here & ((spot // 2) % z.share == part_ref[0])
            sides.append(jnp.where(here, moved, 0.0))
        both = jnp.where(lane_out < half_block, sides[0], sides[1])
        for j in range(z.n_beta):
            device = w // z.halves * z.n_beta + j
            out_ref[device, w % z.halves] = both[j * wide : (j + 1) * wide]


def finish_kernel(z, irrep_ref, rx_ref, diag_ref, coef_ref, out_ref):
    wide = z.src * z.strings
    stride = z.share * z.halves * wide

    def column(first):
        rows = [
            rx_ref[pl.ds(part * z.halves * wide + first, z.sets, stride=stride), :]
            for part in range(z.share)
        ]
        return functools.reduce(jnp.add, rows)

    columns = []
    for t in range(z.src):
        for cc in range(z.strings):
            firsts = [h * wide + t * z.strings + cc for h in range(z.halves)]
            columns.append(jnp.concatenate([column(first) for first in firsts], axis=1))
    added = jnp.concatenate(columns, axis=0).T
    total = diag_ref[...] * coef_ref[...].astype(jnp.float32) + added
    for b in range(z.own):
        at = slice(b * z.block, (b + 1) * z.block)
        out_ref[at, :] = jnp.where(irrep_ref[b] == 0, total[at], 0.0)


def on_device(
    coefficients, diagonal, integrals, alpha_row, alpha_sign, beta_block, beta_sign, block_irrep
):
    z = Sizes(coefficients, integrals, alpha_row, beta_sign, block_irrep)
    f32, i32, bf16 = jnp.float32, jnp.int32, jnp.bfloat16
    alpha_rank = lax.axis_index("alpha")
    params = pltpu.CompilerParams(vmem_limit_bytes=32 * 1024 * 1024)

    first = jnp.minimum(alpha_rank, z.senders - 1) * z.per
    own_signs = lax.dynamic_slice_in_dim(beta_sign, first, z.per, 0)
    own_blocks = lax.dynamic_slice_in_dim(beta_block, first, z.per, 0)
    code = own_signs.reshape(z.per, z.pairs, z.block) * (own_blocks + 1)[:, :, None]
    packed = pl.pallas_call(
        functools.partial(pack_kernel, z),
        out_shape=jax.ShapeDtypeStruct((z.devices * z.pack, LANES), bf16),
        in_specs=[VMEM, VMEM],
        out_specs=VMEM,
        scratch_shapes=[pltpu.VMEM((z.devices * z.pack, LANES), f32)],
        compiler_params=params,
    )(coefficients, code.astype(f32))
    arrived = lax.all_to_all(
        packed.reshape(z.devices, z.pack, LANES), ("alpha", "beta"), 0, 0, tiled=True
    ).reshape(z.devices * z.pack, LANES)

    pad = z.pair_lanes - z.pairs
    wide = z.src * z.strings
    part = (alpha_rank * z.n_beta + lax.axis_index("beta")) % z.share
    integ = jnp.pad(integrals, ((0, pad), (0, pad)))
    lists = [pltpu.SMEM((z.blocks,), i32), pltpu.SMEM((z.blocks + 8,), i32)]
    spots = pl.pallas_call(
        functools.partial(index_kernel, z),
        out_shape=jax.ShapeDtypeStruct((z.tiles, z.pair_rows, LANES), i32),
        in_specs=[SMEM, VMEM, VMEM],
        out_specs=VMEM,
        scratch_shapes=lists,
        compiler_params=pltpu.CompilerParams(vmem_limit_bytes=16 * 1024 * 1024),
        cost_estimate=pl.CostEstimate(
            flops=50 * z.pairs * z.all_rows,
            bytes_accessed=12 * z.pairs * z.all_rows,
            transcendentals=0,
        ),
    )(block_irrep, alpha_row, alpha_sign)
    terms = pl.pallas_call(
        functools.partial(main_kernel, z),
        out_shape=jax.ShapeDtypeStruct((z.devices, z.halves, wide, LANES), f32),
        in_specs=[SMEM, SMEM, VMEM, VMEM, VMEM],
        out_specs=VMEM,
        scratch_shapes=[
            pltpu.VMEM((z.devices * z.pack, LANES), f32),
            pltpu.VMEM((z.tiles, z.lists, LANES), f32),
            pltpu.VMEM((z.tiles, z.lists, LANES), f32),
            pltpu.VMEM((round_up(z.all_rows, WIDE) // WIDE * z.lists, WIDE), bf16),
            pltpu.VMEM((z.pair_tiles, z.lists, LANES), f32),
            pltpu.VMEM((z.pair_rows * z.targets, LANES), f32),
            pltpu.VMEM((z.chunks, LANES, DEPTH), bf16),
            pltpu.VMEM((z.strings, 2 * z.targets, LANES), f32),
            pltpu.VMEM((DEPTH, z.strings * LANES), bf16),
            pltpu.VMEM((z.tiles, z.targets * z.strings, LANES), f32),
        ]
        + lists,
        compiler_params=params,
    )(block_irrep, part.astype(i32)[None], arrived, integ, spots)

    back = lax.all_to_all(terms, ("alpha", "beta"), 0, 0, tiled=True).reshape(-1, LANES)
    own_irrep = lax.dynamic_slice_in_dim(block_irrep, alpha_rank * z.own, z.own, 0)
    return pl.pallas_call(
        functools.partial(finish_kernel, z),
        out_shape=jax.ShapeDtypeStruct((z.rows, z.cols), f32),
        in_specs=[SMEM, VMEM, VMEM, VMEM],
        out_specs=VMEM,
        compiler_params=params,
    )(own_irrep, back, diagonal, coefficients)


def solution(mesh):
    return jax.shard_map(
        on_device,
        mesh=mesh,
        in_specs=(
            P("alpha", "beta"),
            P("alpha", "beta"),
            P(),
            P(),
            P(),
            P("beta", None),
            P("beta", None),
            P(),
        ),
        out_specs=P("alpha", "beta"),
        check_vma=False,
    )
```

```python
import functools

import jax
import jax.numpy as jnp
from jax import lax
from jax.experimental import pallas as pl
from jax.experimental.pallas import tpu as pltpu
from jax.sharding import PartitionSpec as P

LANES = 128
DEPTH = 1024
WIDE = 256
GATHERED = 4
VMEM = pl.BlockSpec(memory_space=pltpu.VMEM)
SMEM = pl.BlockSpec(memory_space=pltpu.SMEM)


def round_up(size, step):
    return -(-size // step) * step


class Sizes:
    def __init__(self, coefficients, integrals, alpha_row, beta_sign, block_irrep):
        self.n_alpha = lax.axis_size("alpha")
        self.n_beta = lax.axis_size("beta")
        self.devices = self.n_alpha * self.n_beta
        self.rows, self.cols = coefficients.shape
        self.pairs = integrals.shape[0]
        self.block = beta_sign.shape[1] // self.pairs
        self.src = self.cols // self.block
        self.targets = self.n_beta * self.src
        self.all_rows = alpha_row.shape[1]
        self.blocks = block_irrep.shape[0]
        self.own = self.rows // self.block
        self.share = max(1, self.devices // self.block)
        self.sets = self.devices // self.share
        self.strings = self.block // self.sets
        self.halves = self.rows // LANES
        self.tiles = self.all_rows // LANES
        self.per = max(1, self.src // self.n_alpha)
        self.senders = self.src // self.per
        self.group = self.src * self.strings
        self.lists = self.n_beta * self.group
        self.chunk_pairs = DEPTH // self.targets
        self.pair_rows = round_up(self.pairs, self.chunk_pairs)
        self.chunks = self.pair_rows // self.chunk_pairs
        self.whole_chunks = self.pairs // self.chunk_pairs
        self.tail_pairs = round_up(self.pairs % self.chunk_pairs, 2)
        self.pair_lanes = round_up(self.pairs, LANES)
        self.pair_tiles = self.pair_lanes // LANES
        self.coef_rows = self.halves * self.group
        self.sign_rows = self.per * self.strings * self.pair_tiles
        self.pack = round_up(self.coef_rows + self.sign_rows, 8)


def pack_kernel(z, coef_ref, sign_ref, out_ref, scratch):
    scratch[...] = jnp.zeros_like(scratch)
    turned = coef_ref[...].astype(jnp.float32).T
    for half in range(z.halves):
        for g in range(z.group):
            row = half * z.group + g
            for part in range(z.share):
                scratch[pl.ds(row + part * z.pack, z.sets, stride=z.share * z.pack), :] = turned[
                    g * z.sets : (g + 1) * z.sets, half * LANES : (half + 1) * LANES
                ]
    for s in range(z.per):
        code = sign_ref[s].T
        code = jnp.concatenate(
            [code, jnp.zeros((z.block, z.pair_lanes - z.pairs), jnp.float32)], axis=1
        )
        for cc in range(z.strings):
            for k in range(z.pair_tiles):
                row = z.coef_rows + (s * z.strings + cc) * z.pair_tiles + k
                for part in range(z.share):
                    scratch[pl.ds(row + part * z.pack, z.sets, stride=z.share * z.pack), :] = code[
                        cc * z.sets : (cc + 1) * z.sets, k * LANES : (k + 1) * LANES
                    ]
    out_ref[...] = scratch[...].astype(jnp.bfloat16)


def live_blocks(z, irrep_ref, rank_ref, list_ref):
    count = jnp.int32(0)
    lane_row = lax.broadcasted_iota(jnp.int32, (1, LANES), 1)
    ranks = jnp.full((1, LANES), -1, jnp.int32)
    for extra in range(z.blocks + 8):
        list_ref[extra] = 0
    for g in range(z.blocks):
        live = irrep_ref[g] == 0
        rank = jnp.where(live, count, -1)
        rank_ref[g] = rank
        list_ref[count] = g
        ranks = jnp.where(lane_row == g, rank, ranks)
        count = count + live.astype(jnp.int32)
    for extra in range(4):
        list_ref[count + extra] = 0
    return count, ranks


def index_kernel(z, irrep_ref, row_ref, sign_ref, out_ref, rank_ref, list_ref):
    count, ranks = live_blocks(z, irrep_ref, rank_ref, list_ref)
    lane_pair = lax.broadcasted_iota(jnp.int32, (z.pairs, LANES), 1)
    tail = z.pairs // 8 * 8

    def compact_step(u, carry):
        first, second = list_ref[2 * u], list_ref[2 * u + 1]
        left_shift = (first % 2) * z.block
        right_shift = (1 - second % 2) * z.block

        def merged(ref):
            at_first = pl.ds(pl.multiple_of(first // 2 * LANES, LANES), LANES)
            at_second = pl.ds(pl.multiple_of(second // 2 * LANES, LANES), LANES)
            return jnp.where(
                lane_pair < z.block,
                pltpu.roll(ref[:, at_first], left_shift, 1),
                pltpu.roll(ref[:, at_second], right_shift, 1),
            )

        source = merged(row_ref)
        signs = merged(sign_ref)
        block = source // z.block
        rank = jnp.take_along_axis(
            jnp.broadcast_to(ranks, (z.pairs, LANES)), block, axis=1, mode="promise_in_bounds"
        )
        spot = rank * z.block + (source & (z.block - 1))
        inside = (lane_pair < z.block) | (2 * u + 1 < count)
        out_ref[u, tail : z.pair_rows, :] = jnp.zeros((z.pair_rows - tail, LANES), jnp.int32)
        out_ref[u, 0 : z.pairs, :] = jnp.where((rank >= 0) & inside, signs * (spot + 1), 0)
        return carry

    lax.fori_loop(0, (count + 1) // 2, compact_step, 0)

    @pl.when(count % 2 == 1)
    def _():
        u = count // 2
        half = z.pair_rows // 2
        even = out_ref[u, pl.ds(0, half, stride=2), :]
        odd = out_ref[u, pl.ds(1, half, stride=2), :]
        out_ref[u, 0:half, :] = even + pltpu.roll(odd, z.block, 1)


def main_kernel(
    z,
    irrep_ref,
    part_ref,
    rx_ref,
    integ_ref,
    spot_ref,
    out_ref,
    rxf,
    full,
    tabf,
    table,
    codes,
    tall,
    weights,
    acc,
    held,
    result,
    rank_ref,
    list_ref,
):
    f32, bf16 = jnp.float32, jnp.bfloat16
    half_block = z.block
    count, _ = live_blocks(z, irrep_ref, rank_ref, list_ref)
    n_tiles = (count + 1) // 2

    rxf[...] = rx_ref[...].astype(f32)
    for i in range(z.n_alpha):
        base = i * z.n_beta * z.pack
        for half in range(z.halves):
            for s in range(z.src):
                for cc in range(z.strings):
                    source = base + half * z.group + s * z.strings + cc
                    dest = cc * z.targets + s
                    full[i * z.halves + half, pl.ds(dest, z.n_beta, stride=z.src), :] = rxf[
                        pl.ds(source, z.n_beta, stride=z.pack), :
                    ]
        for s in range(z.per if i < z.senders else 0):
            for cc in range(z.strings):
                for k in range(z.pair_tiles):
                    source = base + z.coef_rows + (s * z.strings + cc) * z.pair_tiles + k
                    dest = (i * z.per + s) * z.strings + cc
                    codes[k, pl.ds(dest, z.n_beta, stride=z.group), :] = rxf[
                        pl.ds(source, z.n_beta, stride=z.pack), :
                    ]

    step = 4
    target = (lax.broadcasted_iota(jnp.int32, (z.targets, z.pair_lanes), 0) + 1).astype(f32)

    def weight_step(n, carry):
        parts = []
        for m in range(step * z.strings):
            code = jnp.concatenate(
                [codes[k, pl.ds(n * step * z.strings + m, 1), :] for k in range(z.pair_tiles)],
                axis=1,
            )
            hit = jnp.where(code == target, 1.0, 0.0) - jnp.where(code == -target, 1.0, 0.0)
            parts.append(hit)
        hits = jnp.concatenate(parts, axis=0).astype(bf16)
        found = jnp.dot(hits, integ_ref[...], preferred_element_type=f32)
        high = found.astype(bf16).astype(f32)
        low = found - high
        for m in range(step):
            rows = []
            for cc in range(z.strings):
                at = (m * z.strings + cc) * z.targets
                rows += [high[at : at + z.targets], low[at : at + z.targets]]
            turned = jnp.concatenate(rows, axis=0).T
            tall[pl.ds(n * step + m, z.pair_rows, stride=z.targets), :] = turned[0 : z.pair_rows]
        return carry

    lax.fori_loop(0, z.targets // step, weight_step, 0, unroll=min(8, z.targets // step))

    lane_list = lax.broadcasted_iota(jnp.int32, (z.lists, LANES), 1)

    def compact_step(u, carry):
        first, second = list_ref[2 * u], list_ref[2 * u + 1]
        left_shift = (first % 2) * half_block
        right_shift = (1 - second % 2) * half_block
        left = pltpu.roll(full[first // 2], left_shift, 1)
        right = pltpu.roll(full[second // 2], right_shift, 1)
        left = jnp.where(2 * u < count, left, 0.0)
        right = jnp.where(2 * u + 1 < count, right, 0.0)
        tabf[u] = jnp.where(lane_list < half_block, left, right)
        return carry

    lax.fori_loop(0, z.tiles, compact_step, 0)

    side = 2 * z.targets

    def run(blocks, span):
        depth = (blocks * z.block + span - 1) // span
        tiles = (blocks + 1) // 2
        local = lax.broadcasted_iota(jnp.int32, (span, LANES), 0).astype(f32).astype(bf16)
        nothing = jnp.zeros((span, LANES), bf16)

        def tall_row(few):
            return jnp.concatenate([few.astype(f32).astype(bf16)] * (span // 16), axis=0)

        def chunk_of(spot):
            if span & (span - 1) == 0:
                return lax.shift_right_arithmetic(spot, span.bit_length() - 1)
            return sum((spot >= span * m).astype(jnp.int32) for m in range(1, depth))

        for m in range(depth):
            for k in range(0, span, LANES):
                block = (m * span + k) // z.block
                left, right = tabf[min(block // 2, z.tiles - 1)], jnp.zeros((z.lists, LANES), f32)
                if block % 2:
                    left = pltpu.roll(left, half_block, 1)
                    if block // 2 + 1 < z.tiles:
                        right = pltpu.roll(tabf[block // 2 + 1], half_block, 1)
                    left = jnp.where(lane_list < half_block, left, right)
                table[m * z.lists : (m + 1) * z.lists, k : k + LANES] = left.astype(bf16)

        def one_tile(u, carry, turn=False, half=False):
            acc[...] = jnp.zeros_like(acc)
            held[...] = jnp.zeros_like(held)

            def spread(n, rows=DEPTH):
                if turn:
                    at = pl.multiple_of(n * DEPTH, DEPTH)
                    turned = tall[pl.ds(at, DEPTH), :].T.astype(bf16)
                    weights[n] = turned
                else:
                    turned = weights[n]
                total = jnp.dot(
                    turned[:, 0:rows], held[0:rows, :], preferred_element_type=f32
                )
                for cc in range(z.strings):
                    acc[cc] += total[
                        cc * side : (cc + 1) * side, cc * LANES : (cc + 1) * LANES
                    ]

            def keep(q, value):
                sides = [value]
                if half:
                    left = lane_list < half_block
                    sides = [jnp.where(left, value, 0.0), jnp.where(left, 0.0, value)]
                for one, side_value in enumerate(sides):
                    side_value = side_value.astype(bf16)
                    row = (q * len(sides) + one) * z.targets
                    for cc in range(z.strings):
                        held[row : row + z.targets, cc * LANES : (cc + 1) * LANES] = side_value[
                            cc * z.targets : (cc + 1) * z.targets
                        ]

            def gather(q, spot, sign):
                lanes = spot & (LANES - 1)
                tile = lax.shift_right_arithmetic(spot, LANES.bit_length() - 1)
                hits = [tile == k for k in range(tiles)]
                parts = []
                for row in range(0, z.lists, 8):
                    value = jnp.zeros((8, LANES), f32)
                    for k in range(tiles):
                        taken = jnp.take_along_axis(
                            tabf[k, row : row + 8, :], lanes, axis=1, mode="promise_in_bounds"
                        )
                        value = jnp.where(hits[k], taken, value)
                    parts.append(value * sign)
                keep(q, jnp.concatenate(parts, axis=0))

            def one_chunk(n, inner, pairs=z.chunk_pairs):
                spread(jnp.maximum(n - 1, 0))
                columns = pairs // 2 if half else pairs
                short = pairs < z.chunk_pairs
                first = n * (z.chunk_pairs // 2 if half else z.chunk_pairs)
                picks, chunk, chosen = [], [], []
                for q in range(columns):
                    at = pl.ds(first + q, 1)
                    code = jnp.broadcast_to(spot_ref[u, at, :], (16, LANES))
                    spot = jnp.abs(code) - 1
                    sign = jnp.clip(code, -1, 1)
                    if q % GATHERED == GATHERED - 1 and not short:
                        gather(q, spot[0:8], sign[0:8].astype(f32))
                        continue
                    chosen.append(q)
                    part = chunk_of(spot)
                    hit = local == tall_row(spot - part * span)
                    picks.append(jnp.where(hit, tall_row(sign), nothing))
                    chunk.append(part[0:8])
                pick = jnp.concatenate(picks, axis=1)
                found = jnp.dot(
                    table[0 : depth * z.lists, 0:span], pick, preferred_element_type=f32
                )
                for k, q in enumerate(chosen):
                    lanes = slice(k * LANES, (k + 1) * LANES)
                    value = found[0 : z.lists, lanes]
                    for m in range(1, depth):
                        other = found[m * z.lists : (m + 1) * z.lists, lanes]
                        here = jnp.concatenate([chunk[k] == m] * (z.lists // 8), axis=0)
                        value = jnp.where(here, other, value)
                    keep(q, value)
                return inner

            lax.fori_loop(0, z.whole_chunks, one_chunk, 0)
            if z.tail_pairs:
                one_chunk(z.whole_chunks, 0, z.tail_pairs)
                spread(z.whole_chunks, z.tail_pairs * z.targets)
            else:
                spread(z.whole_chunks - 1)
            for cc in range(z.strings):
                total = acc[cc, 0 : z.targets, :] + acc[cc, z.targets : 2 * z.targets, :]
                if half:
                    total = total + pltpu.roll(total, half_block, 1)
                result[u, pl.ds(cc, z.targets, stride=z.strings), :] = total
            return carry

        whole = count // 2
        last_here = count % 2 == 1
        if z.share == 1:
            one_tile(0, 0, turn=True)
            lax.fori_loop(1, whole, one_tile, 0)
        else:
            part = part_ref[0]
            mine = (whole - part + z.share - 1) // z.share
            lax.fori_loop(0, mine, lambda n, carry: one_tile(n * z.share + part, carry, True), 0)
            last_here = last_here & (whole % z.share == part)

        @pl.when(last_here)
        def _():
            one_tile(whole, 0, turn=z.share > 1, half=True)

    lower = 0
    cases = [(6, 192), (8, WIDE), (9, 192), (10, WIDE), (12, WIDE), (16, WIDE), (z.blocks, WIDE)]
    for blocks, span in cases:
        if lower < blocks <= z.blocks:
            pl.when((count > lower) & (count <= blocks))(functools.partial(run, blocks, span))
            lower = blocks

    wide = z.src * z.strings
    lane_out = lax.broadcasted_iota(jnp.int32, (z.targets * z.strings, LANES), 1)
    for w in range(z.tiles):
        sides = []
        for at_side in range(2):
            rank = rank_ref[2 * w + at_side]
            spot = jnp.maximum(rank, 0)
            shift = ((spot + at_side) % 2) * half_block
            moved = pltpu.roll(result[spot // 2], shift, 1)
            here = rank >= 0
            if z.share > 1:
                here = here & ((spot // 2) % z.share == part_ref[0])
            sides.append(jnp.where(here, moved, 0.0))
        both = jnp.where(lane_out < half_block, sides[0], sides[1])
        for j in range(z.n_beta):
            device = w // z.halves * z.n_beta + j
            out_ref[device, w % z.halves] = both[j * wide : (j + 1) * wide]


def finish_kernel(z, irrep_ref, rx_ref, diag_ref, coef_ref, out_ref):
    wide = z.src * z.strings
    stride = z.share * z.halves * wide

    def column(first):
        rows = [
            rx_ref[pl.ds(part * z.halves * wide + first, z.sets, stride=stride), :]
            for part in range(z.share)
        ]
        return functools.reduce(jnp.add, rows)

    columns = []
    for t in range(z.src):
        for cc in range(z.strings):
            firsts = [h * wide + t * z.strings + cc for h in range(z.halves)]
            columns.append(jnp.concatenate([column(first) for first in firsts], axis=1))
    added = jnp.concatenate(columns, axis=0).T
    total = diag_ref[...] * coef_ref[...].astype(jnp.float32) + added
    for b in range(z.own):
        at = slice(b * z.block, (b + 1) * z.block)
        out_ref[at, :] = jnp.where(irrep_ref[b] == 0, total[at], 0.0)


def on_device(
    coefficients, diagonal, integrals, alpha_row, alpha_sign, beta_block, beta_sign, block_irrep
):
    z = Sizes(coefficients, integrals, alpha_row, beta_sign, block_irrep)
    f32, i32, bf16 = jnp.float32, jnp.int32, jnp.bfloat16
    alpha_rank = lax.axis_index("alpha")
    params = pltpu.CompilerParams(vmem_limit_bytes=32 * 1024 * 1024)

    first = jnp.minimum(alpha_rank, z.senders - 1) * z.per
    own_signs = lax.dynamic_slice_in_dim(beta_sign, first, z.per, 0)
    own_blocks = lax.dynamic_slice_in_dim(beta_block, first, z.per, 0)
    code = own_signs.reshape(z.per, z.pairs, z.block) * (own_blocks + 1)[:, :, None]
    packed = pl.pallas_call(
        functools.partial(pack_kernel, z),
        out_shape=jax.ShapeDtypeStruct((z.devices * z.pack, LANES), bf16),
        in_specs=[VMEM, VMEM],
        out_specs=VMEM,
        scratch_shapes=[pltpu.VMEM((z.devices * z.pack, LANES), f32)],
        compiler_params=params,
    )(coefficients, code.astype(f32))
    arrived = lax.all_to_all(
        packed.reshape(z.devices, z.pack, LANES), ("alpha", "beta"), 0, 0, tiled=True
    ).reshape(z.devices * z.pack, LANES)

    pad = z.pair_lanes - z.pairs
    wide = z.src * z.strings
    part = (alpha_rank * z.n_beta + lax.axis_index("beta")) % z.share
    integ = jnp.pad(integrals, ((0, pad), (0, pad)))
    lists = [pltpu.SMEM((z.blocks,), i32), pltpu.SMEM((z.blocks + 8,), i32)]
    spots = pl.pallas_call(
        functools.partial(index_kernel, z),
        out_shape=jax.ShapeDtypeStruct((z.tiles, z.pair_rows, LANES), i32),
        in_specs=[SMEM, VMEM, VMEM],
        out_specs=VMEM,
        scratch_shapes=lists,
        compiler_params=pltpu.CompilerParams(vmem_limit_bytes=16 * 1024 * 1024),
        cost_estimate=pl.CostEstimate(
            flops=50 * z.pairs * z.all_rows,
            bytes_accessed=12 * z.pairs * z.all_rows,
            transcendentals=0,
        ),
    )(block_irrep, alpha_row, alpha_sign)
    terms = pl.pallas_call(
        functools.partial(main_kernel, z),
        out_shape=jax.ShapeDtypeStruct((z.devices, z.halves, wide, LANES), f32),
        in_specs=[SMEM, SMEM, VMEM, VMEM, VMEM],
        out_specs=VMEM,
        scratch_shapes=[
            pltpu.VMEM((z.devices * z.pack, LANES), f32),
            pltpu.VMEM((z.tiles, z.lists, LANES), f32),
            pltpu.VMEM((z.tiles, z.lists, LANES), f32),
            pltpu.VMEM((round_up(z.all_rows, WIDE) // WIDE * z.lists, WIDE), bf16),
            pltpu.VMEM((z.pair_tiles, z.lists, LANES), f32),
            pltpu.VMEM((z.pair_rows * z.targets, LANES), f32),
            pltpu.VMEM((z.chunks, LANES, DEPTH), bf16),
            pltpu.VMEM((z.strings, 2 * z.targets, LANES), f32),
            pltpu.VMEM((DEPTH, z.strings * LANES), bf16),
            pltpu.VMEM((z.tiles, z.targets * z.strings, LANES), f32),
        ]
        + lists,
        compiler_params=params,
    )(block_irrep, part.astype(i32)[None], arrived, integ, spots)

    back = lax.all_to_all(terms, ("alpha", "beta"), 0, 0, tiled=True).reshape(-1, LANES)
    own_irrep = lax.dynamic_slice_in_dim(block_irrep, alpha_rank * z.own, z.own, 0)
    return pl.pallas_call(
        functools.partial(finish_kernel, z),
        out_shape=jax.ShapeDtypeStruct((z.rows, z.cols), f32),
        in_specs=[SMEM, VMEM, VMEM, VMEM],
        out_specs=VMEM,
        compiler_params=params,
    )(own_irrep, back, diagonal, coefficients)


def solution(mesh):
    return jax.shard_map(
        on_device,
        mesh=mesh,
        in_specs=(
            P("alpha", "beta"),
            P("alpha", "beta"),
            P(),
            P(),
            P(),
            P("beta", None),
            P("beta", None),
            P(),
        ),
        out_specs=P("alpha", "beta"),
        check_vma=False,
    )
```

```python
import functools

import jax
import jax.numpy as jnp
from jax import lax
from jax.experimental import pallas as pl
from jax.experimental.pallas import tpu as pltpu
from jax.sharding import PartitionSpec as P

LANES = 128
DEPTH = 2048
TURNED = 512
WIDE = 256
GATHERED = 4
VMEM = pl.BlockSpec(memory_space=pltpu.VMEM)
SMEM = pl.BlockSpec(memory_space=pltpu.SMEM)


def round_up(size, step):
    return -(-size // step) * step


class Sizes:
    def __init__(self, coefficients, integrals, alpha_row, beta_sign, block_irrep):
        self.n_alpha = lax.axis_size("alpha")
        self.n_beta = lax.axis_size("beta")
        self.devices = self.n_alpha * self.n_beta
        self.rows, self.cols = coefficients.shape
        self.pairs = integrals.shape[0]
        self.block = beta_sign.shape[1] // self.pairs
        self.src = self.cols // self.block
        self.targets = self.n_beta * self.src
        self.all_rows = alpha_row.shape[1]
        self.blocks = block_irrep.shape[0]
        self.own = self.rows // self.block
        self.share = max(1, self.devices // self.block)
        self.sets = self.devices // self.share
        self.strings = self.block // self.sets
        self.halves = self.rows // LANES
        self.tiles = self.all_rows // LANES
        self.per = max(1, self.src // self.n_alpha)
        self.senders = self.src // self.per
        self.group = self.src * self.strings
        self.lists = self.n_beta * self.group
        self.chunk_pairs = DEPTH // self.targets
        self.pair_rows = round_up(self.pairs, self.chunk_pairs)
        self.tall_pairs = round_up(self.pairs, 16)
        self.chunks = self.pair_rows // self.chunk_pairs
        self.whole_chunks = self.pairs // self.chunk_pairs
        self.tail_pairs = round_up(self.pairs % self.chunk_pairs, 2)
        self.pair_lanes = round_up(self.pairs, LANES)
        self.pair_tiles = self.pair_lanes // LANES
        self.coef_rows = self.halves * self.group
        self.sign_rows = self.per * self.strings * self.pair_tiles
        self.pack = round_up(self.coef_rows + self.sign_rows, 8)


def pack_kernel(z, coef_ref, sign_ref, out_ref, scratch):
    scratch[...] = jnp.zeros_like(scratch)
    turned = coef_ref[...].astype(jnp.float32).T
    for half in range(z.halves):
        for g in range(z.group):
            row = half * z.group + g
            for part in range(z.share):
                scratch[pl.ds(row + part * z.pack, z.sets, stride=z.share * z.pack), :] = turned[
                    g * z.sets : (g + 1) * z.sets, half * LANES : (half + 1) * LANES
                ]
    for s in range(z.per):
        code = sign_ref[s].T
        code = jnp.concatenate(
            [code, jnp.zeros((z.block, z.pair_lanes - z.pairs), jnp.float32)], axis=1
        )
        for cc in range(z.strings):
            for k in range(z.pair_tiles):
                row = z.coef_rows + (s * z.strings + cc) * z.pair_tiles + k
                for part in range(z.share):
                    scratch[pl.ds(row + part * z.pack, z.sets, stride=z.share * z.pack), :] = code[
                        cc * z.sets : (cc + 1) * z.sets, k * LANES : (k + 1) * LANES
                    ]
    out_ref[...] = scratch[...].astype(jnp.bfloat16)


def live_blocks(z, irrep_ref, rank_ref, list_ref):
    count = jnp.int32(0)
    lane_row = lax.broadcasted_iota(jnp.int32, (1, LANES), 1)
    ranks = jnp.full((1, LANES), -1, jnp.int32)
    for extra in range(z.blocks + 8):
        list_ref[extra] = 0
    for g in range(z.blocks):
        live = irrep_ref[g] == 0
        rank = jnp.where(live, count, -1)
        rank_ref[g] = rank
        list_ref[count] = g
        ranks = jnp.where(lane_row == g, rank, ranks)
        count = count + live.astype(jnp.int32)
    for extra in range(4):
        list_ref[count + extra] = 0
    return count, ranks


def index_kernel(z, irrep_ref, row_ref, sign_ref, out_ref, rank_ref, list_ref):
    count, ranks = live_blocks(z, irrep_ref, rank_ref, list_ref)
    lane_pair = lax.broadcasted_iota(jnp.int32, (z.pairs, LANES), 1)
    tail = z.pairs // 8 * 8

    def compact_step(u, carry):
        first, second = list_ref[2 * u], list_ref[2 * u + 1]
        left_shift = (first % 2) * z.block
        right_shift = (1 - second % 2) * z.block

        def merged(ref):
            at_first = pl.ds(pl.multiple_of(first // 2 * LANES, LANES), LANES)
            at_second = pl.ds(pl.multiple_of(second // 2 * LANES, LANES), LANES)
            return jnp.where(
                lane_pair < z.block,
                pltpu.roll(ref[:, at_first], left_shift, 1),
                pltpu.roll(ref[:, at_second], right_shift, 1),
            )

        source = merged(row_ref)
        signs = merged(sign_ref)
        block = source // z.block
        rank = jnp.take_along_axis(
            jnp.broadcast_to(ranks, (z.pairs, LANES)), block, axis=1, mode="promise_in_bounds"
        )
        spot = rank * z.block + (source & (z.block - 1))
        inside = (lane_pair < z.block) | (2 * u + 1 < count)
        out_ref[u, tail : z.pair_rows, :] = jnp.zeros((z.pair_rows - tail, LANES), jnp.int32)
        out_ref[u, 0 : z.pairs, :] = jnp.where((rank >= 0) & inside, signs * (spot + 1), 0)
        return carry

    lax.fori_loop(0, (count + 1) // 2, compact_step, 0)

    @pl.when(count % 2 == 1)
    def _():
        u = count // 2
        half = z.pair_rows // 2
        even = out_ref[u, pl.ds(0, half, stride=2), :]
        odd = out_ref[u, pl.ds(1, half, stride=2), :]
        out_ref[u, 0:half, :] = even + pltpu.roll(odd, z.block, 1)


def main_kernel(
    z,
    irrep_ref,
    part_ref,
    rx_ref,
    integ_ref,
    spot_ref,
    out_ref,
    rxf,
    full,
    tabf,
    table,
    codes,
    tall,
    weights,
    acc,
    held,
    result,
    rank_ref,
    list_ref,
):
    f32, bf16 = jnp.float32, jnp.bfloat16
    half_block = z.block
    count, _ = live_blocks(z, irrep_ref, rank_ref, list_ref)
    n_tiles = (count + 1) // 2

    rxf[...] = rx_ref[...].astype(f32)
    for i in range(z.n_alpha):
        base = i * z.n_beta * z.pack
        for half in range(z.halves):
            for s in range(z.src):
                for cc in range(z.strings):
                    source = base + half * z.group + s * z.strings + cc
                    dest = cc * z.targets + s
                    full[i * z.halves + half, pl.ds(dest, z.n_beta, stride=z.src), :] = rxf[
                        pl.ds(source, z.n_beta, stride=z.pack), :
                    ]
        for s in range(z.per if i < z.senders else 0):
            for cc in range(z.strings):
                for k in range(z.pair_tiles):
                    source = base + z.coef_rows + (s * z.strings + cc) * z.pair_tiles + k
                    dest = (i * z.per + s) * z.strings + cc
                    codes[k, pl.ds(dest, z.n_beta, stride=z.group), :] = rxf[
                        pl.ds(source, z.n_beta, stride=z.pack), :
                    ]

    step = 4
    target = (lax.broadcasted_iota(jnp.int32, (z.targets, z.pair_lanes), 0) + 1).astype(f32)

    def weight_step(n, carry):
        parts = []
        for m in range(step * z.strings):
            code = jnp.concatenate(
                [codes[k, pl.ds(n * step * z.strings + m, 1), :] for k in range(z.pair_tiles)],
                axis=1,
            )
            hit = jnp.where(code == target, 1.0, 0.0) - jnp.where(code == -target, 1.0, 0.0)
            parts.append(hit)
        hits = jnp.concatenate(parts, axis=0).astype(bf16)
        found = jnp.dot(hits, integ_ref[...], preferred_element_type=f32)
        high = found.astype(bf16).astype(f32)
        low = found - high
        for m in range(step):
            rows = []
            for cc in range(z.strings):
                at = (m * z.strings + cc) * z.targets
                rows += [high[at : at + z.targets], low[at : at + z.targets]]
            turned = jnp.concatenate(rows, axis=0).T
            tall[pl.ds(n * step + m, z.tall_pairs, stride=z.targets), :] = turned[0 : z.tall_pairs]
        return carry

    lax.fori_loop(0, z.targets // step, weight_step, 0, unroll=min(8, z.targets // step))

    def turn_step(n, carry):
        at = pl.multiple_of(n * TURNED, TURNED)
        weights[n // per_chunk, :, pl.ds(pl.multiple_of(n % per_chunk * TURNED, TURNED), TURNED)] = (
            tall[pl.ds(at, TURNED), :].T.astype(bf16)
        )
        return carry

    per_chunk = DEPTH // TURNED
    lax.fori_loop(0, round_up(z.pairs * z.targets, TURNED) // TURNED, turn_step, 0)

    lane_list = lax.broadcasted_iota(jnp.int32, (z.lists, LANES), 1)

    def compact_step(u, carry):
        first, second = list_ref[2 * u], list_ref[2 * u + 1]
        left_shift = (first % 2) * half_block
        right_shift = (1 - second % 2) * half_block
        left = pltpu.roll(full[first // 2], left_shift, 1)
        right = pltpu.roll(full[second // 2], right_shift, 1)
        left = jnp.where(2 * u < count, left, 0.0)
        right = jnp.where(2 * u + 1 < count, right, 0.0)
        tabf[u] = jnp.where(lane_list < half_block, left, right)
        return carry

    lax.fori_loop(0, z.tiles, compact_step, 0)

    side = 2 * z.targets

    def run(lower, blocks, span):
        depth = (blocks * z.block + span - 1) // span
        tiles = (blocks + 1) // 2
        local = lax.broadcasted_iota(jnp.int32, (span, LANES), 0).astype(f32).astype(bf16)
        nothing = jnp.zeros((span, LANES), bf16)

        def tall_row(few):
            return jnp.concatenate([few.astype(f32).astype(bf16)] * (span // 16), axis=0)

        def chunk_of(spot):
            if span & (span - 1) == 0:
                return lax.shift_right_arithmetic(spot, span.bit_length() - 1)
            return sum((spot >= span * m).astype(jnp.int32) for m in range(1, depth))

        for m in range(depth):
            for k in range(0, span, LANES):
                block = (m * span + k) // z.block
                left, right = tabf[min(block // 2, z.tiles - 1)], jnp.zeros((z.lists, LANES), f32)
                if block % 2:
                    left = pltpu.roll(left, half_block, 1)
                    if block // 2 + 1 < z.tiles:
                        right = pltpu.roll(tabf[block // 2 + 1], half_block, 1)
                    left = jnp.where(lane_list < half_block, left, right)
                table[m * z.lists : (m + 1) * z.lists, k : k + LANES] = left.astype(bf16)

        def one_tile(u, carry, half=False):
            acc[...] = jnp.zeros_like(acc)
            held[...] = jnp.zeros_like(held)

            def spread(n, rows=DEPTH):
                total = jnp.dot(
                    weights[n, :, 0:rows], held[0:rows, :], preferred_element_type=f32
                )
                for cc in range(z.strings):
                    acc[cc] += total[
                        cc * side : (cc + 1) * side, cc * LANES : (cc + 1) * LANES
                    ]

            def keep(q, value):
                sides = [value]
                if half:
                    left = lane_list < half_block
                    sides = [jnp.where(left, value, 0.0), jnp.where(left, 0.0, value)]
                for one, side_value in enumerate(sides):
                    side_value = side_value.astype(bf16)
                    row = (q * len(sides) + one) * z.targets
                    for cc in range(z.strings):
                        held[row : row + z.targets, cc * LANES : (cc + 1) * LANES] = side_value[
                            cc * z.targets : (cc + 1) * z.targets
                        ]

            def gather(q, spot, sign):
                lanes = spot & (LANES - 1)
                tile = lax.shift_right_arithmetic(spot, LANES.bit_length() - 1)
                hits = [tile == k for k in range(tiles)]
                parts = []
                for row in range(0, z.lists, 8):
                    value = jnp.zeros((8, LANES), f32)
                    for k in range(tiles):
                        taken = jnp.take_along_axis(
                            tabf[k, row : row + 8, :], lanes, axis=1, mode="promise_in_bounds"
                        )
                        value = jnp.where(hits[k], taken, value)
                    parts.append(value * sign)
                keep(q, jnp.concatenate(parts, axis=0))

            def one_chunk(n, inner, pairs=z.chunk_pairs):
                spread(jnp.maximum(n - 1, 0))
                columns = pairs // 2 if half else pairs
                short = pairs < z.chunk_pairs
                first = n * (z.chunk_pairs // 2 if half else z.chunk_pairs)
                picks, chunk, chosen = [], [], []
                for q in range(columns):
                    at = pl.ds(first + q, 1)
                    code = jnp.broadcast_to(spot_ref[u, at, :], (16, LANES))
                    spot = jnp.abs(code) - 1
                    sign = jnp.clip(code, -1, 1)
                    if q % GATHERED == GATHERED - 1 and not short:
                        gather(q, spot[0:8], sign[0:8].astype(f32))
                        continue
                    chosen.append(q)
                    part = chunk_of(spot)
                    hit = local == tall_row(spot - part * span)
                    picks.append(jnp.where(hit, tall_row(sign), nothing))
                    chunk.append(part[0:8])
                pick = jnp.concatenate(picks, axis=1)
                found = jnp.dot(
                    table[0 : depth * z.lists, 0:span], pick, preferred_element_type=f32
                )
                for k, q in enumerate(chosen):
                    lanes = slice(k * LANES, (k + 1) * LANES)
                    value = found[0 : z.lists, lanes]
                    for m in range(1, depth):
                        other = found[m * z.lists : (m + 1) * z.lists, lanes]
                        here = jnp.concatenate([chunk[k] == m] * (z.lists // 8), axis=0)
                        value = jnp.where(here, other, value)
                    keep(q, value)
                return inner

            lax.fori_loop(0, z.whole_chunks, one_chunk, 0)
            if z.tail_pairs:
                one_chunk(z.whole_chunks, 0, z.tail_pairs)
                spread(z.whole_chunks, z.tail_pairs * z.targets)
            else:
                spread(z.whole_chunks - 1)
            for cc in range(z.strings):
                total = acc[cc, 0 : z.targets, :] + acc[cc, z.targets : 2 * z.targets, :]
                if half:
                    total = total + pltpu.roll(total, half_block, 1)
                result[u, pl.ds(cc, z.targets, stride=z.strings), :] = total
            return carry

        whole = count // 2
        last_here = count % 2 == 1
        if z.share == 1:
            lax.fori_loop(0, whole, one_tile, 0)
        else:
            part = part_ref[0]
            mine = (whole - part + z.share - 1) // z.share
            lax.fori_loop(0, mine, lambda n, carry: one_tile(n * z.share + part, carry), 0)
            last_here = last_here & (whole % z.share == part)

        if blocks - lower > 1 or blocks % 2:

            @pl.when(last_here)
            def _():
                one_tile(whole, 0, half=True)

    lower = 0
    cases = [(8, WIDE), (9, 192), (10, WIDE), (16, WIDE), (z.blocks, WIDE)]
    for blocks, span in cases:
        if lower < blocks <= z.blocks:
            pl.when((count > lower) & (count <= blocks))(functools.partial(run, lower, blocks, span))
            lower = blocks

    wide = z.src * z.strings
    lane_out = lax.broadcasted_iota(jnp.int32, (z.targets * z.strings, LANES), 1)
    for w in range(z.tiles):
        sides = []
        for at_side in range(2):
            rank = rank_ref[2 * w + at_side]
            spot = jnp.maximum(rank, 0)
            shift = ((spot + at_side) % 2) * half_block
            moved = pltpu.roll(result[spot // 2], shift, 1)
            here = rank >= 0
            if z.share > 1:
                here = here & ((spot // 2) % z.share == part_ref[0])
            sides.append(jnp.where(here, moved, 0.0))
        both = jnp.where(lane_out < half_block, sides[0], sides[1])
        for j in range(z.n_beta):
            device = w // z.halves * z.n_beta + j
            out_ref[device, w % z.halves] = both[j * wide : (j + 1) * wide]


def finish_kernel(z, irrep_ref, rx_ref, diag_ref, coef_ref, out_ref):
    wide = z.src * z.strings
    stride = z.share * z.halves * wide

    def column(first):
        rows = [
            rx_ref[pl.ds(part * z.halves * wide + first, z.sets, stride=stride), :]
            for part in range(z.share)
        ]
        return functools.reduce(jnp.add, rows)

    columns = []
    for t in range(z.src):
        for cc in range(z.strings):
            firsts = [h * wide + t * z.strings + cc for h in range(z.halves)]
            columns.append(jnp.concatenate([column(first) for first in firsts], axis=1))
    added = jnp.concatenate(columns, axis=0).T
    total = diag_ref[...] * coef_ref[...].astype(jnp.float32) + added
    for b in range(z.own):
        at = slice(b * z.block, (b + 1) * z.block)
        out_ref[at, :] = jnp.where(irrep_ref[b] == 0, total[at], 0.0)


def on_device(
    coefficients, diagonal, integrals, alpha_row, alpha_sign, beta_block, beta_sign, block_irrep
):
    z = Sizes(coefficients, integrals, alpha_row, beta_sign, block_irrep)
    f32, i32, bf16 = jnp.float32, jnp.int32, jnp.bfloat16
    alpha_rank = lax.axis_index("alpha")
    params = pltpu.CompilerParams(vmem_limit_bytes=32 * 1024 * 1024)

    first = jnp.minimum(alpha_rank, z.senders - 1) * z.per
    own_signs = lax.dynamic_slice_in_dim(beta_sign, first, z.per, 0)
    own_blocks = lax.dynamic_slice_in_dim(beta_block, first, z.per, 0)
    code = own_signs.reshape(z.per, z.pairs, z.block) * (own_blocks + 1)[:, :, None]
    packed = pl.pallas_call(
        functools.partial(pack_kernel, z),
        out_shape=jax.ShapeDtypeStruct((z.devices * z.pack, LANES), bf16),
        in_specs=[VMEM, VMEM],
        out_specs=VMEM,
        scratch_shapes=[pltpu.VMEM((z.devices * z.pack, LANES), f32)],
        compiler_params=params,
    )(coefficients, code.astype(f32))
    arrived = lax.all_to_all(
        packed.reshape(z.devices, z.pack, LANES), ("alpha", "beta"), 0, 0, tiled=True
    ).reshape(z.devices * z.pack, LANES)

    pad = z.pair_lanes - z.pairs
    wide = z.src * z.strings
    part = (alpha_rank * z.n_beta + lax.axis_index("beta")) % z.share
    integ = jnp.pad(integrals, ((0, pad), (0, pad)))
    lists = [pltpu.SMEM((z.blocks,), i32), pltpu.SMEM((z.blocks + 8,), i32)]
    spots = pl.pallas_call(
        functools.partial(index_kernel, z),
        out_shape=jax.ShapeDtypeStruct((z.tiles, z.pair_rows, LANES), i32),
        in_specs=[SMEM, VMEM, VMEM],
        out_specs=VMEM,
        scratch_shapes=lists,
        compiler_params=pltpu.CompilerParams(vmem_limit_bytes=16 * 1024 * 1024),
        cost_estimate=pl.CostEstimate(
            flops=50 * z.pairs * z.all_rows,
            bytes_accessed=12 * z.pairs * z.all_rows,
            transcendentals=0,
        ),
    )(block_irrep, alpha_row, alpha_sign)
    terms = pl.pallas_call(
        functools.partial(main_kernel, z),
        out_shape=jax.ShapeDtypeStruct((z.devices, z.halves, wide, LANES), f32),
        in_specs=[SMEM, SMEM, VMEM, VMEM, VMEM],
        out_specs=VMEM,
        scratch_shapes=[
            pltpu.VMEM((z.devices * z.pack, LANES), f32),
            pltpu.VMEM((z.tiles, z.lists, LANES), f32),
            pltpu.VMEM((z.tiles, z.lists, LANES), f32),
            pltpu.VMEM((round_up(z.all_rows, WIDE) // WIDE * z.lists, WIDE), bf16),
            pltpu.VMEM((z.pair_tiles, z.lists, LANES), f32),
            pltpu.VMEM((z.tall_pairs * z.targets, LANES), f32),
            pltpu.VMEM((z.chunks, LANES, DEPTH), bf16),
            pltpu.VMEM((z.strings, 2 * z.targets, LANES), f32),
            pltpu.VMEM((DEPTH, z.strings * LANES), bf16),
            pltpu.VMEM((z.tiles, z.targets * z.strings, LANES), f32),
        ]
        + lists,
        compiler_params=params,
    )(block_irrep, part.astype(i32)[None], arrived, integ, spots)

    back = lax.all_to_all(terms, ("alpha", "beta"), 0, 0, tiled=True).reshape(-1, LANES)
    own_irrep = lax.dynamic_slice_in_dim(block_irrep, alpha_rank * z.own, z.own, 0)
    return pl.pallas_call(
        functools.partial(finish_kernel, z),
        out_shape=jax.ShapeDtypeStruct((z.rows, z.cols), f32),
        in_specs=[SMEM, VMEM, VMEM, VMEM],
        out_specs=VMEM,
        compiler_params=params,
    )(own_irrep, back, diagonal, coefficients)


def solution(mesh):
    return jax.shard_map(
        on_device,
        mesh=mesh,
        in_specs=(
            P("alpha", "beta"),
            P("alpha", "beta"),
            P(),
            P(),
            P(),
            P("beta", None),
            P("beta", None),
            P(),
        ),
        out_specs=P("alpha", "beta"),
        check_vma=False,
    )
```

```python
import functools

import jax
import jax.numpy as jnp
from jax import lax
from jax.experimental import pallas as pl
from jax.experimental.pallas import tpu as pltpu
from jax.sharding import PartitionSpec as P

LANES = 128
DEPTH = 2560
TURNED = 512
WIDE = 256
GATHERED = 4
VMEM = pl.BlockSpec(memory_space=pltpu.VMEM)
SMEM = pl.BlockSpec(memory_space=pltpu.SMEM)


def round_up(size, step):
    return -(-size // step) * step


class Sizes:
    def __init__(self, coefficients, integrals, alpha_row, beta_sign, block_irrep):
        self.n_alpha = lax.axis_size("alpha")
        self.n_beta = lax.axis_size("beta")
        self.devices = self.n_alpha * self.n_beta
        self.rows, self.cols = coefficients.shape
        self.pairs = integrals.shape[0]
        self.block = beta_sign.shape[1] // self.pairs
        self.src = self.cols // self.block
        self.targets = self.n_beta * self.src
        self.all_rows = alpha_row.shape[1]
        self.blocks = block_irrep.shape[0]
        self.own = self.rows // self.block
        self.share = max(1, self.devices // self.block)
        self.sets = self.devices // self.share
        self.strings = self.block // self.sets
        self.halves = self.rows // LANES
        self.tiles = self.all_rows // LANES
        self.per = max(1, self.src // self.n_alpha)
        self.senders = self.src // self.per
        self.group = self.src * self.strings
        self.lists = self.n_beta * self.group
        self.chunk_pairs = DEPTH // self.targets
        self.pair_rows = round_up(self.pairs, self.chunk_pairs)
        self.tall_pairs = round_up(self.pairs, 16)
        self.chunks = self.pair_rows // self.chunk_pairs
        self.whole_chunks = self.pairs // self.chunk_pairs
        self.tail_pairs = round_up(self.pairs % self.chunk_pairs, 2)
        self.pair_lanes = round_up(self.pairs, LANES)
        self.pair_tiles = self.pair_lanes // LANES
        self.coef_rows = self.halves * self.group
        self.sign_rows = self.per * self.strings * self.pair_tiles
        self.pack = round_up(self.coef_rows + self.sign_rows, 8)


def pack_kernel(z, coef_ref, sign_ref, out_ref, scratch):
    scratch[...] = jnp.zeros_like(scratch)
    turned = coef_ref[...].astype(jnp.float32).T
    for half in range(z.halves):
        for g in range(z.group):
            row = half * z.group + g
            for part in range(z.share):
                scratch[pl.ds(row + part * z.pack, z.sets, stride=z.share * z.pack), :] = turned[
                    g * z.sets : (g + 1) * z.sets, half * LANES : (half + 1) * LANES
                ]
    for s in range(z.per):
        code = sign_ref[s].T
        code = jnp.concatenate(
            [code, jnp.zeros((z.block, z.pair_lanes - z.pairs), jnp.float32)], axis=1
        )
        for cc in range(z.strings):
            for k in range(z.pair_tiles):
                row = z.coef_rows + (s * z.strings + cc) * z.pair_tiles + k
                for part in range(z.share):
                    scratch[pl.ds(row + part * z.pack, z.sets, stride=z.share * z.pack), :] = code[
                        cc * z.sets : (cc + 1) * z.sets, k * LANES : (k + 1) * LANES
                    ]
    out_ref[...] = scratch[...].astype(jnp.bfloat16)


def live_blocks(z, irrep_ref, rank_ref, list_ref):
    count = jnp.int32(0)
    lane_row = lax.broadcasted_iota(jnp.int32, (1, LANES), 1)
    ranks = jnp.full((1, LANES), -1, jnp.int32)
    for extra in range(z.blocks + 8):
        list_ref[extra] = 0
    for g in range(z.blocks):
        live = irrep_ref[g] == 0
        rank = jnp.where(live, count, -1)
        rank_ref[g] = rank
        list_ref[count] = g
        ranks = jnp.where(lane_row == g, rank, ranks)
        count = count + live.astype(jnp.int32)
    for extra in range(4):
        list_ref[count + extra] = 0
    return count, ranks


def index_kernel(z, irrep_ref, row_ref, sign_ref, out_ref, rank_ref, list_ref):
    count, ranks = live_blocks(z, irrep_ref, rank_ref, list_ref)
    lane_pair = lax.broadcasted_iota(jnp.int32, (z.pairs, LANES), 1)
    tail = z.pairs // 8 * 8

    def compact_step(u, carry):
        first, second = list_ref[2 * u], list_ref[2 * u + 1]
        left_shift = (first % 2) * z.block
        right_shift = (1 - second % 2) * z.block

        def merged(ref):
            at_first = pl.ds(pl.multiple_of(first // 2 * LANES, LANES), LANES)
            at_second = pl.ds(pl.multiple_of(second // 2 * LANES, LANES), LANES)
            return jnp.where(
                lane_pair < z.block,
                pltpu.roll(ref[:, at_first], left_shift, 1),
                pltpu.roll(ref[:, at_second], right_shift, 1),
            )

        source = merged(row_ref)
        signs = merged(sign_ref)
        block = source // z.block
        rank = jnp.take_along_axis(
            jnp.broadcast_to(ranks, (z.pairs, LANES)), block, axis=1, mode="promise_in_bounds"
        )
        spot = rank * z.block + (source & (z.block - 1))
        inside = (lane_pair < z.block) | (2 * u + 1 < count)
        out_ref[u, tail : z.pair_rows, :] = jnp.zeros((z.pair_rows - tail, LANES), jnp.int32)
        out_ref[u, 0 : z.pairs, :] = jnp.where((rank >= 0) & inside, signs * (spot + 1), 0)
        return carry

    lax.fori_loop(0, (count + 1) // 2, compact_step, 0)

    @pl.when(count % 2 == 1)
    def _():
        u = count // 2
        half = z.pair_rows // 2
        even = out_ref[u, pl.ds(0, half, stride=2), :]
        odd = out_ref[u, pl.ds(1, half, stride=2), :]
        out_ref[u, 0:half, :] = even + pltpu.roll(odd, z.block, 1)


def main_kernel(
    z,
    irrep_ref,
    part_ref,
    rx_ref,
    integ_ref,
    spot_ref,
    out_ref,
    rxf,
    full,
    tabf,
    table,
    codes,
    tall,
    weights,
    acc,
    held,
    result,
    rank_ref,
    list_ref,
):
    f32, bf16 = jnp.float32, jnp.bfloat16
    half_block = z.block
    count, _ = live_blocks(z, irrep_ref, rank_ref, list_ref)
    n_tiles = (count + 1) // 2

    rxf[...] = rx_ref[...].astype(f32)
    for i in range(z.n_alpha):
        base = i * z.n_beta * z.pack
        for half in range(z.halves):
            for s in range(z.src):
                for cc in range(z.strings):
                    source = base + half * z.group + s * z.strings + cc
                    dest = cc * z.targets + s
                    full[i * z.halves + half, pl.ds(dest, z.n_beta, stride=z.src), :] = rxf[
                        pl.ds(source, z.n_beta, stride=z.pack), :
                    ]
        for s in range(z.per if i < z.senders else 0):
            for cc in range(z.strings):
                for k in range(z.pair_tiles):
                    source = base + z.coef_rows + (s * z.strings + cc) * z.pair_tiles + k
                    dest = (i * z.per + s) * z.strings + cc
                    codes[k, pl.ds(dest, z.n_beta, stride=z.group), :] = rxf[
                        pl.ds(source, z.n_beta, stride=z.pack), :
                    ]

    step = 4
    target = (lax.broadcasted_iota(jnp.int32, (z.targets, z.pair_lanes), 0) + 1).astype(f32)

    def weight_step(n, carry):
        parts = []
        for m in range(step * z.strings):
            code = jnp.concatenate(
                [codes[k, pl.ds(n * step * z.strings + m, 1), :] for k in range(z.pair_tiles)],
                axis=1,
            )
            hit = jnp.where(code == target, 1.0, 0.0) - jnp.where(code == -target, 1.0, 0.0)
            parts.append(hit)
        hits = jnp.concatenate(parts, axis=0).astype(bf16)
        found = jnp.dot(hits, integ_ref[...], preferred_element_type=f32)
        high = found.astype(bf16).astype(f32)
        low = found - high
        for m in range(step):
            rows = []
            for cc in range(z.strings):
                at = (m * z.strings + cc) * z.targets
                rows += [high[at : at + z.targets], low[at : at + z.targets]]
            turned = jnp.concatenate(rows, axis=0).T
            tall[pl.ds(n * step + m, z.tall_pairs, stride=z.targets), :] = turned[0 : z.tall_pairs]
        return carry

    lax.fori_loop(0, z.targets // step, weight_step, 0, unroll=min(8, z.targets // step))

    def turn_step(n, carry):
        at = pl.multiple_of(n * TURNED, TURNED)
        weights[n // per_chunk, :, pl.ds(pl.multiple_of(n % per_chunk * TURNED, TURNED), TURNED)] = (
            tall[pl.ds(at, TURNED), :].T.astype(bf16)
        )
        return carry

    per_chunk = DEPTH // TURNED
    lax.fori_loop(0, z.tall_pairs * z.targets // TURNED, turn_step, 0, unroll=7)

    lane_list = lax.broadcasted_iota(jnp.int32, (z.lists, LANES), 1)

    def compact_step(u, carry):
        first, second = list_ref[2 * u], list_ref[2 * u + 1]
        left_shift = (first % 2) * half_block
        right_shift = (1 - second % 2) * half_block
        left = pltpu.roll(full[first // 2], left_shift, 1)
        right = pltpu.roll(full[second // 2], right_shift, 1)
        left = jnp.where(2 * u < count, left, 0.0)
        right = jnp.where(2 * u + 1 < count, right, 0.0)
        tabf[u] = jnp.where(lane_list < half_block, left, right)
        return carry

    lax.fori_loop(0, z.tiles, compact_step, 0)

    side = 2 * z.targets

    def run(lower, blocks, span):
        depth = (blocks * z.block + span - 1) // span
        tiles = (blocks + 1) // 2
        local = lax.broadcasted_iota(jnp.int32, (span, LANES), 0).astype(f32).astype(bf16)
        nothing = jnp.zeros((span, LANES), bf16)

        def tall_row(few):
            return jnp.concatenate([few.astype(f32).astype(bf16)] * (span // 16), axis=0)

        def chunk_of(spot):
            if span & (span - 1) == 0:
                return lax.shift_right_arithmetic(spot, span.bit_length() - 1)
            return sum((spot >= span * m).astype(jnp.int32) for m in range(1, depth))

        for m in range(depth):
            for k in range(0, span, LANES):
                block = (m * span + k) // z.block
                left, right = tabf[min(block // 2, z.tiles - 1)], jnp.zeros((z.lists, LANES), f32)
                if block % 2:
                    left = pltpu.roll(left, half_block, 1)
                    if block // 2 + 1 < z.tiles:
                        right = pltpu.roll(tabf[block // 2 + 1], half_block, 1)
                    left = jnp.where(lane_list < half_block, left, right)
                table[m * z.lists : (m + 1) * z.lists, k : k + LANES] = left.astype(bf16)

        def one_tile(u, carry, half=False):
            acc[...] = jnp.zeros_like(acc)
            held[...] = jnp.zeros_like(held)

            def spread(n, rows=DEPTH):
                total = jnp.dot(
                    weights[n, :, 0:rows], held[0:rows, :], preferred_element_type=f32
                )
                for cc in range(z.strings):
                    acc[cc] += total[
                        cc * side : (cc + 1) * side, cc * LANES : (cc + 1) * LANES
                    ]

            def keep(q, value):
                sides = [value]
                if half:
                    left = lane_list < half_block
                    sides = [jnp.where(left, value, 0.0), jnp.where(left, 0.0, value)]
                for one, side_value in enumerate(sides):
                    side_value = side_value.astype(bf16)
                    row = (q * len(sides) + one) * z.targets
                    for cc in range(z.strings):
                        held[row : row + z.targets, cc * LANES : (cc + 1) * LANES] = side_value[
                            cc * z.targets : (cc + 1) * z.targets
                        ]

            def gather(q, spot, sign):
                lanes = spot & (LANES - 1)
                tile = lax.shift_right_arithmetic(spot, LANES.bit_length() - 1)
                hits = [tile == k for k in range(tiles)]
                parts = []
                for row in range(0, z.lists, 8):
                    value = jnp.zeros((8, LANES), f32)
                    for k in range(tiles):
                        taken = jnp.take_along_axis(
                            tabf[k, row : row + 8, :], lanes, axis=1, mode="promise_in_bounds"
                        )
                        value = jnp.where(hits[k], taken, value)
                    parts.append(value * sign)
                keep(q, jnp.concatenate(parts, axis=0))

            def one_chunk(n, inner, pairs=z.chunk_pairs):
                spread(jnp.maximum(n - 1, 0))
                columns = pairs // 2 if half else pairs
                short = pairs < z.chunk_pairs
                first = n * (z.chunk_pairs // 2 if half else z.chunk_pairs)
                picks, chunk, chosen = [], [], []
                for q in range(columns):
                    at = pl.ds(first + q, 1)
                    code = jnp.broadcast_to(spot_ref[u, at, :], (16, LANES))
                    spot = jnp.abs(code) - 1
                    sign = jnp.clip(code, -1, 1)
                    if q % GATHERED == GATHERED - 1 and not short:
                        gather(q, spot[0:8], sign[0:8].astype(f32))
                        continue
                    chosen.append(q)
                    part = chunk_of(spot)
                    hit = local == tall_row(spot - part * span)
                    picks.append(jnp.where(hit, tall_row(sign), nothing))
                    chunk.append(part[0:8])
                pick = jnp.concatenate(picks, axis=1)
                found = jnp.dot(
                    table[0 : depth * z.lists, 0:span], pick, preferred_element_type=f32
                )
                for k, q in enumerate(chosen):
                    lanes = slice(k * LANES, (k + 1) * LANES)
                    value = found[0 : z.lists, lanes]
                    for m in range(1, depth):
                        other = found[m * z.lists : (m + 1) * z.lists, lanes]
                        here = jnp.concatenate([chunk[k] == m] * (z.lists // 8), axis=0)
                        value = jnp.where(here, other, value)
                    keep(q, value)
                return inner

            lax.fori_loop(0, z.whole_chunks, one_chunk, 0)
            if z.tail_pairs:
                one_chunk(z.whole_chunks, 0, z.tail_pairs)
                spread(z.whole_chunks, z.tail_pairs * z.targets)
            else:
                spread(z.whole_chunks - 1)
            for cc in range(z.strings):
                total = acc[cc, 0 : z.targets, :] + acc[cc, z.targets : 2 * z.targets, :]
                if half:
                    total = total + pltpu.roll(total, half_block, 1)
                result[u, pl.ds(cc, z.targets, stride=z.strings), :] = total
            return carry

        whole = count // 2
        last_here = count % 2 == 1
        if z.share == 1:
            lax.fori_loop(0, whole, one_tile, 0)
        else:
            part = part_ref[0]
            mine = (whole - part + z.share - 1) // z.share
            lax.fori_loop(0, mine, lambda n, carry: one_tile(n * z.share + part, carry), 0)
            last_here = last_here & (whole % z.share == part)

        if blocks - lower > 1 or blocks % 2:

            @pl.when(last_here)
            def _():
                one_tile(whole, 0, half=True)

    lower = 0
    cases = [(8, WIDE), (10, WIDE), (16, WIDE), (z.blocks, WIDE)]
    for blocks, span in cases:
        if lower < blocks <= z.blocks:
            pl.when((count > lower) & (count <= blocks))(functools.partial(run, lower, blocks, span))
            lower = blocks

    wide = z.src * z.strings
    lane_out = lax.broadcasted_iota(jnp.int32, (z.targets * z.strings, LANES), 1)
    for w in range(z.tiles):
        sides = []
        for at_side in range(2):
            rank = rank_ref[2 * w + at_side]
            spot = jnp.maximum(rank, 0)
            shift = ((spot + at_side) % 2) * half_block
            moved = pltpu.roll(result[spot // 2], shift, 1)
            here = rank >= 0
            if z.share > 1:
                here = here & ((spot // 2) % z.share == part_ref[0])
            sides.append(jnp.where(here, moved, 0.0))
        both = jnp.where(lane_out < half_block, sides[0], sides[1])
        for j in range(z.n_beta):
            device = w // z.halves * z.n_beta + j
            out_ref[device, w % z.halves] = both[j * wide : (j + 1) * wide]


def finish_kernel(z, irrep_ref, rx_ref, diag_ref, coef_ref, out_ref):
    wide = z.src * z.strings
    stride = z.share * z.halves * wide

    def column(first):
        rows = [
            rx_ref[pl.ds(part * z.halves * wide + first, z.sets, stride=stride), :]
            for part in range(z.share)
        ]
        return functools.reduce(jnp.add, rows)

    columns = []
    for t in range(z.src):
        for cc in range(z.strings):
            firsts = [h * wide + t * z.strings + cc for h in range(z.halves)]
            columns.append(jnp.concatenate([column(first) for first in firsts], axis=1))
    added = jnp.concatenate(columns, axis=0).T
    total = diag_ref[...] * coef_ref[...].astype(jnp.float32) + added
    for b in range(z.own):
        at = slice(b * z.block, (b + 1) * z.block)
        out_ref[at, :] = jnp.where(irrep_ref[b] == 0, total[at], 0.0)


def on_device(
    coefficients, diagonal, integrals, alpha_row, alpha_sign, beta_block, beta_sign, block_irrep
):
    z = Sizes(coefficients, integrals, alpha_row, beta_sign, block_irrep)
    f32, i32, bf16 = jnp.float32, jnp.int32, jnp.bfloat16
    alpha_rank = lax.axis_index("alpha")
    params = pltpu.CompilerParams(vmem_limit_bytes=32 * 1024 * 1024)

    first = jnp.minimum(alpha_rank, z.senders - 1) * z.per
    own_signs = lax.dynamic_slice_in_dim(beta_sign, first, z.per, 0)
    own_blocks = lax.dynamic_slice_in_dim(beta_block, first, z.per, 0)
    code = own_signs.reshape(z.per, z.pairs, z.block) * (own_blocks + 1)[:, :, None]
    packed = pl.pallas_call(
        functools.partial(pack_kernel, z),
        out_shape=jax.ShapeDtypeStruct((z.devices * z.pack, LANES), bf16),
        in_specs=[VMEM, VMEM],
        out_specs=VMEM,
        scratch_shapes=[pltpu.VMEM((z.devices * z.pack, LANES), f32)],
        compiler_params=params,
    )(coefficients, code.astype(f32))
    arrived = lax.all_to_all(
        packed.reshape(z.devices, z.pack, LANES), ("alpha", "beta"), 0, 0, tiled=True
    ).reshape(z.devices * z.pack, LANES)

    pad = z.pair_lanes - z.pairs
    wide = z.src * z.strings
    part = (alpha_rank * z.n_beta + lax.axis_index("beta")) % z.share
    integ = jnp.pad(integrals, ((0, pad), (0, pad)))
    lists = [pltpu.SMEM((z.blocks,), i32), pltpu.SMEM((z.blocks + 8,), i32)]
    spots = pl.pallas_call(
        functools.partial(index_kernel, z),
        out_shape=jax.ShapeDtypeStruct((z.tiles, z.pair_rows, LANES), i32),
        in_specs=[SMEM, VMEM, VMEM],
        out_specs=VMEM,
        scratch_shapes=lists,
        compiler_params=pltpu.CompilerParams(vmem_limit_bytes=16 * 1024 * 1024),
        cost_estimate=pl.CostEstimate(
            flops=50 * z.pairs * z.all_rows,
            bytes_accessed=12 * z.pairs * z.all_rows,
            transcendentals=0,
        ),
    )(block_irrep, alpha_row, alpha_sign)
    terms = pl.pallas_call(
        functools.partial(main_kernel, z),
        out_shape=jax.ShapeDtypeStruct((z.devices, z.halves, wide, LANES), f32),
        in_specs=[SMEM, SMEM, VMEM, VMEM, VMEM],
        out_specs=VMEM,
        scratch_shapes=[
            pltpu.VMEM((z.devices * z.pack, LANES), f32),
            pltpu.VMEM((z.tiles, z.lists, LANES), f32),
            pltpu.VMEM((z.tiles, z.lists, LANES), f32),
            pltpu.VMEM((round_up(z.all_rows, WIDE) // WIDE * z.lists, WIDE), bf16),
            pltpu.VMEM((z.pair_tiles, z.lists, LANES), f32),
            pltpu.VMEM((z.tall_pairs * z.targets, LANES), f32),
            pltpu.VMEM((z.chunks, LANES, DEPTH), bf16),
            pltpu.VMEM((z.strings, 2 * z.targets, LANES), f32),
            pltpu.VMEM((DEPTH, z.strings * LANES), bf16),
            pltpu.VMEM((z.tiles, z.targets * z.strings, LANES), f32),
        ]
        + lists,
        compiler_params=params,
    )(block_irrep, part.astype(i32)[None], arrived, integ, spots)

    back = lax.all_to_all(terms, ("alpha", "beta"), 0, 0, tiled=True).reshape(-1, LANES)
    own_irrep = lax.dynamic_slice_in_dim(block_irrep, alpha_rank * z.own, z.own, 0)
    return pl.pallas_call(
        functools.partial(finish_kernel, z),
        out_shape=jax.ShapeDtypeStruct((z.rows, z.cols), f32),
        in_specs=[SMEM, VMEM, VMEM, VMEM],
        out_specs=VMEM,
        compiler_params=params,
    )(own_irrep, back, diagonal, coefficients)


def solution(mesh):
    return jax.shard_map(
        on_device,
        mesh=mesh,
        in_specs=(
            P("alpha", "beta"),
            P("alpha", "beta"),
            P(),
            P(),
            P(),
            P("beta", None),
            P("beta", None),
            P(),
        ),
        out_specs=P("alpha", "beta"),
        check_vma=False,
    )
```

```python
import functools

import jax
import jax.numpy as jnp
from jax import lax
from jax.experimental import pallas as pl
from jax.experimental.pallas import tpu as pltpu
from jax.sharding import PartitionSpec as P

LANES = 128
DEPTH = 3456
TURNED = 384
WIDE = 256
GATHERED = 4
VMEM = pl.BlockSpec(memory_space=pltpu.VMEM)
SMEM = pl.BlockSpec(memory_space=pltpu.SMEM)


def round_up(size, step):
    return -(-size // step) * step


class Sizes:
    def __init__(self, coefficients, integrals, alpha_row, beta_sign, block_irrep):
        self.n_alpha = lax.axis_size("alpha")
        self.n_beta = lax.axis_size("beta")
        self.devices = self.n_alpha * self.n_beta
        self.rows, self.cols = coefficients.shape
        self.pairs = integrals.shape[0]
        self.block = beta_sign.shape[1] // self.pairs
        self.src = self.cols // self.block
        self.targets = self.n_beta * self.src
        self.all_rows = alpha_row.shape[1]
        self.blocks = block_irrep.shape[0]
        self.own = self.rows // self.block
        self.share = max(1, self.devices // self.block)
        self.sets = self.devices // self.share
        self.strings = self.block // self.sets
        self.halves = self.rows // LANES
        self.tiles = self.all_rows // LANES
        self.per = max(1, self.src // self.n_alpha)
        self.senders = self.src // self.per
        self.group = self.src * self.strings
        self.lists = self.n_beta * self.group
        self.chunk_pairs = DEPTH // self.targets
        self.pair_rows = round_up(self.pairs, self.chunk_pairs)
        self.tall_pairs = round_up(self.pair_rows, 8)
        self.chunks = self.pair_rows // self.chunk_pairs
        self.whole_chunks = self.pairs // self.chunk_pairs
        self.tail_pairs = round_up(self.pairs % self.chunk_pairs, 2)
        self.pair_lanes = round_up(self.pairs, LANES)
        self.pair_tiles = self.pair_lanes // LANES
        self.coef_rows = self.halves * self.group
        self.sign_rows = self.per * self.strings * self.pair_tiles
        self.pack = round_up(self.coef_rows + self.sign_rows, 8)


def pack_kernel(z, coef_ref, sign_ref, out_ref, scratch):
    scratch[...] = jnp.zeros_like(scratch)
    turned = coef_ref[...].astype(jnp.float32).T
    for half in range(z.halves):
        for g in range(z.group):
            row = half * z.group + g
            for part in range(z.share):
                scratch[pl.ds(row + part * z.pack, z.sets, stride=z.share * z.pack), :] = turned[
                    g * z.sets : (g + 1) * z.sets, half * LANES : (half + 1) * LANES
                ]
    for s in range(z.per):
        code = sign_ref[s].T
        code = jnp.concatenate(
            [code, jnp.zeros((z.block, z.pair_lanes - z.pairs), jnp.float32)], axis=1
        )
        for cc in range(z.strings):
            for k in range(z.pair_tiles):
                row = z.coef_rows + (s * z.strings + cc) * z.pair_tiles + k
                for part in range(z.share):
                    scratch[pl.ds(row + part * z.pack, z.sets, stride=z.share * z.pack), :] = code[
                        cc * z.sets : (cc + 1) * z.sets, k * LANES : (k + 1) * LANES
                    ]
    out_ref[...] = scratch[...].astype(jnp.bfloat16)


def live_blocks(z, irrep_ref, rank_ref, list_ref):
    count = jnp.int32(0)
    lane_row = lax.broadcasted_iota(jnp.int32, (1, LANES), 1)
    ranks = jnp.full((1, LANES), -1, jnp.int32)
    for extra in range(z.blocks + 8):
        list_ref[extra] = 0
    for g in range(z.blocks):
        live = irrep_ref[g] == 0
        rank = jnp.where(live, count, -1)
        rank_ref[g] = rank
        list_ref[count] = g
        ranks = jnp.where(lane_row == g, rank, ranks)
        count = count + live.astype(jnp.int32)
    for extra in range(4):
        list_ref[count + extra] = 0
    return count, ranks


def index_kernel(
    z, irrep_ref, row_ref, sign_ref, integ_ref, out_ref, padded_ref, square, rank_ref, list_ref
):
    square[...] = jnp.zeros_like(square)
    square[0 : z.pairs, 0 : z.pairs] = integ_ref[...].astype(jnp.float32)
    padded_ref[...] = square[...].astype(jnp.bfloat16)
    count, ranks = live_blocks(z, irrep_ref, rank_ref, list_ref)
    lane_pair = lax.broadcasted_iota(jnp.int32, (z.pairs, LANES), 1)
    tail = z.pairs // 8 * 8

    def compact_step(u, carry):
        first, second = list_ref[2 * u], list_ref[2 * u + 1]
        left_shift = (first % 2) * z.block
        right_shift = (1 - second % 2) * z.block

        def merged(ref):
            at_first = pl.ds(pl.multiple_of(first // 2 * LANES, LANES), LANES)
            at_second = pl.ds(pl.multiple_of(second // 2 * LANES, LANES), LANES)
            return jnp.where(
                lane_pair < z.block,
                pltpu.roll(ref[:, at_first], left_shift, 1),
                pltpu.roll(ref[:, at_second], right_shift, 1),
            )

        source = merged(row_ref)
        signs = merged(sign_ref)
        block = source // z.block
        rank = jnp.take_along_axis(
            jnp.broadcast_to(ranks, (z.pairs, LANES)), block, axis=1, mode="promise_in_bounds"
        )
        spot = rank * z.block + (source & (z.block - 1))
        inside = (lane_pair < z.block) | (2 * u + 1 < count)
        out_ref[u, tail : z.pair_rows, :] = jnp.zeros((z.pair_rows - tail, LANES), jnp.int32)
        out_ref[u, 0 : z.pairs, :] = jnp.where((rank >= 0) & inside, signs * (spot + 1), 0)
        return carry

    lax.fori_loop(0, (count + 1) // 2, compact_step, 0)

    @pl.when(count % 2 == 1)
    def _():
        u = count // 2
        half = z.pair_rows // 2
        even = out_ref[u, pl.ds(0, half, stride=2), :]
        odd = out_ref[u, pl.ds(1, half, stride=2), :]
        out_ref[u, 0:half, :] = even + pltpu.roll(odd, z.block, 1)


def main_kernel(
    z,
    irrep_ref,
    part_ref,
    rx_ref,
    integ_ref,
    spot_ref,
    out_ref,
    rxf,
    full,
    tabf,
    table,
    codes,
    tall,
    weights,
    acc,
    held,
    result,
    rank_ref,
    list_ref,
):
    f32, bf16 = jnp.float32, jnp.bfloat16
    half_block = z.block
    count, _ = live_blocks(z, irrep_ref, rank_ref, list_ref)
    n_tiles = (count + 1) // 2

    rxf[...] = rx_ref[...].astype(f32)
    for i in range(z.n_alpha):
        base = i * z.n_beta * z.pack
        for half in range(z.halves):
            for s in range(z.src):
                for cc in range(z.strings):
                    source = base + half * z.group + s * z.strings + cc
                    dest = cc * z.targets + s
                    full[i * z.halves + half, pl.ds(dest, z.n_beta, stride=z.src), :] = rxf[
                        pl.ds(source, z.n_beta, stride=z.pack), :
                    ]
        for s in range(z.per if i < z.senders else 0):
            for cc in range(z.strings):
                for k in range(z.pair_tiles):
                    source = base + z.coef_rows + (s * z.strings + cc) * z.pair_tiles + k
                    dest = (i * z.per + s) * z.strings + cc
                    codes[k, pl.ds(dest, z.n_beta, stride=z.group), :] = rxf[
                        pl.ds(source, z.n_beta, stride=z.pack), :
                    ]

    step = 4
    target = (lax.broadcasted_iota(jnp.int32, (z.targets, z.pair_lanes), 0) + 1).astype(f32)

    def weight_step(n, carry):
        parts = []
        for m in range(step * z.strings):
            code = jnp.concatenate(
                [codes[k, pl.ds(n * step * z.strings + m, 1), :] for k in range(z.pair_tiles)],
                axis=1,
            )
            hit = jnp.where(code == target, 1.0, 0.0) - jnp.where(code == -target, 1.0, 0.0)
            parts.append(hit)
        hits = jnp.concatenate(parts, axis=0).astype(bf16)
        found = jnp.dot(hits, integ_ref[...], preferred_element_type=f32)
        high = found.astype(bf16).astype(f32)
        low = found - high
        for m in range(step):
            rows = []
            for cc in range(z.strings):
                at = (m * z.strings + cc) * z.targets
                rows += [high[at : at + z.targets], low[at : at + z.targets]]
            turned = jnp.concatenate(rows, axis=0).T
            tall[pl.ds(n * step + m, z.tall_pairs, stride=z.targets), :] = turned[0 : z.tall_pairs]
        return carry

    lax.fori_loop(0, z.targets // step, weight_step, 0, unroll=min(8, z.targets // step))

    def turn_step(n, carry):
        at = pl.multiple_of(n * TURNED, TURNED)
        weights[n // per_chunk, :, pl.ds(pl.multiple_of(n % per_chunk * TURNED, TURNED), TURNED)] = (
            tall[pl.ds(at, TURNED), :].T.astype(bf16)
        )
        return carry

    per_chunk = DEPTH // TURNED
    lax.fori_loop(0, z.chunks * per_chunk, turn_step, 0, unroll=9)

    lane_list = lax.broadcasted_iota(jnp.int32, (z.lists, LANES), 1)

    def compact_step(u, carry):
        first, second = list_ref[2 * u], list_ref[2 * u + 1]
        left_shift = (first % 2) * half_block
        right_shift = (1 - second % 2) * half_block
        left = pltpu.roll(full[first // 2], left_shift, 1)
        right = pltpu.roll(full[second // 2], right_shift, 1)
        left = jnp.where(2 * u < count, left, 0.0)
        right = jnp.where(2 * u + 1 < count, right, 0.0)
        tabf[u] = jnp.where(lane_list < half_block, left, right)
        return carry

    lax.fori_loop(0, z.tiles, compact_step, 0)

    side = 2 * z.targets

    def run(lower, blocks, span):
        depth = (blocks * z.block + span - 1) // span
        tiles = (blocks + 1) // 2
        local = lax.broadcasted_iota(jnp.int32, (span, LANES), 0).astype(f32).astype(bf16)
        nothing = jnp.zeros((span, LANES), bf16)

        def tall_row(few):
            return jnp.concatenate([few.astype(f32).astype(bf16)] * (span // 16), axis=0)

        def chunk_of(spot):
            if span & (span - 1) == 0:
                return lax.shift_right_arithmetic(spot, span.bit_length() - 1)
            return sum((spot >= span * m).astype(jnp.int32) for m in range(1, depth))

        for m in range(depth):
            for k in range(0, span, LANES):
                block = (m * span + k) // z.block
                left, right = tabf[min(block // 2, z.tiles - 1)], jnp.zeros((z.lists, LANES), f32)
                if block % 2:
                    left = pltpu.roll(left, half_block, 1)
                    if block // 2 + 1 < z.tiles:
                        right = pltpu.roll(tabf[block // 2 + 1], half_block, 1)
                    left = jnp.where(lane_list < half_block, left, right)
                table[m * z.lists : (m + 1) * z.lists, k : k + LANES] = left.astype(bf16)

        def one_tile(u, carry, half=False):
            acc[...] = jnp.zeros_like(acc)
            held[...] = jnp.zeros_like(held)

            def spread(n, rows=DEPTH):
                total = jnp.dot(
                    weights[n, :, 0:rows], held[0:rows, :], preferred_element_type=f32
                )
                for cc in range(z.strings):
                    acc[cc] += total[
                        cc * side : (cc + 1) * side, cc * LANES : (cc + 1) * LANES
                    ]

            def keep(q, value):
                sides = [value]
                if half:
                    left = lane_list < half_block
                    sides = [jnp.where(left, value, 0.0), jnp.where(left, 0.0, value)]
                for one, side_value in enumerate(sides):
                    side_value = side_value.astype(bf16)
                    row = (q * len(sides) + one) * z.targets
                    for cc in range(z.strings):
                        held[row : row + z.targets, cc * LANES : (cc + 1) * LANES] = side_value[
                            cc * z.targets : (cc + 1) * z.targets
                        ]

            def gather(q, spot, sign):
                lanes = spot & (LANES - 1)
                tile = lax.shift_right_arithmetic(spot, LANES.bit_length() - 1)
                hits = [tile == k for k in range(tiles)]
                parts = []
                for row in range(0, z.lists, 8):
                    value = jnp.zeros((8, LANES), f32)
                    for k in range(tiles):
                        taken = jnp.take_along_axis(
                            tabf[k, row : row + 8, :], lanes, axis=1, mode="promise_in_bounds"
                        )
                        value = jnp.where(hits[k], taken, value)
                    parts.append(value * sign)
                keep(q, jnp.concatenate(parts, axis=0))

            def one_chunk(n, inner, pairs=z.chunk_pairs):
                spread(jnp.maximum(n - 1, 0))
                columns = pairs // 2 if half else pairs
                first = n * (z.chunk_pairs // 2 if half else z.chunk_pairs)
                picks, chunk, chosen = [], [], []
                for q in range(columns):
                    at = pl.ds(first + q, 1)
                    code = jnp.broadcast_to(spot_ref[u, at, :], (16, LANES))
                    spot = jnp.abs(code) - 1
                    sign = jnp.clip(code, -1, 1)
                    if q % GATHERED == GATHERED - 1 or q == 1:
                        gather(q, spot[0:8], sign[0:8].astype(f32))
                        continue
                    chosen.append(q)
                    part = chunk_of(spot)
                    hit = local == tall_row(spot - part * span)
                    picks.append(jnp.where(hit, tall_row(sign), nothing))
                    chunk.append(part[0:8])
                pick = jnp.concatenate(picks, axis=1)
                found = jnp.dot(
                    table[0 : depth * z.lists, 0:span], pick, preferred_element_type=f32
                )
                for k, q in enumerate(chosen):
                    lanes = slice(k * LANES, (k + 1) * LANES)
                    value = found[0 : z.lists, lanes]
                    for m in range(1, depth):
                        other = found[m * z.lists : (m + 1) * z.lists, lanes]
                        here = jnp.concatenate([chunk[k] == m] * (z.lists // 8), axis=0)
                        value = jnp.where(here, other, value)
                    keep(q, value)
                return inner

            lax.fori_loop(0, z.whole_chunks, one_chunk, 0)
            if z.tail_pairs:
                one_chunk(z.whole_chunks, 0, z.tail_pairs)
                spread(z.whole_chunks, z.tail_pairs * z.targets)
            else:
                spread(z.whole_chunks - 1)
            for cc in range(z.strings):
                total = acc[cc, 0 : z.targets, :] + acc[cc, z.targets : 2 * z.targets, :]
                if half:
                    total = total + pltpu.roll(total, half_block, 1)
                result[u, pl.ds(cc, z.targets, stride=z.strings), :] = total
            return carry

        whole = count // 2
        last_here = count % 2 == 1
        if z.share == 1:
            lax.fori_loop(0, whole, one_tile, 0)
        else:
            part = part_ref[0]
            mine = (whole - part + z.share - 1) // z.share
            lax.fori_loop(0, mine, lambda n, carry: one_tile(n * z.share + part, carry), 0)
            last_here = last_here & (whole % z.share == part)

        if blocks - lower > 1 or blocks % 2:

            @pl.when(last_here)
            def _():
                one_tile(whole, 0, half=True)

    lower = 0
    cases = [(8, WIDE), (10, WIDE), (16, WIDE), (z.blocks, WIDE)]
    for blocks, span in cases:
        if lower < blocks <= z.blocks:
            pl.when((count > lower) & (count <= blocks))(functools.partial(run, lower, blocks, span))
            lower = blocks

    wide = z.src * z.strings
    lane_out = lax.broadcasted_iota(jnp.int32, (z.targets * z.strings, LANES), 1)
    for w in range(z.tiles):
        sides = []
        for at_side in range(2):
            rank = rank_ref[2 * w + at_side]
            spot = jnp.maximum(rank, 0)
            shift = ((spot + at_side) % 2) * half_block
            moved = pltpu.roll(result[spot // 2], shift, 1)
            here = rank >= 0
            if z.share > 1:
                here = here & ((spot // 2) % z.share == part_ref[0])
            sides.append(jnp.where(here, moved, 0.0))
        both = jnp.where(lane_out < half_block, sides[0], sides[1])
        for j in range(z.n_beta):
            device = w // z.halves * z.n_beta + j
            out_ref[device, w % z.halves] = both[j * wide : (j + 1) * wide]


def finish_kernel(z, irrep_ref, rx_ref, diag_ref, coef_ref, out_ref):
    wide = z.src * z.strings
    stride = z.share * z.halves * wide

    def column(first):
        rows = [
            rx_ref[pl.ds(part * z.halves * wide + first, z.sets, stride=stride), :]
            for part in range(z.share)
        ]
        return functools.reduce(jnp.add, rows)

    columns = []
    for t in range(z.src):
        for cc in range(z.strings):
            firsts = [h * wide + t * z.strings + cc for h in range(z.halves)]
            columns.append(jnp.concatenate([column(first) for first in firsts], axis=1))
    added = jnp.concatenate(columns, axis=0).T
    total = diag_ref[...] * coef_ref[...].astype(jnp.float32) + added
    for b in range(z.own):
        at = slice(b * z.block, (b + 1) * z.block)
        out_ref[at, :] = jnp.where(irrep_ref[b] == 0, total[at], 0.0)


def on_device(
    coefficients, diagonal, integrals, alpha_row, alpha_sign, beta_block, beta_sign, block_irrep
):
    z = Sizes(coefficients, integrals, alpha_row, beta_sign, block_irrep)
    f32, i32, bf16 = jnp.float32, jnp.int32, jnp.bfloat16
    alpha_rank = lax.axis_index("alpha")
    params = pltpu.CompilerParams(vmem_limit_bytes=40 * 1024 * 1024)

    first = jnp.minimum(alpha_rank, z.senders - 1) * z.per
    own_signs = lax.dynamic_slice_in_dim(beta_sign, first, z.per, 0)
    own_blocks = lax.dynamic_slice_in_dim(beta_block, first, z.per, 0)
    code = own_signs.reshape(z.per, z.pairs, z.block) * (own_blocks + 1)[:, :, None]
    packed = pl.pallas_call(
        functools.partial(pack_kernel, z),
        out_shape=jax.ShapeDtypeStruct((z.devices * z.pack, LANES), bf16),
        in_specs=[VMEM, VMEM],
        out_specs=VMEM,
        scratch_shapes=[pltpu.VMEM((z.devices * z.pack, LANES), f32)],
        compiler_params=params,
    )(coefficients, code.astype(f32))
    arrived = lax.all_to_all(
        packed.reshape(z.devices, z.pack, LANES), ("alpha", "beta"), 0, 0, tiled=True
    ).reshape(z.devices * z.pack, LANES)

    wide = z.src * z.strings
    part = (alpha_rank * z.n_beta + lax.axis_index("beta")) % z.share
    lists = [pltpu.SMEM((z.blocks,), i32), pltpu.SMEM((z.blocks + 8,), i32)]
    spots, integ = pl.pallas_call(
        functools.partial(index_kernel, z),
        out_shape=(
            jax.ShapeDtypeStruct((z.tiles, z.pair_rows, LANES), i32),
            jax.ShapeDtypeStruct((z.pair_lanes, z.pair_lanes), bf16),
        ),
        in_specs=[SMEM, VMEM, VMEM, VMEM],
        out_specs=(VMEM, VMEM),
        scratch_shapes=[pltpu.VMEM((z.pair_lanes, z.pair_lanes), f32)] + lists,
        compiler_params=pltpu.CompilerParams(vmem_limit_bytes=16 * 1024 * 1024),
        cost_estimate=pl.CostEstimate(
            flops=50 * z.pairs * z.all_rows,
            bytes_accessed=12 * z.pairs * z.all_rows,
            transcendentals=0,
        ),
    )(block_irrep, alpha_row, alpha_sign, integrals)
    terms = pl.pallas_call(
        functools.partial(main_kernel, z),
        out_shape=jax.ShapeDtypeStruct((z.devices, z.halves, wide, LANES), f32),
        in_specs=[SMEM, SMEM, VMEM, VMEM, VMEM],
        out_specs=VMEM,
        scratch_shapes=[
            pltpu.VMEM((z.devices * z.pack, LANES), f32),
            pltpu.VMEM((z.tiles, z.lists, LANES), f32),
            pltpu.VMEM((z.tiles, z.lists, LANES), f32),
            pltpu.VMEM((round_up(z.all_rows, WIDE) // WIDE * z.lists, WIDE), bf16),
            pltpu.VMEM((z.pair_tiles, z.lists, LANES), f32),
            pltpu.VMEM((z.tall_pairs * z.targets, LANES), f32),
            pltpu.VMEM((z.chunks, LANES, DEPTH), bf16),
            pltpu.VMEM((z.strings, 2 * z.targets, LANES), f32),
            pltpu.VMEM((DEPTH, z.strings * LANES), bf16),
            pltpu.VMEM((z.tiles, z.targets * z.strings, LANES), f32),
        ]
        + lists,
        compiler_params=params,
    )(block_irrep, part.astype(i32)[None], arrived, integ, spots)

    back = lax.all_to_all(terms, ("alpha", "beta"), 0, 0, tiled=True).reshape(-1, LANES)
    own_irrep = lax.dynamic_slice_in_dim(block_irrep, alpha_rank * z.own, z.own, 0)
    return pl.pallas_call(
        functools.partial(finish_kernel, z),
        out_shape=jax.ShapeDtypeStruct((z.rows, z.cols), f32),
        in_specs=[SMEM, VMEM, VMEM, VMEM],
        out_specs=VMEM,
        compiler_params=params,
    )(own_irrep, back, diagonal, coefficients)


def solution(mesh):
    return jax.shard_map(
        on_device,
        mesh=mesh,
        in_specs=(
            P("alpha", "beta"),
            P("alpha", "beta"),
            P(),
            P(),
            P(),
            P("beta", None),
            P("beta", None),
            P(),
        ),
        out_specs=P("alpha", "beta"),
        check_vma=False,
    )
```

```python
import functools

import jax
import jax.numpy as jnp
from jax import lax
from jax.experimental import pallas as pl
from jax.experimental.pallas import tpu as pltpu
from jax.sharding import PartitionSpec as P

LANES = 128
DEPTH = 3456
TURNED = 384
WIDE = 256
GATHERED = 4
VMEM = pl.BlockSpec(memory_space=pltpu.VMEM)
SMEM = pl.BlockSpec(memory_space=pltpu.SMEM)


def round_up(size, step):
    return -(-size // step) * step


class Sizes:
    def __init__(self, coefficients, integrals, alpha_row, beta_sign, block_irrep):
        self.n_alpha = lax.axis_size("alpha")
        self.n_beta = lax.axis_size("beta")
        self.devices = self.n_alpha * self.n_beta
        self.rows, self.cols = coefficients.shape
        self.pairs = integrals.shape[0]
        self.block = beta_sign.shape[1] // self.pairs
        self.src = self.cols // self.block
        self.targets = self.n_beta * self.src
        self.all_rows = alpha_row.shape[1]
        self.blocks = block_irrep.shape[0]
        self.own = self.rows // self.block
        self.share = max(1, self.devices // self.block)
        self.sets = self.devices // self.share
        self.strings = self.block // self.sets
        self.halves = self.rows // LANES
        self.tiles = self.all_rows // LANES
        self.per = max(1, self.src // self.n_alpha)
        self.senders = self.src // self.per
        self.group = self.src * self.strings
        self.lists = self.n_beta * self.group
        self.chunk_pairs = DEPTH // self.targets
        self.pair_rows = round_up(self.pairs, self.chunk_pairs)
        self.tall_pairs = round_up(self.pair_rows, 8)
        self.chunks = self.pair_rows // self.chunk_pairs
        self.whole_chunks = self.pairs // self.chunk_pairs
        self.tail_pairs = round_up(self.pairs % self.chunk_pairs, 2)
        self.pair_lanes = round_up(self.pairs, LANES)
        self.pair_tiles = self.pair_lanes // LANES
        self.coef_rows = self.halves * self.group
        self.sign_rows = self.per * self.strings * self.pair_tiles
        self.pack = round_up(self.coef_rows + self.sign_rows, 8)


def turn_kernel(z, first_ref, coef_ref, block_ref, out_ref, number_ref):
    out_ref[...] = jnp.zeros_like(out_ref)
    turned = coef_ref[...].astype(jnp.float32).T
    for half in range(z.halves):
        for g in range(z.group):
            row = half * z.group + g
            for part in range(z.share):
                out_ref[pl.ds(row + part * z.pack, z.sets, stride=z.share * z.pack), :] = turned[
                    g * z.sets : (g + 1) * z.sets, half * LANES : (half + 1) * LANES
                ]
    number = block_ref[pl.ds(first_ref[0], z.per), :] + 1
    number_ref[...] = number.astype(jnp.float32)


def pack_kernel(z, turned_ref, number_ref, sign_ref, out_ref, scratch):
    scratch[...] = turned_ref[...]
    for s in range(z.per):
        code = sign_ref[s].astype(jnp.float32).T * number_ref[s : s + 1, :]
        code = jnp.concatenate(
            [code, jnp.zeros((z.block, z.pair_lanes - z.pairs), jnp.float32)], axis=1
        )
        for cc in range(z.strings):
            for k in range(z.pair_tiles):
                row = z.coef_rows + (s * z.strings + cc) * z.pair_tiles + k
                for part in range(z.share):
                    scratch[pl.ds(row + part * z.pack, z.sets, stride=z.share * z.pack), :] = code[
                        cc * z.sets : (cc + 1) * z.sets, k * LANES : (k + 1) * LANES
                    ]
    out_ref[...] = scratch[...].astype(jnp.bfloat16)


def live_blocks(z, irrep_ref, rank_ref, list_ref):
    count = jnp.int32(0)
    lane_row = lax.broadcasted_iota(jnp.int32, (1, LANES), 1)
    ranks = jnp.full((1, LANES), -1, jnp.int32)
    for extra in range(z.blocks + 8):
        list_ref[extra] = 0
    for g in range(z.blocks):
        live = irrep_ref[g] == 0
        rank = jnp.where(live, count, -1)
        rank_ref[g] = rank
        list_ref[count] = g
        ranks = jnp.where(lane_row == g, rank, ranks)
        count = count + live.astype(jnp.int32)
    for extra in range(4):
        list_ref[count + extra] = 0
    return count, ranks


def index_kernel(
    z, irrep_ref, row_ref, sign_ref, integ_ref, out_ref, padded_ref, square, rank_ref, list_ref
):
    square[...] = jnp.zeros_like(square)
    square[0 : z.pairs, 0 : z.pairs] = integ_ref[...].astype(jnp.float32)
    padded_ref[...] = square[...].astype(jnp.bfloat16)
    count, ranks = live_blocks(z, irrep_ref, rank_ref, list_ref)
    lane_pair = lax.broadcasted_iota(jnp.int32, (z.pairs, LANES), 1)
    tail = z.pairs // 8 * 8

    def compact_step(u, carry):
        first, second = list_ref[2 * u], list_ref[2 * u + 1]
        left_shift = (first % 2) * z.block
        right_shift = (1 - second % 2) * z.block

        def merged(ref):
            at_first = pl.ds(pl.multiple_of(first // 2 * LANES, LANES), LANES)
            at_second = pl.ds(pl.multiple_of(second // 2 * LANES, LANES), LANES)
            return jnp.where(
                lane_pair < z.block,
                pltpu.roll(ref[:, at_first], left_shift, 1),
                pltpu.roll(ref[:, at_second], right_shift, 1),
            )

        source = merged(row_ref)
        signs = merged(sign_ref)
        block = source // z.block
        rank = jnp.take_along_axis(
            jnp.broadcast_to(ranks, (z.pairs, LANES)), block, axis=1, mode="promise_in_bounds"
        )
        spot = rank * z.block + (source & (z.block - 1))
        inside = (lane_pair < z.block) | (2 * u + 1 < count)
        out_ref[u, tail : z.pair_rows, :] = jnp.zeros((z.pair_rows - tail, LANES), jnp.int32)
        out_ref[u, 0 : z.pairs, :] = jnp.where((rank >= 0) & inside, signs * (spot + 1), 0)
        return carry

    lax.fori_loop(0, (count + 1) // 2, compact_step, 0)

    @pl.when(count % 2 == 1)
    def _():
        u = count // 2
        half = z.pair_rows // 2
        even = out_ref[u, pl.ds(0, half, stride=2), :]
        odd = out_ref[u, pl.ds(1, half, stride=2), :]
        out_ref[u, 0:half, :] = even + pltpu.roll(odd, z.block, 1)


def main_kernel(
    z,
    irrep_ref,
    part_ref,
    rx_ref,
    integ_ref,
    spot_ref,
    out_ref,
    rxf,
    full,
    tabf,
    table,
    codes,
    tall,
    weights,
    acc,
    held,
    result,
    rank_ref,
    list_ref,
):
    f32, bf16 = jnp.float32, jnp.bfloat16
    half_block = z.block
    count, _ = live_blocks(z, irrep_ref, rank_ref, list_ref)
    n_tiles = (count + 1) // 2

    rxf[...] = rx_ref[...].astype(f32)
    for i in range(z.n_alpha):
        base = i * z.n_beta * z.pack
        for half in range(z.halves):
            for s in range(z.src):
                for cc in range(z.strings):
                    source = base + half * z.group + s * z.strings + cc
                    dest = cc * z.targets + s
                    full[i * z.halves + half, pl.ds(dest, z.n_beta, stride=z.src), :] = rxf[
                        pl.ds(source, z.n_beta, stride=z.pack), :
                    ]
        for s in range(z.per if i < z.senders else 0):
            for cc in range(z.strings):
                for k in range(z.pair_tiles):
                    source = base + z.coef_rows + (s * z.strings + cc) * z.pair_tiles + k
                    dest = (i * z.per + s) * z.strings + cc
                    codes[k, pl.ds(dest, z.n_beta, stride=z.group), :] = rxf[
                        pl.ds(source, z.n_beta, stride=z.pack), :
                    ]

    step = 4
    target = lax.broadcasted_iota(jnp.int32, (z.targets, z.pair_lanes), 0) + 1
    target = target.astype(f32).astype(bf16)
    one, none = jnp.ones(target.shape, bf16), jnp.zeros(target.shape, bf16)

    def weight_step(n, carry):
        parts = []
        for m in range(step * z.strings):
            code = jnp.concatenate(
                [codes[k, pl.ds(n * step * z.strings + m, 1), :] for k in range(z.pair_tiles)],
                axis=1,
            )
            code = jnp.broadcast_to(code, (16, z.pair_lanes)).astype(bf16)
            code = jnp.concatenate([code] * (z.targets // 16), axis=0)
            parts.append(jnp.where(code == target, one, jnp.where(code == -target, -one, none)))
        hits = jnp.concatenate(parts, axis=0)
        found = jnp.dot(hits, integ_ref[...], preferred_element_type=f32)
        high = found.astype(bf16).astype(f32)
        low = found - high
        for m in range(step):
            rows = []
            for cc in range(z.strings):
                at = (m * z.strings + cc) * z.targets
                rows += [high[at : at + z.targets], low[at : at + z.targets]]
            turned = jnp.concatenate(rows, axis=0).T
            tall[pl.ds(n * step + m, z.tall_pairs, stride=z.targets), :] = turned[0 : z.tall_pairs]
        return carry

    lax.fori_loop(0, z.targets // step, weight_step, 0, unroll=min(8, z.targets // step))

    def turn_step(n, carry):
        at = pl.multiple_of(n * TURNED, TURNED)
        weights[n // per_chunk, :, pl.ds(pl.multiple_of(n % per_chunk * TURNED, TURNED), TURNED)] = (
            tall[pl.ds(at, TURNED), :].T.astype(bf16)
        )
        return carry

    per_chunk = DEPTH // TURNED
    lax.fori_loop(0, z.chunks * per_chunk, turn_step, 0, unroll=9)

    lane_list = lax.broadcasted_iota(jnp.int32, (z.lists, LANES), 1)

    def compact_step(u, carry):
        first, second = list_ref[2 * u], list_ref[2 * u + 1]
        left_shift = (first % 2) * half_block
        right_shift = (1 - second % 2) * half_block
        left = pltpu.roll(full[first // 2], left_shift, 1)
        right = pltpu.roll(full[second // 2], right_shift, 1)
        left = jnp.where(2 * u < count, left, 0.0)
        right = jnp.where(2 * u + 1 < count, right, 0.0)
        tabf[u] = jnp.where(lane_list < half_block, left, right)
        return carry

    lax.fori_loop(0, z.tiles, compact_step, 0)

    side = 2 * z.targets

    def run(lower, blocks, span):
        depth = (blocks * z.block + span - 1) // span
        tiles = (blocks + 1) // 2
        local = lax.broadcasted_iota(jnp.int32, (span, LANES), 0).astype(f32).astype(bf16)
        nothing = jnp.zeros((span, LANES), bf16)

        def tall_row(few):
            return jnp.concatenate([few.astype(f32).astype(bf16)] * (span // 16), axis=0)

        def chunk_of(spot):
            if span & (span - 1) == 0:
                return lax.shift_right_arithmetic(spot, span.bit_length() - 1)
            return sum((spot >= span * m).astype(jnp.int32) for m in range(1, depth))

        for m in range(depth):
            for k in range(0, span, LANES):
                block = (m * span + k) // z.block
                left, right = tabf[min(block // 2, z.tiles - 1)], jnp.zeros((z.lists, LANES), f32)
                if block % 2:
                    left = pltpu.roll(left, half_block, 1)
                    if block // 2 + 1 < z.tiles:
                        right = pltpu.roll(tabf[block // 2 + 1], half_block, 1)
                    left = jnp.where(lane_list < half_block, left, right)
                table[m * z.lists : (m + 1) * z.lists, k : k + LANES] = left.astype(bf16)

        def one_tile(u, carry, half=False):
            acc[...] = jnp.zeros_like(acc)
            held[...] = jnp.zeros_like(held)

            def spread(n, rows=DEPTH):
                total = jnp.dot(
                    weights[n, :, 0:rows], held[0:rows, :], preferred_element_type=f32
                )
                for cc in range(z.strings):
                    acc[cc] += total[
                        cc * side : (cc + 1) * side, cc * LANES : (cc + 1) * LANES
                    ]

            def keep(q, value):
                sides = [value]
                if half:
                    left = lane_list < half_block
                    sides = [jnp.where(left, value, 0.0), jnp.where(left, 0.0, value)]
                for one, side_value in enumerate(sides):
                    side_value = side_value.astype(bf16)
                    row = (q * len(sides) + one) * z.targets
                    for cc in range(z.strings):
                        held[row : row + z.targets, cc * LANES : (cc + 1) * LANES] = side_value[
                            cc * z.targets : (cc + 1) * z.targets
                        ]

            def gather(q, spot, sign):
                lanes = spot & (LANES - 1)
                tile = lax.shift_right_arithmetic(spot, LANES.bit_length() - 1)
                hits = [tile == k for k in range(tiles)]
                parts = []
                for row in range(0, z.lists, 8):
                    value = jnp.zeros((8, LANES), f32)
                    for k in range(tiles):
                        taken = jnp.take_along_axis(
                            tabf[k, row : row + 8, :], lanes, axis=1, mode="promise_in_bounds"
                        )
                        value = jnp.where(hits[k], taken, value)
                    parts.append(value * sign)
                keep(q, jnp.concatenate(parts, axis=0))

            def one_chunk(n, inner, pairs=z.chunk_pairs):
                spread(jnp.maximum(n - 1, 0))
                columns = pairs // 2 if half else pairs
                first = n * (z.chunk_pairs // 2 if half else z.chunk_pairs)
                picks, chunk, chosen = [], [], []
                for q in range(columns):
                    at = pl.ds(first + q, 1)
                    code = jnp.broadcast_to(spot_ref[u, at, :], (16, LANES))
                    spot = jnp.abs(code) - 1
                    sign = jnp.clip(code, -1, 1)
                    if q % GATHERED == GATHERED - 1 or q == 1:
                        gather(q, spot[0:8], sign[0:8].astype(f32))
                        continue
                    chosen.append(q)
                    part = chunk_of(spot)
                    hit = local == tall_row(spot - part * span)
                    picks.append(jnp.where(hit, tall_row(sign), nothing))
                    chunk.append(part[0:8])
                pick = jnp.concatenate(picks, axis=1)
                found = jnp.dot(
                    table[0 : depth * z.lists, 0:span], pick, preferred_element_type=f32
                )
                for k, q in enumerate(chosen):
                    lanes = slice(k * LANES, (k + 1) * LANES)
                    value = found[0 : z.lists, lanes]
                    for m in range(1, depth):
                        other = found[m * z.lists : (m + 1) * z.lists, lanes]
                        here = jnp.concatenate([chunk[k] == m] * (z.lists // 8), axis=0)
                        value = jnp.where(here, other, value)
                    keep(q, value)
                return inner

            lax.fori_loop(0, z.whole_chunks, one_chunk, 0)
            if z.tail_pairs:
                one_chunk(z.whole_chunks, 0, z.tail_pairs)
                spread(z.whole_chunks, z.tail_pairs * z.targets)
            else:
                spread(z.whole_chunks - 1)
            for cc in range(z.strings):
                total = acc[cc, 0 : z.targets, :] + acc[cc, z.targets : 2 * z.targets, :]
                if half:
                    total = total + pltpu.roll(total, half_block, 1)
                result[u, pl.ds(cc, z.targets, stride=z.strings), :] = total
            return carry

        whole = count // 2
        last_here = count % 2 == 1
        if z.share == 1:
            lax.fori_loop(0, whole, one_tile, 0)
        else:
            part = part_ref[0]
            mine = (whole - part + z.share - 1) // z.share
            lax.fori_loop(0, mine, lambda n, carry: one_tile(n * z.share + part, carry), 0)
            last_here = last_here & (whole % z.share == part)

        if blocks - lower > 1 or blocks % 2:

            @pl.when(last_here)
            def _():
                one_tile(whole, 0, half=True)

    lower = 0
    cases = [(8, WIDE), (10, WIDE), (16, WIDE), (z.blocks, WIDE)]
    for blocks, span in cases:
        if lower < blocks <= z.blocks:
            pl.when((count > lower) & (count <= blocks))(functools.partial(run, lower, blocks, span))
            lower = blocks

    wide = z.src * z.strings
    lane_out = lax.broadcasted_iota(jnp.int32, (z.targets * z.strings, LANES), 1)
    for w in range(z.tiles):
        sides = []
        for at_side in range(2):
            rank = rank_ref[2 * w + at_side]
            spot = jnp.maximum(rank, 0)
            shift = ((spot + at_side) % 2) * half_block
            moved = pltpu.roll(result[spot // 2], shift, 1)
            here = rank >= 0
            if z.share > 1:
                here = here & ((spot // 2) % z.share == part_ref[0])
            sides.append(jnp.where(here, moved, 0.0))
        both = jnp.where(lane_out < half_block, sides[0], sides[1])
        for j in range(z.n_beta):
            device = w // z.halves * z.n_beta + j
            out_ref[device, w % z.halves] = both[j * wide : (j + 1) * wide]


def finish_kernel(z, irrep_ref, rx_ref, diag_ref, coef_ref, out_ref):
    wide = z.src * z.strings
    stride = z.share * z.halves * wide

    def column(first):
        rows = [
            rx_ref[pl.ds(part * z.halves * wide + first, z.sets, stride=stride), :]
            for part in range(z.share)
        ]
        return functools.reduce(jnp.add, rows)

    columns = []
    for t in range(z.src):
        for cc in range(z.strings):
            firsts = [h * wide + t * z.strings + cc for h in range(z.halves)]
            columns.append(jnp.concatenate([column(first) for first in firsts], axis=1))
    added = jnp.concatenate(columns, axis=0).T
    total = diag_ref[...] * coef_ref[...].astype(jnp.float32) + added
    for b in range(z.own):
        at = slice(b * z.block, (b + 1) * z.block)
        out_ref[at, :] = jnp.where(irrep_ref[b] == 0, total[at], 0.0)


def on_device(
    coefficients, diagonal, integrals, alpha_row, alpha_sign, beta_block, beta_sign, block_irrep
):
    z = Sizes(coefficients, integrals, alpha_row, beta_sign, block_irrep)
    f32, i32, bf16 = jnp.float32, jnp.int32, jnp.bfloat16
    alpha_rank = lax.axis_index("alpha")
    params = pltpu.CompilerParams(vmem_limit_bytes=40 * 1024 * 1024)

    first = jnp.minimum(alpha_rank, z.senders - 1) * z.per
    own_signs = lax.dynamic_slice_in_dim(beta_sign, first, z.per, 0)
    small = pltpu.CompilerParams(vmem_limit_bytes=8 * 1024 * 1024)
    turned, number = pl.pallas_call(
        functools.partial(turn_kernel, z),
        out_shape=(
            jax.ShapeDtypeStruct((z.devices * z.pack, LANES), f32),
            jax.ShapeDtypeStruct((z.per, z.pairs), f32),
        ),
        in_specs=[SMEM, VMEM, VMEM],
        out_specs=(VMEM, VMEM),
        compiler_params=small,
    )(first.astype(i32)[None], coefficients, beta_block)
    packed = pl.pallas_call(
        functools.partial(pack_kernel, z),
        out_shape=jax.ShapeDtypeStruct((z.devices * z.pack, LANES), bf16),
        in_specs=[VMEM, VMEM, VMEM],
        out_specs=VMEM,
        scratch_shapes=[pltpu.VMEM((z.devices * z.pack, LANES), f32)],
        compiler_params=small,
    )(turned, number, own_signs.reshape(z.per, z.pairs, z.block))
    arrived = lax.all_to_all(
        packed.reshape(z.devices, z.pack, LANES), ("alpha", "beta"), 0, 0, tiled=True
    ).reshape(z.devices * z.pack, LANES)

    wide = z.src * z.strings
    part = (alpha_rank * z.n_beta + lax.axis_index("beta")) % z.share
    lists = [pltpu.SMEM((z.blocks,), i32), pltpu.SMEM((z.blocks + 8,), i32)]
    spots, integ = pl.pallas_call(
        functools.partial(index_kernel, z),
        out_shape=(
            jax.ShapeDtypeStruct((z.tiles, z.pair_rows, LANES), i32),
            jax.ShapeDtypeStruct((z.pair_lanes, z.pair_lanes), bf16),
        ),
        in_specs=[SMEM, VMEM, VMEM, VMEM],
        out_specs=(VMEM, VMEM),
        scratch_shapes=[pltpu.VMEM((z.pair_lanes, z.pair_lanes), f32)] + lists,
        compiler_params=pltpu.CompilerParams(vmem_limit_bytes=16 * 1024 * 1024),
        cost_estimate=pl.CostEstimate(
            flops=50 * z.pairs * z.all_rows,
            bytes_accessed=12 * z.pairs * z.all_rows,
            transcendentals=0,
        ),
    )(block_irrep, alpha_row, alpha_sign, integrals)
    terms = pl.pallas_call(
        functools.partial(main_kernel, z),
        out_shape=jax.ShapeDtypeStruct((z.devices, z.halves, wide, LANES), f32),
        in_specs=[SMEM, SMEM, VMEM, VMEM, VMEM],
        out_specs=VMEM,
        scratch_shapes=[
            pltpu.VMEM((z.devices * z.pack, LANES), f32),
            pltpu.VMEM((z.tiles, z.lists, LANES), f32),
            pltpu.VMEM((z.tiles, z.lists, LANES), f32),
            pltpu.VMEM((round_up(z.all_rows, WIDE) // WIDE * z.lists, WIDE), bf16),
            pltpu.VMEM((z.pair_tiles, z.lists, LANES), f32),
            pltpu.VMEM((z.tall_pairs * z.targets, LANES), f32),
            pltpu.VMEM((z.chunks, LANES, DEPTH), bf16),
            pltpu.VMEM((z.strings, 2 * z.targets, LANES), f32),
            pltpu.VMEM((DEPTH, z.strings * LANES), bf16),
            pltpu.VMEM((z.tiles, z.targets * z.strings, LANES), f32),
        ]
        + lists,
        compiler_params=params,
    )(block_irrep, part.astype(i32)[None], arrived, integ, spots)

    back = lax.all_to_all(terms, ("alpha", "beta"), 0, 0, tiled=True).reshape(-1, LANES)
    own_irrep = lax.dynamic_slice_in_dim(block_irrep, alpha_rank * z.own, z.own, 0)
    return pl.pallas_call(
        functools.partial(finish_kernel, z),
        out_shape=jax.ShapeDtypeStruct((z.rows, z.cols), f32),
        in_specs=[SMEM, VMEM, VMEM, VMEM],
        out_specs=VMEM,
        compiler_params=params,
    )(own_irrep, back, diagonal, coefficients)


def solution(mesh):
    return jax.shard_map(
        on_device,
        mesh=mesh,
        in_specs=(
            P("alpha", "beta"),
            P("alpha", "beta"),
            P(),
            P(),
            P(),
            P("beta", None),
            P("beta", None),
            P(),
        ),
        out_specs=P("alpha", "beta"),
        check_vma=False,
    )
```
